256 devices in a mesh: dom: 64 (over y, z, x_lo), rep: 4 (over x_hi, core).
Axes of the slice: x: 4 (x_hi: 2, x_lo: 2; x = x_hi * 2 + x_lo), y: 4, z: 8, core: 2. Of those that a mesh axis runs over, the one named last changes fastest.
Arguments:
- entity_table: bfloat16 [200, 32768], P(None, ('dom', 'rep')), may hold values from -1.5 to 1.5
- relation_diag: bfloat16 [200, 2176], replicated, may hold values from -4 to 4
- plan: int32 [4], replicated, may hold values from 1 to 63, as said below
- edge_count: int32 [4, 64], replicated, may hold values from 1025 to 4096, as said below
- src_rows: int32 [4, 262144], P(None, ('dom', 'rep')), may hold values from 0 to 511
- dst_rows: int32 [4, 262144], P(None, ('dom', 'rep')), may hold values from 0 to 511
- rel_ids: int32 [4, 262144], P(None, ('dom', 'rep')), may hold values from 0 to 2175
- neg_rows: int32 [4, 1024, 1024], P(None, ('dom', 'rep')), may hold values from 0 to 511
Outputs:
- entity_grad: float32 [200, 32768], P(None, ('dom', 'rep'))
- relation_grad: float32 [200, 2176], replicated
The draws below stay inside these ranges and needn't reach their ends.
Inputs may be any that keep to these rules, and one draw needn't show every extreme that they name: `plan`: the offsets of the 4 rounds are distinct, and 1, 32 and 63 are among them. `edge_count`: in every round one bucket is full.
All inputs are finite; a program needn't handle non-finite values.
Results may differ from the reference program's by a relative error of at most 0.002.
Values may be sent and summed in bfloat16 or wider, within the bound.
No kernel may reach another device: no remote copies, remote signals or barrier semaphores. Data moves between devices by JAX's collectives and lax.ppermute only.
A program may use at most 64 MiB of HBM per device.

```python
import math
import jax
import jax.numpy as jnp
import numpy as np
from jax import lax

D = 200
NREL = 2176
SPAN = 256
NEG = 1024
SPANS_DEV = 4
ROUNDS = 4
PART = 512
ENTITIES = 32768
EDGE_CAP = 4096
BLOCKS = 1024
SLOTS = 262144
N_DOM = 64
N_REP = 4


def draw_plan(key, part):
    key = jax.random.fold_in(key, 11)
    half = N_DOM // 2
    picks = jax.random.permutation(key, N_DOM - 4)[:ROUNDS - 3].astype(jnp.int32) + 2
    picks = jnp.where(picks >= half, picks + 1, picks).astype(jnp.int32)
    offsets = jnp.concatenate([picks, jnp.array([1, half, N_DOM - 1], jnp.int32)])
    return jax.random.permutation(jax.random.fold_in(key, 1), offsets).astype(jnp.int32)


def draw_edge_count(key, part):
    key = jax.random.fold_in(key, 23)
    floor_count = EDGE_CAP // 4 + 1
    spare = EDGE_CAP - floor_count
    draws = jax.random.randint(key, (ROUNDS, N_DOM), 0, 65).astype(jnp.int32)
    extra = spare * draws // 64
    extra = extra * draws // 64
    extra = extra * draws // 64
    counts = floor_count + extra
    fullest = jax.random.randint(jax.random.fold_in(key, 1), (ROUNDS, 1), 0, N_DOM).astype(jnp.int32)
    columns = jnp.arange(N_DOM, dtype=jnp.int32)[None, :]
    counts = jnp.where(columns == fullest, EDGE_CAP, counts)
    return jnp.clip(counts, floor_count, EDGE_CAP).astype(jnp.int32)


def place_ends(result, key, low, top_value):
    extent = result.shape
    place = [jax.random.randint(jax.random.fold_in(key, axis), (), 0, extent[axis]) for axis in range(len(extent))]
    result = result.at[tuple(place)].set(low)
    longest = extent.index(max(extent))
    place[longest] = (place[longest] + 1) % extent[longest]
    return result.at[tuple(place)].set(top_value)


def levels(own_key, extent, shards, low, top_value):
    def one(dim, parts):
        steps = jax.random.uniform(jax.random.fold_in(jax.random.fold_in(own_key, 6), dim), (parts,), jnp.float32, low / len(shards), top_value / len(shards))
        return jnp.repeat(jnp.exp(steps), extent[dim] // parts).reshape((-1,) + (1,) * (len(extent) - dim - 1))

    gain = one(*shards[0])
    for cut in shards[1:]:
        gain = gain * one(*cut)
    return gain


def rank_bounds(number_of, skew):
    loads = [(1 << 20) // math.isqrt(standing ** skew) + 1 for standing in range(1, number_of + 1)]
    spread = 1 + sum(loads) // (1 << 30)
    return np.cumsum(np.array([max(1, weight // spread) for weight in loads]))


def ranked_ids(stream_key, extent, count, slope):
    grid = rank_bounds(count, slope)
    lot = jax.random.randint(jax.random.fold_in(stream_key, 1), extent, 0, int(grid[count - 1]))
    grade = jnp.searchsorted(jnp.asarray(grid, jnp.int32), lot, side="right")
    return jax.random.permutation(jax.random.fold_in(stream_key, 2), count)[grade].astype(jnp.int32)


def bell_draw(rng, extent, width, reach, pieces=(), kind=jnp.bfloat16):
    level = levels(rng, extent, pieces, -0.22, 0.18) if pieces else 1.0
    drawn = jax.random.normal(rng, extent, jnp.float32) * width * level
    return jnp.minimum(jnp.maximum(drawn, -reach), reach).astype(kind)


def setup_inputs(seed: int = 0) -> dict:
    key_of = jax.random.split(jax.random.key(seed), 9)
    entity_table = bell_draw(key_of[0], (D, ENTITIES), 0.25, 1.5, ((1, 256),))
    relation_diag = bell_draw(key_of[1], (D, NREL), 1.0, 4.0)
    plan = draw_plan(jax.random.fold_in(key_of[8], 71), 0)
    edge_count = draw_edge_count(jax.random.fold_in(key_of[8], 71), 0)
    src_rows = place_ends(jax.random.randint(key_of[4], (ROUNDS, SLOTS), 0, PART), jax.random.fold_in(key_of[4], 1), 0, PART - 1).astype(jnp.int32)
    dst_rows = place_ends(jax.random.randint(key_of[5], (ROUNDS, SLOTS), 0, PART), jax.random.fold_in(key_of[5], 1), 0, PART - 1).astype(jnp.int32)
    rel_ids = place_ends(ranked_ids(key_of[6], (ROUNDS, SLOTS), NREL, 2), jax.random.fold_in(key_of[6], 3), 0, NREL - 1).astype(jnp.int32)
    neg_rows = place_ends(jax.random.randint(key_of[7], (ROUNDS, BLOCKS, NEG), 0, PART), jax.random.fold_in(key_of[7], 1), 0, PART - 1).astype(jnp.int32)
    return dict(entity_table=entity_table, relation_diag=relation_diag, plan=plan, edge_count=edge_count, src_rows=src_rows, dst_rows=dst_rows, rel_ids=rel_ids, neg_rows=neg_rows)


def rounded(values):
    narrow = lax.optimization_barrier(values.astype(jnp.bfloat16))
    return narrow.astype(jnp.float32)


def block_grads(src_part, dst_part, relation_diag, src_idx, dst_idx, rel_idx, neg_idx, live):
    src_emb = jnp.take(src_part, src_idx, axis=1)
    dst_emb = jnp.take(dst_part, dst_idx, axis=1)
    neg_emb = jnp.take(dst_part, neg_idx, axis=1)
    rel_emb = jnp.take(relation_diag, rel_idx, axis=1)
    rel_wide = rel_emb.astype(jnp.float32)
    src_wide = src_emb.astype(jnp.float32)
    lhs = (src_wide * rel_wide).astype(jnp.bfloat16)
    lhs_wide = lhs.astype(jnp.float32)
    positive = jnp.sum(lhs_wide * dst_emb.astype(jnp.float32), axis=0)
    negative = jnp.dot(lhs.T, neg_emb, preferred_element_type=jnp.float32)
    pos_weight = -live * jax.nn.sigmoid(-positive)
    neg_weight = (live[:, None] * (neg_emb.shape[1] ** -0.5) * jax.nn.sigmoid(negative)).astype(jnp.bfloat16)
    grad_lhs = pos_weight[None, :] * dst_emb.astype(jnp.float32) + jnp.dot(
        neg_emb, neg_weight.T, preferred_element_type=jnp.float32)
    grad_neg = jnp.dot(lhs, neg_weight, preferred_element_type=jnp.float32)
    return (rounded(grad_lhs * rel_wide), rounded(grad_lhs * src_wide),
            rounded(pos_weight[None, :] * lhs_wide), rounded(grad_neg))


def add_block(src_acc, dst_acc, rel_acc, terms, src_idx, dst_idx, rel_idx, neg_idx):
    grad_src, grad_rel, grad_dst, grad_neg = terms
    src_acc = src_acc.at[:, src_idx].add(grad_src)
    dst_acc = dst_acc.at[:, dst_idx].add(grad_dst).at[:, neg_idx].add(grad_neg)
    rel_acc = rel_acc.at[:, rel_idx].add(grad_rel)
    return src_acc, dst_acc, rel_acc


def add_columns(table, start, extra):
    current = lax.dynamic_slice_in_dim(table, start, extra.shape[1], 1)
    return lax.dynamic_update_slice_in_dim(table, current + extra, start, 1)


def reference(entity_table, relation_diag, plan, edge_count, src_rows, dst_rows, rel_ids, neg_rows):
    per_bucket = N_REP * SPANS_DEV
    ent_total = jnp.zeros((D, ENTITIES), jnp.float32)
    rel_total = jnp.zeros((D, NREL), jnp.float32)
    for step in range(ROUNDS):
        offset = plan[step]
        src_round = src_rows[step]
        dst_round = dst_rows[step]
        rel_round = rel_ids[step]
        neg_round = neg_rows[step]
        count_round = edge_count[step]

        def bucket(index, carry):
            ent_acc, rel_acc = carry
            index = jnp.asarray(index).astype(jnp.int32)
            target = ((index + offset) % N_DOM).astype(jnp.int32)
            src_part = lax.dynamic_slice_in_dim(entity_table, index * PART, PART, 1)
            dst_part = lax.dynamic_slice_in_dim(entity_table, target * PART, PART, 1)
            count = count_round[index]
            srcs = lax.dynamic_slice_in_dim(src_round, index * EDGE_CAP, EDGE_CAP, 0).reshape(per_bucket, SPAN)
            dsts = lax.dynamic_slice_in_dim(dst_round, index * EDGE_CAP, EDGE_CAP, 0).reshape(per_bucket, SPAN)
            rels = lax.dynamic_slice_in_dim(rel_round, index * EDGE_CAP, EDGE_CAP, 0).reshape(per_bucket, SPAN)
            negs = lax.dynamic_slice_in_dim(neg_round, index * per_bucket, per_bucket, 0)
            used = (count + SPAN - 1) // SPAN

            def one_block(block, inner):
                s_acc, d_acc, r_acc = inner
                slot = block * SPAN + jnp.arange(SPAN).astype(jnp.int32)
                live = (slot < count).astype(jnp.float32)
                src_idx = srcs[block]
                dst_idx = dsts[block]
                rel_idx = rels[block]
                neg_idx = negs[block]
                terms = block_grads(src_part, dst_part, relation_diag, src_idx, dst_idx, rel_idx, neg_idx, live)
                return add_block(s_acc, d_acc, r_acc, terms, src_idx, dst_idx, rel_idx, neg_idx)

            empty = jnp.zeros((D, PART), jnp.float32)
            s_acc, d_acc, rel_acc = lax.fori_loop(jnp.int32(0), used.astype(jnp.int32), one_block, (empty, empty, rel_acc))
            ent_acc = add_columns(ent_acc, index * PART, s_acc)
            ent_acc = add_columns(ent_acc, target * PART, d_acc)
            return ent_acc, rel_acc

        ent_total, rel_total = lax.fori_loop(0, N_DOM, bucket, (ent_total, rel_total))
    return ent_total, rel_total
```

```python
import functools

import jax
import jax.numpy as jnp
from jax import lax
from jax.experimental import pallas as pl
from jax.experimental.pallas import tpu as pltpu
from jax.sharding import Mesh, PartitionSpec as P

DOM = ("y", "z", "xl")
REP = ("xh", "core")
CHIPS = ("y", "z", "xl", "xh")
LANES = 128
SPAN = 256
KNOWN = (1, 32, 63)
F32 = jnp.float32
BF16 = jnp.bfloat16


def mm(a, b):
    return jnp.dot(a, b, preferred_element_type=F32)


def mm_nt(a, b):
    return lax.dot_general(a, b, (((1,), (1,)), ((), ())), preferred_element_type=F32)


def one_hot(index, first, height):
    rows = lax.broadcasted_iota(jnp.int32, (height, index.shape[1]), 0) + first
    return jnp.where(rows == index, 1.0, 0.0).astype(BF16)


def rel_chunks(n_rel):
    return [(a, min(2 * LANES, n_rel - a)) for a in range(0, n_rel, 2 * LANES)]


def place(tile, half_tiles):
    return (0, tile) if tile < half_tiles else (1, tile - half_tiles)


def round_kernel(first, half_tiles, meta, src_q, dst_q, rel, srcs, dsts, rels, negs, *rest):
    if first:
        src_o, rel_o, dst_o, hot = rest
        src_o[...] = jnp.zeros_like(src_o)
        rel_o[...] = jnp.zeros_like(rel_o)
    else:
        src_in, rel_in, src_o, rel_o, dst_o, hot = rest
        src_o[...] = src_in[...]
        rel_o[...] = rel_in[...]
    dst_o[...] = jnp.zeros_like(dst_o)
    width, n_rel = rel.shape
    n_q = src_q.shape[0]
    src_t = jnp.concatenate([src_q[q] for q in range(n_q)], axis=1)
    dst_t = jnp.concatenate([dst_q[q] for q in range(n_q)], axis=1)
    dst_wide = dst_t.astype(F32)
    dst_rows = dst_wide.T.astype(BF16)
    part = src_t.shape[1]
    row = meta[0]
    used = meta[1]
    count = meta[2]
    block0 = meta[3]
    stride = meta[4]
    n_neg = negs.shape[2]
    scale = n_neg ** -0.5

    def one_block(k, carry):
        lanes = pl.ds(pl.multiple_of(k * SPAN, SPAN), SPAN)
        src_i = srcs[pl.ds(row, 1), lanes]
        dst_i = dsts[pl.ds(row, 1), lanes]
        rel_i = rels[pl.ds(row, 1), lanes]
        neg_i = negs[row, pl.ds(k, 1), :]
        slot = (block0 + k * stride) * SPAN + lax.broadcasted_iota(jnp.int32, (1, SPAN), 1)
        live = (slot < count).astype(F32)
        src_hot = one_hot(src_i, 0, part)
        dst_hot = one_hot(dst_i, 0, part)
        w = jnp.zeros((width, SPAN), F32)
        for a, n in rel_chunks(n_rel):
            chunk = one_hot(rel_i, a, n)
            hot[a:a + n, :] = chunk
            w = w + mm(rel[:, a:a + n], chunk)
        s = mm(src_t, src_hot)
        t = mm(dst_t, dst_hot)
        lhs = (s * w).astype(BF16)
        lhs_wide = lhs.astype(F32)
        positive = jnp.sum(lhs_wide * t, axis=0, keepdims=True)
        pos_weight = -live * jax.nn.sigmoid(-positive)
        scores = mm(dst_rows, lhs)
        weight = ((live * scale) * jax.nn.sigmoid(scores)).astype(BF16)
        low = one_hot(jnp.bitwise_and(neg_i, LANES - 1), 0, LANES)
        high = one_hot(jnp.right_shift(neg_i, 7), 0, 16)
        times = mm_nt(high, low)
        times = jnp.concatenate([times[q:q + 1, :] for q in range(n_q)], axis=1)
        counted = times * dst_wide
        counted_hi = counted.astype(BF16)
        counted_lo = (counted - counted_hi.astype(F32)).astype(BF16)
        grad_lhs = pos_weight * t + (mm(counted_hi, weight) + mm(counted_lo, weight))
        grad_src = (grad_lhs * w).astype(BF16)
        grad_rel = (grad_lhs * s).astype(BF16)
        grad_dst = (pos_weight * lhs_wide).astype(BF16)
        src_part = mm_nt(grad_src, src_hot)
        grad_neg = mm_nt(lhs, weight).astype(BF16).astype(F32)
        dst_part = mm_nt(grad_dst, dst_hot) + times * grad_neg
        for q in range(n_q):
            cols = slice(q * LANES, (q + 1) * LANES)
            src_o[q] += src_part[:, cols]
            dst_o[q] += dst_part[:, cols]
        for a, n in rel_chunks(n_rel):
            term = mm_nt(grad_rel, hot[a:a + n, :])
            for b in range(n // LANES):
                half, at = place(a // LANES + b, half_tiles)
                rel_o[half, at * width:(at + 1) * width, :] += term[:, b * LANES:(b + 1) * LANES]
        return carry

    lax.fori_loop(0, used, one_block, 0)


def run_round(meta, src_q, dst_q, rel, srcs, dsts, rels, negs, carried):
    n_q, width, lanes = src_q.shape
    n_rel = rel.shape[1]
    half_tiles = -(-(n_rel // LANES) // 2)
    half_rows = -(-half_tiles * width // 2048) * 2048
    vmem = pl.BlockSpec(memory_space=pltpu.VMEM)
    smem = pl.BlockSpec(memory_space=pltpu.SMEM)
    part = jax.ShapeDtypeStruct((n_q, width, lanes), F32)
    ops = [meta, src_q, dst_q, rel, srcs, dsts, rels, negs] + list(carried)
    return pl.pallas_call(
        functools.partial(round_kernel, not carried, half_tiles),
        out_shape=(part, jax.ShapeDtypeStruct((2, half_rows, LANES), F32), part),
        in_specs=[smem] + [vmem] * (len(ops) - 1),
        out_specs=(vmem, vmem, vmem),
        scratch_shapes=[pltpu.VMEM((n_rel, SPAN), BF16)],
        compiler_params=pltpu.CompilerParams(vmem_limit_bytes=48 * 1024 * 1024),
        name="bucket_round",
    )(*ops)


def join_kernel(half_tiles, core, mine, other, out):
    width = out.shape[0]
    n_tiles = out.shape[1] // LANES

    def put(halves):
        for tile in range(n_tiles):
            half, at = place(tile, half_tiles)
            out[:, tile * LANES:(tile + 1) * LANES] = halves[half][at * width:(at + 1) * width, :]

    @pl.when(core[0] == 0)
    def _():
        put((mine, other))

    @pl.when(core[0] != 0)
    def _():
        put((other, mine))


def join_relations(core, mine, other, shape):
    half_tiles = -(-(shape[1] // LANES) // 2)
    vmem = pl.BlockSpec(memory_space=pltpu.VMEM)
    smem = pl.BlockSpec(memory_space=pltpu.SMEM)
    return pl.pallas_call(
        functools.partial(join_kernel, half_tiles),
        out_shape=jax.ShapeDtypeStruct(shape, F32),
        in_specs=[smem, vmem, vmem],
        out_specs=vmem,
        compiler_params=pltpu.CompilerParams(vmem_limit_bytes=24 * 1024 * 1024),
        name="join_relations",
    )(core, mine, other)


def shifted(value, axes, steps):
    count = 1
    for axis in axes:
        count *= lax.axis_size(axis)
    return lax.ppermute(value, axes, [(a, (a + steps) % count) for a in range(count)])


def shifted_by(value, axes, steps):
    for unit in (1, 4, 16):
        digit = (steps // unit) % 4
        moved = [value] + [shifted(value, axes, unit * d) for d in (1, 2, 3)]
        value = jnp.where(
            digit < 2,
            jnp.where(digit == 0, moved[0], moved[1]),
            jnp.where(digit == 2, moved[2], moved[3]),
        )
    return value


def swap(value, axis):
    return lax.ppermute(value, axis, [(0, 1), (1, 0)])


def pick(value, index, axis):
    return lax.dynamic_index_in_dim(value, index, axis, keepdims=False)


def per_device(
    entity_table, relation_diag, plan, edge_count, src_rows, dst_rows, rel_ids, neg_rows
):
    n_dom = 64
    rounds = plan.shape[0]
    blocks_dev = neg_rows.shape[1]
    width, quarter = entity_table.shape
    dom_index = lax.axis_index(DOM)
    rep_index = lax.axis_index(REP)
    core = lax.axis_index("core")
    x_high = lax.axis_index("xh")

    known = jnp.array(KNOWN, jnp.int32)
    is_known = (plan[:, None] == known[None, :]).any(axis=1)
    free_row = jnp.argmin(is_known.astype(jnp.int32)).astype(jnp.int32)
    free_offset = plan[free_row]
    order = [jnp.argmax((plan == k).astype(jnp.int32)).astype(jnp.int32) for k in KNOWN]
    rows = [order[0], order[1], order[2], free_row]

    free_quarter = shifted_by(entity_table, DOM, (n_dom - free_offset) % n_dom)
    src_q = lax.all_gather(entity_table, REP, axis=0, tiled=False)
    dst_parts = [shifted(src_q, DOM, n_dom - k) for k in KNOWN]
    dst_parts.append(lax.all_gather(free_quarter, REP, axis=0, tiled=False))

    first_block = rep_index * blocks_dev
    carried = ()
    returns = []
    for row, dst_q in zip(rows, dst_parts):
        count = edge_count[row, dom_index]
        total = (count + SPAN - 1) // SPAN
        used = jnp.clip(total - first_block, 0, blocks_dev)
        meta = jnp.stack([row, used, count, first_block, jnp.int32(1)]).astype(jnp.int32)
        src_acc, rel_acc, dst_acc = run_round(
            meta, src_q, dst_q, relation_diag, src_rows, dst_rows, rel_ids, neg_rows, carried
        )
        carried = (src_acc, rel_acc)
        returns.append(dst_acc)

    half = pick(rel_acc, core, 0) + swap(pick(rel_acc, 1 - core, 0), "core")
    pieces = lax.all_to_all(half, CHIPS, 0, 0, tiled=True)
    peers = 128
    piece = pieces.reshape(peers, -1, LANES).sum(axis=0)
    whole = lax.all_to_all(jnp.tile(piece, (peers, 1)), CHIPS, 0, 0, tiled=True)
    relation_grad = join_relations(
        core.astype(jnp.int32).reshape(1), whole, swap(whole, "core"), relation_diag.shape
    )

    parts = jnp.stack(returns + [src_acc]).reshape(rounds + 1, 2, 2, width, quarter)
    parts = pick(parts, core, 2) + swap(pick(parts, 1 - core, 2), "core")
    parts = pick(parts, x_high, 1) + swap(pick(parts, 1 - x_high, 1), "xh")
    entity_grad = parts[rounds]
    for at, k in enumerate(KNOWN):
        entity_grad = entity_grad + shifted(parts[at], DOM, k)
    entity_grad = entity_grad + shifted_by(parts[rounds - 1], DOM, free_offset)
    return entity_grad, relation_grad


def solution(mesh):
    fine = Mesh(mesh.devices.reshape(4, 8, 2, 2, 2), DOM + REP)
    cols = P(None, DOM + REP)
    in_specs = (cols, P(), P(), P(), cols, cols, cols, P(None, DOM + REP, None))
    return jax.shard_map(
        per_device, mesh=fine, in_specs=in_specs, out_specs=(cols, P()), check_vma=False
    )
```

```python
import functools

import jax
import jax.numpy as jnp
from jax import lax
from jax.experimental import pallas as pl
from jax.experimental.pallas import tpu as pltpu
from jax.sharding import Mesh, PartitionSpec as P

DOM = ("y", "z", "xl")
REP = ("xh", "core")
CHIPS = ("y", "z", "xl", "xh")
LANES = 128
SPAN = 256
KNOWN = (1, 32, 63)
N_DOM = 64
GROUP = 2
F32 = jnp.float32
BF16 = jnp.bfloat16


def mm(a, b):
    return jnp.dot(a, b, preferred_element_type=F32)


def mm_nt(a, b):
    return lax.dot_general(a, b, (((1,), (1,)), ((), ())), preferred_element_type=F32)


def one_hot(index, height):
    rows = lax.broadcasted_iota(jnp.int32, (height, index.shape[1]), 0)
    return jnp.where(rows == index, 1.0, 0.0).astype(BF16)


def rel_chunks(n_rel):
    return [(a, min(2 * LANES, n_rel - a)) for a in range(0, n_rel, 2 * LANES)]


def place(tile, half_tiles):
    return (0, tile) if tile < half_tiles else (1, tile - half_tiles)


def bucket_row(known, plan):
    row = jnp.int32(0)
    for r in range(plan.shape[0]):
        if known is None:
            hit = plan[r] != KNOWN[0]
            for k in KNOWN[1:]:
                hit = jnp.logical_and(hit, plan[r] != k)
        else:
            hit = plan[r] == known
        row = jnp.where(hit, r, row)
    return row


def pack_kernel(where, srcs, dsts, rels, negs, *packs):
    n_rep = len(packs)
    rounds = srcs.shape[0]
    for s, out in enumerate(packs):
        for r in range(rounds):
            k = lax.rem(where[1] + (s - r) % n_rep, n_rep)
            lanes = pl.ds(pl.multiple_of(k * SPAN, SPAN), SPAN)
            out[r:r + 1, 0:SPAN] = srcs[r:r + 1, lanes]
            out[r:r + 1, SPAN:2 * SPAN] = dsts[r:r + 1, lanes]
            out[r:r + 1, 2 * SPAN:3 * SPAN] = rels[r:r + 1, lanes]
            out[r:r + 1, 3 * SPAN:] = negs[r, pl.ds(k, 1), :]


def pack_indices(where, srcs, dsts, rels, negs):
    rounds, n_rep, n_neg = negs.shape
    vmem = pl.BlockSpec(memory_space=pltpu.VMEM)
    smem = pl.BlockSpec(memory_space=pltpu.SMEM)
    pack = jax.ShapeDtypeStruct((rounds, 3 * SPAN + n_neg), jnp.int32)
    return pl.pallas_call(
        pack_kernel,
        out_shape=(pack,) * n_rep,
        in_specs=[smem] + [vmem] * 4,
        out_specs=(vmem,) * n_rep,
        name="pack_indices",
    )(where, srcs, dsts, rels, negs)


def round_kernel(known, n_in, half_tiles, plan, edge_count, where, *refs):
    ins, rest = refs[:n_in], refs[n_in:]
    if known is None:
        src_q, d0, d1, d2, d3, rel, *packs = ins
        dst_pieces = (d0, d1, d2, d3)
    else:
        src_q, dst_q, rel, *packs = ins
    src_o, rel_o, dst_o, hot, idx, dst_buf = rest
    n_rep = src_q.shape[0]
    if len(packs) > n_rep:
        packs, (src_in, rel_in) = packs[:n_rep], packs[n_rep:]
        src_o[...] = src_in[...]
        rel_o[...] = rel_in[...]
    else:
        src_o[...] = jnp.zeros_like(src_o)
        rel_o[...] = jnp.zeros_like(rel_o)
    dst_o[...] = jnp.zeros_like(dst_o)
    width, n_rel = rel.shape
    row = bucket_row(known, plan)
    dom, rep = where[0], where[1]
    count = edge_count[row, dom]
    total = (count + (SPAN - 1)) // SPAN
    lane = lax.rem(rep - row + n_rep, n_rep)
    used = jnp.maximum(total - lane + (n_rep - 1), 0) // n_rep
    for s in range(n_rep):
        origin = lax.rem(rep + (n_rep - s), n_rep)
        idx[pl.ds(origin, 1), :] = packs[s][pl.ds(row, 1), :]
        if known is None:
            dst_buf[origin] = dst_pieces[s][...]
        else:
            dst_buf[s] = dst_q[s]
    src_t = jnp.concatenate([src_q[q] for q in range(n_rep)], axis=1)
    dst_t = jnp.concatenate([dst_buf[q] for q in range(n_rep)], axis=1)
    dst_wide = dst_t.astype(F32)
    dst_rows = dst_wide.T.astype(BF16)
    part = src_t.shape[1]
    n_neg = idx.shape[1] - 3 * SPAN
    scale = n_neg ** -0.5
    span = GROUP * SPAN

    def take(first_row, a, n):
        return [idx[pl.ds(first_row + g, 1), a:a + n] for g in range(GROUP)]

    def one_group(i, carry):
        first_row = i * GROUP
        src_i = jnp.concatenate(take(first_row, 0, SPAN), axis=1)
        dst_i = jnp.concatenate(take(first_row, SPAN, SPAN), axis=1)
        rel_i = jnp.concatenate(take(first_row, 2 * SPAN, SPAN), axis=1)
        neg_i = take(first_row, 3 * SPAN, n_neg)
        at = lax.broadcasted_iota(jnp.int32, (1, SPAN), 1)
        live = jnp.concatenate(
            [
                (((first_row + g) * n_rep + lane) * SPAN + at < count).astype(F32)
                for g in range(GROUP)
            ],
            axis=1,
        )
        src_hot = one_hot(src_i, part)
        dst_hot = one_hot(dst_i, part)
        w = jnp.zeros((width, span), F32)
        for a, n in rel_chunks(n_rel):
            chunk = one_hot(rel_i - a, n)
            hot[a:a + n, :] = chunk
            w = w + mm(rel[:, a:a + n], chunk)
        s = mm(src_t, src_hot)
        t = mm(dst_t, dst_hot)
        lhs = (s * w).astype(BF16)
        lhs_wide = lhs.astype(F32)
        positive = jnp.sum(lhs_wide * t, axis=0, keepdims=True)
        pos_weight = -live * jax.nn.sigmoid(-positive)
        scores = mm(dst_rows, lhs)
        weight = ((live * scale) * jax.nn.sigmoid(scores)).astype(BF16)
        from_neg = []
        dst_part = mm_nt((pos_weight * lhs_wide).astype(BF16), dst_hot)
        for g in range(GROUP):
            edges = slice(g * SPAN, (g + 1) * SPAN)
            low = one_hot(jnp.bitwise_and(neg_i[g], LANES - 1), LANES)
            high = one_hot(jnp.right_shift(neg_i[g], 7), 16)
            times = mm_nt(high, low)
            times = jnp.concatenate([times[q:q + 1, :] for q in range(n_rep)], axis=1)
            counted = times * dst_wide
            counted_hi = counted.astype(BF16)
            counted_lo = (counted - counted_hi.astype(F32)).astype(BF16)
            from_neg.append(mm(counted_hi, weight[:, edges]) + mm(counted_lo, weight[:, edges]))
            grad_neg = mm_nt(lhs[:, edges], weight[:, edges]).astype(BF16).astype(F32)
            dst_part = dst_part + times * grad_neg
        grad_lhs = pos_weight * t + jnp.concatenate(from_neg, axis=1)
        grad_src = (grad_lhs * w).astype(BF16)
        grad_rel = (grad_lhs * s).astype(BF16)
        src_part = mm_nt(grad_src, src_hot)
        for q in range(n_rep):
            cols = slice(q * LANES, (q + 1) * LANES)
            src_o[q] += src_part[:, cols]
            dst_o[q] += dst_part[:, cols]
        for a, n in rel_chunks(n_rel):
            term = mm_nt(grad_rel, hot[a:a + n, :])
            for b in range(n // LANES):
                half, tile = place(a // LANES + b, half_tiles)
                rel_o[half, tile * width:(tile + 1) * width, :] += term[:, b * LANES:(b + 1) * LANES]
        return carry

    lax.fori_loop(0, (used + (GROUP - 1)) // GROUP, one_group, 0)


def run_round(known, plan, edge_count, where, src_q, dst, rel, packs, carried):
    n_q, width, lanes = src_q.shape
    n_rel = rel.shape[1]
    half_tiles = -(-(n_rel // LANES) // 2)
    half_rows = -(-half_tiles * width // 2048) * 2048
    vmem = pl.BlockSpec(memory_space=pltpu.VMEM)
    smem = pl.BlockSpec(memory_space=pltpu.SMEM)
    part = jax.ShapeDtypeStruct((n_q, width, lanes), F32)
    ops = [src_q, *dst, rel, *packs, *carried]
    return pl.pallas_call(
        functools.partial(round_kernel, known, len(ops), half_tiles),
        out_shape=(part, jax.ShapeDtypeStruct((2, half_rows, LANES), F32), part),
        in_specs=[smem] * 3 + [vmem] * len(ops),
        out_specs=(vmem, vmem, vmem),
        scratch_shapes=[
            pltpu.VMEM((n_rel, GROUP * SPAN), BF16),
            pltpu.VMEM((n_q, packs[0].shape[1]), jnp.int32),
            pltpu.VMEM((n_q, width, lanes), BF16),
        ],
        compiler_params=pltpu.CompilerParams(vmem_limit_bytes=32 * 1024 * 1024),
        cost_estimate=pl.CostEstimate(flops=9 * 10 ** 9, bytes_accessed=6 * 10 ** 6, transcendentals=0),
        name="bucket_round",
    )(plan, edge_count, where, *ops)


def choose_kernel(unit, sign, plan, v0, v1, v2, v3, out):
    offset = plan[0]
    for r in range(1, plan.shape[0]):
        offset = offset + plan[r]
    offset = offset - sum(KNOWN)
    if sign < 0:
        offset = N_DOM - offset
    digit = lax.rem(lax.div(offset, jnp.int32(unit)), jnp.int32(4))
    for d, v in enumerate((v0, v1, v2, v3)):
        @pl.when(digit == d)
        def _(v=v):
            out[...] = v[...]


def choose(unit, sign, plan, values):
    vmem = pl.BlockSpec(memory_space=pltpu.VMEM)
    smem = pl.BlockSpec(memory_space=pltpu.SMEM)
    return pl.pallas_call(
        functools.partial(choose_kernel, unit, sign),
        out_shape=jax.ShapeDtypeStruct(values[0].shape, values[0].dtype),
        in_specs=[smem] + [vmem] * 4,
        out_specs=vmem,
        name="choose",
    )(plan, *values)


def join_kernel(half_tiles, core, mine, other, out):
    width = out.shape[0]
    n_tiles = out.shape[1] // LANES

    def put(halves):
        for tile in range(n_tiles):
            half, at = place(tile, half_tiles)
            out[:, tile * LANES:(tile + 1) * LANES] = halves[half][at * width:(at + 1) * width, :]

    @pl.when(core[0] == 0)
    def _():
        put((mine, other))

    @pl.when(core[0] != 0)
    def _():
        put((other, mine))


def join_relations(core, mine, other, shape):
    half_tiles = -(-(shape[1] // LANES) // 2)
    vmem = pl.BlockSpec(memory_space=pltpu.VMEM)
    smem = pl.BlockSpec(memory_space=pltpu.SMEM)
    return pl.pallas_call(
        functools.partial(join_kernel, half_tiles),
        out_shape=jax.ShapeDtypeStruct(shape, F32),
        in_specs=[smem, vmem, vmem],
        out_specs=vmem,
        compiler_params=pltpu.CompilerParams(vmem_limit_bytes=24 * 1024 * 1024),
        name="join_relations",
    )(core, mine, other)


def shifted(value, axes, steps):
    count = 1
    for axis in axes:
        count *= lax.axis_size(axis)
    return lax.ppermute(value, axes, [(a, (a + steps) % count) for a in range(count)])


def options(value, axes, unit):
    return [value] + [shifted(value, axes, unit * d) for d in (1, 2, 3)]


def swap(value, axis):
    return lax.ppermute(value, axis, [(0, 1), (1, 0)])


def pick(value, index, axis):
    return lax.dynamic_index_in_dim(value, index, axis, keepdims=False)


def together(*values):
    return lax.optimization_barrier(values)


def per_device(
    entity_table, relation_diag, plan, edge_count, src_rows, dst_rows, rel_ids, neg_rows
):
    rounds = plan.shape[0]
    width, quarter = entity_table.shape
    core = lax.axis_index("core")
    x_high = lax.axis_index("xh")
    where = jnp.stack([lax.axis_index(DOM), lax.axis_index(REP)]).astype(jnp.int32)

    packed = pack_indices(where, src_rows, dst_rows, rel_ids, neg_rows)
    packs = [packed[0]] + [shifted(packed[s], REP, s) for s in (1, 2, 3)]
    hop = options(entity_table, DOM, 1)
    src_q = lax.all_gather(entity_table, REP, axis=0, tiled=False)
    dst_parts = [(shifted(src_q, DOM, N_DOM - k),) for k in KNOWN]

    def go(known, dst, carried):
        return run_round(
            known, plan, edge_count, where, src_q, dst, relation_diag, packs, carried
        )

    free = choose(1, -1, plan, hop)
    first, free = together(dst_parts[0][0], free)
    hop = options(free, DOM, 4)
    src_acc, rel_acc, dst_1 = go(KNOWN[0], (first,), ())
    *hop, src_acc = together(*hop, src_acc)
    free = choose(4, -1, plan, hop)
    second, free = together(dst_parts[1][0], free)
    hop = options(free, DOM, 16)
    src_acc, rel_acc, dst_2 = go(KNOWN[1], (second,), (src_acc, rel_acc))
    *hop, src_acc = together(*hop, src_acc)
    free = choose(16, -1, plan, hop)
    third, free = together(dst_parts[2][0], free)
    pieces = [free] + [shifted(free, REP, s) for s in (1, 2, 3)]
    src_acc, rel_acc, dst_3 = go(KNOWN[2], (third,), (src_acc, rel_acc))
    *pieces, src_acc = together(*pieces, src_acc)
    src_acc, rel_acc, dst_4 = go(None, pieces, (src_acc, rel_acc))

    half = pick(rel_acc, core, 0) + swap(pick(rel_acc, 1 - core, 0), "core")
    pieces = lax.all_to_all(half, CHIPS, 0, 0, tiled=True)

    parts = jnp.stack([dst_1, dst_2, dst_3, dst_4, src_acc])
    parts = parts.reshape(rounds + 1, 2, 2, width, quarter)
    parts = pick(parts, core, 2) + swap(pick(parts, 1 - core, 2), "core")
    parts = pick(parts, x_high, 1) + swap(pick(parts, 1 - x_high, 1), "xh")
    pieces, parts = together(pieces, parts)

    peers = 128
    piece = pieces.reshape(peers, -1, LANES).sum(axis=0)
    whole = lax.all_to_all(jnp.tile(piece, (peers, 1)), CHIPS, 0, 0, tiled=True)

    entity_grad = parts[rounds]
    for at, k in enumerate(KNOWN):
        entity_grad = entity_grad + shifted(parts[at], DOM, k)
    back = parts[rounds - 1]
    for unit in (1, 4, 16):
        back = choose(unit, 1, plan, options(back, DOM, unit))
    entity_grad = entity_grad + back
    whole, entity_grad = together(whole, entity_grad)
    relation_grad = join_relations(
        core.astype(jnp.int32).reshape(1), whole, swap(whole, "core"), relation_diag.shape
    )
    return entity_grad, relation_grad


def solution(mesh):
    fine = Mesh(mesh.devices.reshape(4, 8, 2, 2, 2), DOM + REP)
    cols = P(None, DOM + REP)
    in_specs = (cols, P(), P(), P(), cols, cols, cols, P(None, DOM + REP, None))
    return jax.shard_map(
        per_device, mesh=fine, in_specs=in_specs, out_specs=(cols, P()), check_vma=False
    )
```

```python
import functools

import jax
import jax.numpy as jnp
from jax import lax
from jax.experimental import pallas as pl
from jax.experimental.pallas import tpu as pltpu
from jax.sharding import Mesh, PartitionSpec as P

DOM = ("y", "z", "xl")
REP = ("xh", "core")
CHIPS = ("y", "z", "xl", "xh")
LANES = 128
SPAN = 256
KNOWN = (1, 32, 63)
N_DOM = 64
GROUP = 2
F32 = jnp.float32
BF16 = jnp.bfloat16


def mm(a, b):
    return jnp.dot(a, b, preferred_element_type=F32)


def mm_nt(a, b):
    return lax.dot_general(a, b, (((1,), (1,)), ((), ())), preferred_element_type=F32)


def one_hot(index, height):
    rows = lax.broadcasted_iota(jnp.int32, (height, index.shape[1]), 0)
    return jnp.where(rows == index, 1.0, 0.0).astype(BF16)


def rel_chunks(n_rel):
    return [(a, min(2 * LANES, n_rel - a)) for a in range(0, n_rel, 2 * LANES)]


def place(tile, half_tiles):
    return (0, tile) if tile < half_tiles else (1, tile - half_tiles)


def bucket_row(known, plan):
    row = jnp.int32(0)
    for r in range(plan.shape[0]):
        if known is None:
            hit = plan[r] != KNOWN[0]
            for k in KNOWN[1:]:
                hit = jnp.logical_and(hit, plan[r] != k)
        else:
            hit = plan[r] == known
        row = jnp.where(hit, r, row)
    return row


def pack_kernel(where, srcs, dsts, rels, negs, out):
    rounds, blocks, _ = negs.shape
    half = blocks // 2
    for r in range(rounds):
        away = lax.rem(where[1] + (r + 1), 2)
        for i in range(half):
            k = 2 * i + away
            at = r * half + i
            lanes = pl.ds(pl.multiple_of(k * SPAN, SPAN), SPAN)
            out[at:at + 1, 0:SPAN] = srcs[r:r + 1, lanes]
            out[at:at + 1, SPAN:2 * SPAN] = dsts[r:r + 1, lanes]
            out[at:at + 1, 2 * SPAN:3 * SPAN] = rels[r:r + 1, lanes]
            out[at:at + 1, 3 * SPAN:] = negs[r, pl.ds(k, 1), :]


def pack_indices(where, srcs, dsts, rels, negs):
    rounds, blocks, n_neg = negs.shape
    vmem = pl.BlockSpec(memory_space=pltpu.VMEM)
    smem = pl.BlockSpec(memory_space=pltpu.SMEM)
    return pl.pallas_call(
        pack_kernel,
        out_shape=jax.ShapeDtypeStruct((rounds * blocks // 2, 3 * SPAN + n_neg), jnp.int32),
        in_specs=[smem] + [vmem] * 4,
        out_specs=vmem,
        name="pack_indices",
    )(where, srcs, dsts, rels, negs)


def rounds_kernel(half_tiles, plan, edge_count, where, *refs):
    src_q, d0, d1, d2, d3, rel, srcs, dsts, rels, negs, pack = refs[:11]
    parts_keep, parts_send, rel_keep, rel_send = refs[11:15]
    acc, rel_acc, hot, idx, dst_buf = refs[15:]
    n_rep = src_q.shape[0]
    width, n_rel = rel.shape
    rounds, blocks, n_neg = negs.shape
    half = blocks // 2
    part = n_rep * LANES
    scale = n_neg ** -0.5
    span = GROUP * SPAN
    dom, high, core = where[0], where[1], where[2]

    acc[...] = jnp.zeros_like(acc)
    rel_acc[...] = jnp.zeros_like(rel_acc)
    for i, d in enumerate((d0, d1, d2, d3)):
        dst_buf[i] = jnp.concatenate([d[q] for q in range(n_rep)], axis=1)
    for r in range(rounds):
        home = lax.rem(high + r, 2)
        for i in range(half):
            lanes = pl.ds(pl.multiple_of((2 * i + home) * SPAN, SPAN), SPAN)
            mine = pl.ds(r * blocks + half * high + i, 1)
            idx[mine, 0:SPAN] = srcs[r:r + 1, lanes]
            idx[mine, SPAN:2 * SPAN] = dsts[r:r + 1, lanes]
            idx[mine, 2 * SPAN:3 * SPAN] = rels[r:r + 1, lanes]
            idx[mine, 3 * SPAN:] = negs[r, pl.ds(2 * i + home, 1), :]
            other = pl.ds(r * blocks + half * (1 - high) + i, 1)
            idx[other, :] = pack[r * half + i:r * half + i + 1, :]
    src_t = jnp.concatenate([src_q[q] for q in range(n_rep)], axis=1)
    known_rows = [bucket_row(known, plan) for known in KNOWN + (None,)]

    def one_round(which, carry):
        row = known_rows[rounds - 1]
        for i in range(rounds - 1):
            row = jnp.where(which == i, known_rows[i], row)
        count = edge_count[row, dom]
        total = (count + (SPAN - 1)) // SPAN
        home = lax.rem(high + row, 2)

        def global_block(i):
            return (i // half) * (2 * blocks) + core * blocks + 2 * (i % half) + home

        used = jnp.int32(0)
        for i in range(blocks):
            used = used + (global_block(i) < total).astype(jnp.int32)
        dst_t = dst_buf[which]
        dst_wide = dst_t.astype(F32)
        dst_rows = dst_wide.T.astype(BF16)

        def one_group(step, inner):
            first = step * GROUP
            at = row * blocks + first

            def take(a, n):
                return [idx[pl.ds(at + g, 1), a:a + n] for g in range(GROUP)]

            src_i = jnp.concatenate(take(0, SPAN), axis=1)
            dst_i = jnp.concatenate(take(SPAN, SPAN), axis=1)
            rel_i = jnp.concatenate(take(2 * SPAN, SPAN), axis=1)
            neg_i = take(3 * SPAN, n_neg)
            lane = lax.broadcasted_iota(jnp.int32, (1, SPAN), 1)
            live = jnp.concatenate(
                [
                    (global_block(first + g) * SPAN + lane < count).astype(F32)
                    for g in range(GROUP)
                ],
                axis=1,
            )
            src_hot = one_hot(src_i, part)
            dst_hot = one_hot(dst_i, part)
            w = jnp.zeros((width, span), F32)
            for a, n in rel_chunks(n_rel):
                chunk = one_hot(rel_i - a, n)
                hot[a:a + n, :] = chunk
                w = w + mm(rel[:, a:a + n], chunk)
            s = mm(src_t, src_hot)
            t = mm(dst_t, dst_hot)
            lhs = (s * w).astype(BF16)
            lhs_wide = lhs.astype(F32)
            positive = jnp.sum(lhs_wide * t, axis=0, keepdims=True)
            pos_weight = -live * jax.nn.sigmoid(-positive)
            scores = mm(dst_rows, lhs)
            weight = ((live * scale) * jax.nn.sigmoid(scores)).astype(BF16)
            from_neg = []
            dst_part = mm_nt((pos_weight * lhs_wide).astype(BF16), dst_hot)
            for g in range(GROUP):
                edges = slice(g * SPAN, (g + 1) * SPAN)
                low = one_hot(jnp.bitwise_and(neg_i[g], LANES - 1), LANES)
                far = one_hot(jnp.right_shift(neg_i[g], 7), 16)
                times = mm_nt(far, low)
                times = jnp.concatenate([times[q:q + 1, :] for q in range(n_rep)], axis=1)
                counted = times * dst_wide
                counted_hi = counted.astype(BF16)
                counted_lo = (counted - counted_hi.astype(F32)).astype(BF16)
                from_neg.append(
                    mm(counted_hi, weight[:, edges]) + mm(counted_lo, weight[:, edges])
                )
                grad_neg = mm_nt(lhs[:, edges], weight[:, edges]).astype(BF16).astype(F32)
                dst_part = dst_part + times * grad_neg
            grad_lhs = pos_weight * t + jnp.concatenate(from_neg, axis=1)
            grad_src = (grad_lhs * w).astype(BF16)
            grad_rel = (grad_lhs * s).astype(BF16)
            src_part = mm_nt(grad_src, src_hot)
            for q in range(n_rep):
                cols = slice(q * LANES, (q + 1) * LANES)
                acc[rounds, q] += src_part[:, cols]
                acc[which, q] += dst_part[:, cols]
            for a, n in rel_chunks(n_rel):
                term = mm_nt(grad_rel, hot[a:a + n, :])
                for b in range(n // LANES):
                    side, tile = place(a // LANES + b, half_tiles)
                    rel_acc[side, tile * width:(tile + 1) * width, :] += term[
                        :, b * LANES:(b + 1) * LANES
                    ]
            return inner

        lax.fori_loop(0, (used + (GROUP - 1)) // GROUP, one_group, 0)
        return carry

    lax.fori_loop(0, rounds, one_round, 0)
    rel_keep[...] = rel_acc[core]
    rel_send[...] = rel_acc[1 - core]
    for i in range(rounds + 1):
        for h in range(2):
            parts_keep[i, h] = acc[i, 2 * h + core]
            parts_send[i, h] = acc[i, 2 * h + 1 - core]


def run_rounds(plan, edge_count, where, src_q, dsts_q, rel, indices, pack):
    n_q, width, lanes = src_q.shape
    n_rel = rel.shape[1]
    rounds = plan.shape[0]
    half_tiles = -(-(n_rel // LANES) // 2)
    half_rows = -(-half_tiles * width // 2048) * 2048
    vmem = pl.BlockSpec(memory_space=pltpu.VMEM)
    smem = pl.BlockSpec(memory_space=pltpu.SMEM)
    parts = jax.ShapeDtypeStruct((rounds + 1, 2, width, lanes), F32)
    side = jax.ShapeDtypeStruct((half_rows, LANES), F32)
    ops = [src_q, *dsts_q, rel, *indices, pack]
    return pl.pallas_call(
        functools.partial(rounds_kernel, half_tiles),
        out_shape=(parts, parts, side, side),
        in_specs=[smem] * 3 + [vmem] * len(ops),
        out_specs=(vmem,) * 4,
        scratch_shapes=[
            pltpu.VMEM((rounds + 1, n_q, width, lanes), F32),
            pltpu.VMEM((2, half_rows, LANES), F32),
            pltpu.VMEM((n_rel, GROUP * SPAN), BF16),
            pltpu.VMEM((2 * pack.shape[0], pack.shape[1]), jnp.int32),
            pltpu.VMEM((rounds, width, n_q * lanes), BF16),
        ],
        compiler_params=pltpu.CompilerParams(vmem_limit_bytes=40 * 1024 * 1024),
        cost_estimate=pl.CostEstimate(flops=2 * 10 ** 10, bytes_accessed=10 ** 7, transcendentals=0),
        name="bucket_rounds",
    )(plan, edge_count, where, *ops)


def join_kernel(half_tiles, core, mine, other, out):
    width = out.shape[0]
    n_tiles = out.shape[1] // LANES

    def put(halves):
        for tile in range(n_tiles):
            half, at = place(tile, half_tiles)
            out[:, tile * LANES:(tile + 1) * LANES] = halves[half][at * width:(at + 1) * width, :]

    @pl.when(core[0] == 0)
    def _():
        put((mine, other))

    @pl.when(core[0] != 0)
    def _():
        put((other, mine))


def join_relations(core, mine, other, shape):
    half_tiles = -(-(shape[1] // LANES) // 2)
    vmem = pl.BlockSpec(memory_space=pltpu.VMEM)
    smem = pl.BlockSpec(memory_space=pltpu.SMEM)
    return pl.pallas_call(
        functools.partial(join_kernel, half_tiles),
        out_shape=jax.ShapeDtypeStruct(shape, F32),
        in_specs=[smem, vmem, vmem],
        out_specs=vmem,
        compiler_params=pltpu.CompilerParams(vmem_limit_bytes=24 * 1024 * 1024),
        name="join_relations",
    )(core, mine, other)


def shifted(value, axes, steps):
    count = 1
    for axis in axes:
        count *= lax.axis_size(axis)
    return lax.ppermute(value, axes, [(a, (a + steps) % count) for a in range(count)])


def shifted_by(value, axes, steps):
    for unit in (1, 8):
        moves = [
            functools.partial(shifted, axes=axes, steps=unit * d) if d else (lambda v: v)
            for d in range(8)
        ]
        value = lax.switch((steps // unit) % 8, moves, value)
    return value


def swap(value, axis):
    return lax.ppermute(value, axis, [(0, 1), (1, 0)])


def pick(value, index, axis):
    return lax.dynamic_index_in_dim(value, index, axis, keepdims=False)


def together(*values):
    return lax.optimization_barrier(values)


def per_device(
    entity_table, relation_diag, plan, edge_count, src_rows, dst_rows, rel_ids, neg_rows
):
    rounds = plan.shape[0]
    core = lax.axis_index("core")
    x_high = lax.axis_index("xh")
    where = jnp.stack([lax.axis_index(DOM), x_high, core]).astype(jnp.int32)
    free_offset = jnp.sum(plan) - sum(KNOWN)
    indices = (src_rows, dst_rows, rel_ids, neg_rows)

    pack = swap(pack_indices(where, *indices), "xh")
    src_q = lax.all_gather(entity_table, REP, axis=0, tiled=False)
    dst_parts = [shifted(src_q, DOM, N_DOM - k) for k in KNOWN]
    free, src_q = together(entity_table, src_q)
    free = shifted_by(free, DOM, N_DOM - free_offset)
    dst_parts.append(lax.all_gather(free, REP, axis=0, tiled=False))
    parts, parts_send, half, half_send = run_rounds(
        plan, edge_count, where, src_q, dst_parts, relation_diag, indices, pack
    )

    half = half + swap(half_send, "core")
    pieces = lax.all_to_all(half, CHIPS, 0, 0, tiled=True)
    parts = parts + swap(parts_send, "core")
    parts = pick(parts, x_high, 1) + swap(pick(parts, 1 - x_high, 1), "xh")
    pieces, parts = together(pieces, parts)

    peers = 128
    piece = pieces.reshape(peers, -1, LANES).sum(axis=0)
    whole = lax.all_to_all(jnp.tile(piece, (peers, 1)), CHIPS, 0, 0, tiled=True)

    entity_grad = parts[rounds]
    for at, k in enumerate(KNOWN):
        entity_grad = entity_grad + shifted(parts[at], DOM, k)
    entity_grad = entity_grad + shifted_by(parts[rounds - 1], DOM, free_offset)
    whole, entity_grad = together(whole, entity_grad)
    relation_grad = join_relations(
        core.astype(jnp.int32).reshape(1), whole, swap(whole, "core"), relation_diag.shape
    )
    return entity_grad, relation_grad


def solution(mesh):
    fine = Mesh(mesh.devices.reshape(4, 8, 2, 2, 2), DOM + REP)
    cols = P(None, DOM + REP)
    in_specs = (cols, P(), P(), P(), cols, cols, cols, P(None, DOM + REP, None))
    return jax.shard_map(
        per_device, mesh=fine, in_specs=in_specs, out_specs=(cols, P()), check_vma=False
    )
```

```python
import functools

import jax
import jax.numpy as jnp
from jax import lax
from jax.experimental import pallas as pl
from jax.experimental.pallas import tpu as pltpu
from jax.sharding import Mesh, PartitionSpec as P

DOM = ("y", "z", "xl")
REP = ("xh", "core")
CHIPS = ("y", "z", "xl", "xh")
LANES = 128
SPAN = 256
KNOWN = (1, 32, 63)
N_DOM = 64
GROUP = 2
F32 = jnp.float32
BF16 = jnp.bfloat16


def mm(a, b):
    return jnp.dot(a, b, preferred_element_type=F32)


def mm_nt(a, b):
    return lax.dot_general(a, b, (((1,), (1,)), ((), ())), preferred_element_type=F32)


def one_hot(index, height):
    rows = lax.broadcasted_iota(jnp.int32, (height, index.shape[1]), 0)
    return jnp.where(rows == index, 1.0, 0.0).astype(BF16)


def rel_chunks(n_rel):
    return [(a, min(2 * LANES, n_rel - a)) for a in range(0, n_rel, 2 * LANES)]


def place(tile, half_tiles):
    return (0, tile) if tile < half_tiles else (1, tile - half_tiles)


def bucket_row(known, plan):
    row = jnp.int32(0)
    for r in range(plan.shape[0]):
        if known is None:
            hit = plan[r] != KNOWN[0]
            for k in KNOWN[1:]:
                hit = jnp.logical_and(hit, plan[r] != k)
        else:
            hit = plan[r] == known
        row = jnp.where(hit, r, row)
    return row


def pack_kernel(plan, where, srcs, dsts, rels, negs, out, digits):
    rounds, blocks, _ = negs.shape
    half = blocks // 2
    offset = plan[0]
    for r in range(1, rounds):
        offset = offset + plan[r]
    offset = offset - sum(KNOWN)
    for i, steps in enumerate((N_DOM - offset, offset)):
        digits[2 * i] = lax.rem(steps, 8)
        digits[2 * i + 1] = lax.div(steps, jnp.int32(8))
    for r in range(rounds):
        away = lax.rem(where[1] + (r + 1), 2)
        for i in range(half):
            k = 2 * i + away
            at = r * half + i
            lanes = pl.ds(pl.multiple_of(k * SPAN, SPAN), SPAN)
            out[at:at + 1, 0:SPAN] = srcs[r:r + 1, lanes]
            out[at:at + 1, SPAN:2 * SPAN] = dsts[r:r + 1, lanes]
            out[at:at + 1, 2 * SPAN:3 * SPAN] = rels[r:r + 1, lanes]
            out[at:at + 1, 3 * SPAN:] = negs[r, pl.ds(k, 1), :]


def pack_indices(plan, where, srcs, dsts, rels, negs):
    rounds, blocks, n_neg = negs.shape
    vmem = pl.BlockSpec(memory_space=pltpu.VMEM)
    smem = pl.BlockSpec(memory_space=pltpu.SMEM)
    return pl.pallas_call(
        pack_kernel,
        out_shape=(
            jax.ShapeDtypeStruct((rounds * blocks // 2, 3 * SPAN + n_neg), jnp.int32),
            jax.ShapeDtypeStruct((4,), jnp.int32),
        ),
        in_specs=[smem] * 2 + [vmem] * 4,
        out_specs=(vmem, smem),
        name="pack_indices",
    )(plan, where, srcs, dsts, rels, negs)


def rounds_kernel(half_tiles, plan, edge_count, where, *refs):
    quarters, rel, srcs, dsts, rels, negs, pack = refs[:7]
    parts_keep, parts_send, rel_keep, rel_send = refs[7:11]
    acc, rel_acc, hot, idx, dst_buf = refs[11:]
    n_rep = quarters.shape[0]
    width, n_rel = rel.shape
    rounds, blocks, n_neg = negs.shape
    half = blocks // 2
    part = n_rep * LANES
    scale = n_neg ** -0.5
    span = GROUP * SPAN
    dom, high, core = where[0], where[1], where[2]

    acc[...] = jnp.zeros_like(acc)
    rel_acc[...] = jnp.zeros_like(rel_acc)
    for i in range(rounds):
        dst_buf[i] = jnp.concatenate([quarters[q, 1 + i] for q in range(n_rep)], axis=1)
    for r in range(rounds):
        home = lax.rem(high + r, 2)
        for i in range(half):
            lanes = pl.ds(pl.multiple_of((2 * i + home) * SPAN, SPAN), SPAN)
            mine = pl.ds(r * blocks + half * high + i, 1)
            idx[mine, 0:SPAN] = srcs[r:r + 1, lanes]
            idx[mine, SPAN:2 * SPAN] = dsts[r:r + 1, lanes]
            idx[mine, 2 * SPAN:3 * SPAN] = rels[r:r + 1, lanes]
            idx[mine, 3 * SPAN:] = negs[r, pl.ds(2 * i + home, 1), :]
            other = pl.ds(r * blocks + half * (1 - high) + i, 1)
            idx[other, :] = pack[r * half + i:r * half + i + 1, :]
    src_t = jnp.concatenate([quarters[q, 0] for q in range(n_rep)], axis=1)
    known_rows = [bucket_row(known, plan) for known in KNOWN + (None,)]

    def one_round(which, carry):
        row = known_rows[rounds - 1]
        for i in range(rounds - 1):
            row = jnp.where(which == i, known_rows[i], row)
        count = edge_count[row, dom]
        total = (count + (SPAN - 1)) // SPAN
        home = lax.rem(high + row, 2)

        def global_block(i):
            return (i // half) * (2 * blocks) + core * blocks + 2 * (i % half) + home

        used = jnp.int32(0)
        for i in range(blocks):
            used = used + (global_block(i) < total).astype(jnp.int32)
        dst_at = which + which // (rounds - 1)
        dst_t = dst_buf[which]
        dst_wide = dst_t.astype(F32)
        dst_rows = dst_wide.T.astype(BF16)

        def one_group(step, inner):
            first = step * GROUP
            at = row * blocks + first

            def take(a, n):
                return [idx[pl.ds(at + g, 1), a:a + n] for g in range(GROUP)]

            src_i = jnp.concatenate(take(0, SPAN), axis=1)
            dst_i = jnp.concatenate(take(SPAN, SPAN), axis=1)
            rel_i = jnp.concatenate(take(2 * SPAN, SPAN), axis=1)
            neg_i = take(3 * SPAN, n_neg)
            lane = lax.broadcasted_iota(jnp.int32, (1, SPAN), 1)
            live = jnp.concatenate(
                [
                    (global_block(first + g) * SPAN + lane < count).astype(F32)
                    for g in range(GROUP)
                ],
                axis=1,
            )
            src_hot = one_hot(src_i, part)
            dst_hot = one_hot(dst_i, part)
            w = jnp.zeros((width, span), F32)
            for a, n in rel_chunks(n_rel):
                chunk = one_hot(rel_i - a, n)
                hot[a:a + n, :] = chunk
                w = w + mm(rel[:, a:a + n], chunk)
            s = mm(src_t, src_hot)
            t = mm(dst_t, dst_hot)
            lhs = (s * w).astype(BF16)
            lhs_wide = lhs.astype(F32)
            positive = jnp.sum(lhs_wide * t, axis=0, keepdims=True)
            pos_weight = -live * jax.nn.sigmoid(-positive)
            scores = mm(dst_rows, lhs)
            weight = ((live * scale) * jax.nn.sigmoid(scores)).astype(BF16)
            from_neg = []
            dst_part = mm_nt((pos_weight * lhs_wide).astype(BF16), dst_hot)
            for g in range(GROUP):
                edges = slice(g * SPAN, (g + 1) * SPAN)
                low = one_hot(jnp.bitwise_and(neg_i[g], LANES - 1), LANES)
                far = one_hot(jnp.right_shift(neg_i[g], 7), 16)
                times = mm_nt(far, low)
                times = jnp.concatenate([times[q:q + 1, :] for q in range(n_rep)], axis=1)
                counted = times * dst_wide
                counted_hi = counted.astype(BF16)
                counted_lo = (counted - counted_hi.astype(F32)).astype(BF16)
                from_neg.append(
                    mm(counted_hi, weight[:, edges]) + mm(counted_lo, weight[:, edges])
                )
                grad_neg = mm_nt(lhs[:, edges], weight[:, edges]).astype(BF16).astype(F32)
                dst_part = dst_part + times * grad_neg
            grad_lhs = pos_weight * t + jnp.concatenate(from_neg, axis=1)
            grad_src = (grad_lhs * w).astype(BF16)
            grad_rel = (grad_lhs * s).astype(BF16)
            src_part = mm_nt(grad_src, src_hot)
            for q in range(n_rep):
                cols = slice(q * LANES, (q + 1) * LANES)
                acc[rounds - 1, q] += src_part[:, cols]
                acc[dst_at, q] += dst_part[:, cols]
            for a, n in rel_chunks(n_rel):
                term = mm_nt(grad_rel, hot[a:a + n, :])
                for b in range(n // LANES):
                    side, tile = place(a // LANES + b, half_tiles)
                    rel_acc[side, tile * width:(tile + 1) * width, :] += term[
                        :, b * LANES:(b + 1) * LANES
                    ]
            return inner

        lax.fori_loop(0, (used + (GROUP - 1)) // GROUP, one_group, 0)
        return carry

    lax.fori_loop(0, rounds, one_round, 0)
    rel_keep[...] = rel_acc[core]
    rel_send[...] = rel_acc[1 - core]
    for i in range(rounds + 1):
        for h, side in enumerate((high, 1 - high)):
            parts_keep[h, i] = acc[i, 2 * side + core]
            parts_send[h, i] = acc[i, 2 * side + 1 - core]


def run_rounds(plan, edge_count, where, quarters, rel, indices, pack):
    n_q, _, width, lanes = quarters.shape
    n_rel = rel.shape[1]
    rounds = plan.shape[0]
    half_tiles = -(-(n_rel // LANES) // 2)
    half_rows = -(-half_tiles * width // 2048) * 2048
    vmem = pl.BlockSpec(memory_space=pltpu.VMEM)
    smem = pl.BlockSpec(memory_space=pltpu.SMEM)
    parts = jax.ShapeDtypeStruct((2, rounds + 1, width, lanes), F32)
    side = jax.ShapeDtypeStruct((half_rows, LANES), F32)
    ops = [quarters, rel, *indices, pack]
    return pl.pallas_call(
        functools.partial(rounds_kernel, half_tiles),
        out_shape=(parts, parts, side, side),
        in_specs=[smem] * 3 + [vmem] * len(ops),
        out_specs=(vmem,) * 4,
        scratch_shapes=[
            pltpu.VMEM((rounds + 1, n_q, width, lanes), F32),
            pltpu.VMEM((2, half_rows, LANES), F32),
            pltpu.VMEM((n_rel, GROUP * SPAN), BF16),
            pltpu.VMEM((2 * pack.shape[0], pack.shape[1]), jnp.int32),
            pltpu.VMEM((rounds, width, n_q * lanes), BF16),
        ],
        compiler_params=pltpu.CompilerParams(vmem_limit_bytes=40 * 1024 * 1024),
        cost_estimate=pl.CostEstimate(flops=2 * 10 ** 10, bytes_accessed=10 ** 7, transcendentals=0),
        name="bucket_rounds",
    )(plan, edge_count, where, *ops)


def join_kernel(half_tiles, core, mine, other, out):
    width = out.shape[0]
    n_tiles = out.shape[1] // LANES

    def put(halves):
        for tile in range(n_tiles):
            half, at = place(tile, half_tiles)
            out[:, tile * LANES:(tile + 1) * LANES] = halves[half][at * width:(at + 1) * width, :]

    @pl.when(core[0] == 0)
    def _():
        put((mine, other))

    @pl.when(core[0] != 0)
    def _():
        put((other, mine))


def join_relations(core, mine, other, shape):
    half_tiles = -(-(shape[1] // LANES) // 2)
    vmem = pl.BlockSpec(memory_space=pltpu.VMEM)
    smem = pl.BlockSpec(memory_space=pltpu.SMEM)
    return pl.pallas_call(
        functools.partial(join_kernel, half_tiles),
        out_shape=jax.ShapeDtypeStruct(shape, F32),
        in_specs=[smem, vmem, vmem],
        out_specs=vmem,
        compiler_params=pltpu.CompilerParams(vmem_limit_bytes=24 * 1024 * 1024),
        name="join_relations",
    )(core, mine, other)


def shifted(value, axes, steps):
    count = 1
    for axis in axes:
        count *= lax.axis_size(axis)
    return lax.ppermute(value, axes, [(a, (a + steps) % count) for a in range(count)])


def crossed(value, axes, axis, steps):
    count = 1
    for name in axes:
        count *= lax.axis_size(name)
    pairs = [
        (2 * a + h, 2 * ((a + steps) % count) + 1 - h) for a in range(count) for h in range(2)
    ]
    return lax.ppermute(value, axes + (axis,), pairs)


def shifted_by(digit, unit, value):
    def move(d):
        return lambda v: shifted(v, DOM, unit * d) if d else v

    return lax.switch(digit, [move(d) for d in range(8)], value)


def gathered_by(digit, unit, keep, send):
    def move(d):
        return lambda k, s: (shifted(k, DOM, unit * d) if d else k) + crossed(
            s, DOM, "xh", unit * d
        )

    return lax.switch(digit, [move(d) for d in range(8)], keep, send)


def swap(value, axis):
    return lax.ppermute(value, axis, [(0, 1), (1, 0)])


def together(*values):
    return lax.optimization_barrier(values)


def per_device(
    entity_table, relation_diag, plan, edge_count, src_rows, dst_rows, rel_ids, neg_rows
):
    rounds = plan.shape[0]
    core = lax.axis_index("core")
    where = jnp.stack([lax.axis_index(DOM), lax.axis_index("xh"), core]).astype(jnp.int32)
    indices = (src_rows, dst_rows, rel_ids, neg_rows)

    known = [shifted(entity_table, DOM, N_DOM - k) for k in KNOWN]
    pack, digits = pack_indices(plan, where, *indices)
    pack = swap(pack, "xh")
    free = shifted_by(digits[0], 1, entity_table)
    free = shifted_by(digits[1], 8, free)
    quarters = jnp.stack([entity_table] + known + [free])
    quarters = lax.all_gather(quarters, REP, axis=0, tiled=False)
    parts, parts_send, half, half_send = run_rounds(
        plan, edge_count, where, quarters, relation_diag, indices, pack
    )

    half = half + swap(half_send, "core")
    pieces = lax.all_to_all(half, CHIPS, 0, 0, tiled=True)
    parts = parts + swap(parts_send, "core")
    free = gathered_by(digits[2], 1, parts[0, rounds], parts[1, rounds])
    parts = parts[0, :rounds] + swap(parts[1, :rounds], "xh")
    pieces, parts, free = together(pieces, parts, free)

    peers = 128
    piece = pieces.reshape(peers, -1, LANES).sum(axis=0)
    whole = lax.all_to_all(jnp.tile(piece, (peers, 1)), CHIPS, 0, 0, tiled=True)

    entity_grad = parts[rounds - 1]
    for at, k in enumerate(KNOWN):
        entity_grad = entity_grad + shifted(parts[at], DOM, k)
    entity_grad = entity_grad + shifted_by(digits[3], 8, free)
    whole, entity_grad = together(whole, entity_grad)
    relation_grad = join_relations(
        core.astype(jnp.int32).reshape(1), whole, swap(whole, "core"), relation_diag.shape
    )
    return entity_grad, relation_grad


def solution(mesh):
    fine = Mesh(mesh.devices.reshape(4, 8, 2, 2, 2), DOM + REP)
    cols = P(None, DOM + REP)
    in_specs = (cols, P(), P(), P(), cols, cols, cols, P(None, DOM + REP, None))
    return jax.shard_map(
        per_device, mesh=fine, in_specs=in_specs, out_specs=(cols, P()), check_vma=False
    )
```

```python
import functools

import jax
import jax.numpy as jnp
from jax import lax
from jax.experimental import pallas as pl
from jax.experimental.pallas import tpu as pltpu
from jax.sharding import Mesh, PartitionSpec as P

DOM = ("y", "z", "xl")
REP = ("xh", "core")
CHIPS = ("y", "z", "xl", "xh")
LANES = 128
SPAN = 256
KNOWN = (1, 63, 32)
N_DOM = 64
GROUP = 2
F32 = jnp.float32
BF16 = jnp.bfloat16


def mm(a, b):
    return jnp.dot(a, b, preferred_element_type=F32)


def mm_nt(a, b):
    return lax.dot_general(a, b, (((1,), (1,)), ((), ())), preferred_element_type=F32)


def one_hot(index, height):
    rows = lax.broadcasted_iota(jnp.int32, (height, index.shape[1]), 0)
    return jnp.where(rows == index, 1.0, 0.0).astype(BF16)


def rel_chunks(n_rel):
    return [(a, min(2 * LANES, n_rel - a)) for a in range(0, n_rel, 2 * LANES)]


def place(tile, half_tiles):
    return (0, tile) if tile < half_tiles else (1, tile - half_tiles)


def bucket_row(known, plan):
    row = jnp.int32(0)
    for r in range(plan.shape[0]):
        if known is None:
            hit = plan[r] != KNOWN[0]
            for k in KNOWN[1:]:
                hit = jnp.logical_and(hit, plan[r] != k)
        else:
            hit = plan[r] == known
        row = jnp.where(hit, r, row)
    return row


def pack_kernel(plan, where, srcs, dsts, rels, negs, out, digits):
    rounds, blocks, _ = negs.shape
    half = blocks // 2
    offset = plan[0]
    for r in range(1, rounds):
        offset = offset + plan[r]
    offset = offset - sum(KNOWN)
    for i, steps in enumerate((N_DOM - offset, offset)):
        digits[2 * i] = lax.rem(steps, 8)
        digits[2 * i + 1] = lax.div(steps, jnp.int32(8))
    for r in range(rounds):
        away = lax.rem(where[1] + (r + 1), 2)
        for i in range(half):
            k = 2 * i + away
            at = r * half + i
            lanes = pl.ds(pl.multiple_of(k * SPAN, SPAN), SPAN)
            out[at:at + 1, 0:SPAN] = srcs[r:r + 1, lanes]
            out[at:at + 1, SPAN:2 * SPAN] = dsts[r:r + 1, lanes]
            out[at:at + 1, 2 * SPAN:3 * SPAN] = rels[r:r + 1, lanes]
            out[at:at + 1, 3 * SPAN:] = negs[r, pl.ds(k, 1), :]


def pack_indices(plan, where, srcs, dsts, rels, negs):
    rounds, blocks, n_neg = negs.shape
    vmem = pl.BlockSpec(memory_space=pltpu.VMEM)
    smem = pl.BlockSpec(memory_space=pltpu.SMEM)
    return pl.pallas_call(
        pack_kernel,
        out_shape=(
            jax.ShapeDtypeStruct((rounds * blocks // 2, 3 * SPAN + n_neg), jnp.int32),
            jax.ShapeDtypeStruct((4,), jnp.int32),
        ),
        in_specs=[smem] * 2 + [vmem] * 4,
        out_specs=(vmem, smem),
        name="pack_indices",
    )(plan, where, srcs, dsts, rels, negs)


def rounds_kernel(half_tiles, plan, edge_count, where, *refs):
    quarters = refs[:6]
    rel, srcs, dsts, rels, negs, pack = refs[6:12]
    parts_keep, parts_send, rel_keep, rel_send = refs[12:16]
    acc, rel_acc, hot, idx, tables = refs[16:]
    n_rep = acc.shape[1]
    width, n_rel = rel.shape
    rounds, blocks, n_neg = negs.shape
    half = blocks // 2
    part = n_rep * LANES
    scale = n_neg ** -0.5
    span = GROUP * SPAN
    dom, high, core = where[0], where[1], where[2]

    acc[...] = jnp.zeros_like(acc)
    rel_acc[...] = jnp.zeros_like(rel_acc)
    sides = [(high, core), (1 - high, core), (high, 1 - core), (1 - high, 1 - core)]
    for (h, c), known_q, free_q in zip(
        sides,
        (quarters[0], quarters[1], quarters[3], quarters[4]),
        (quarters[2].at[0], quarters[2].at[1], quarters[5].at[0], quarters[5].at[1]),
    ):
        cols = pl.ds(pl.multiple_of((2 * h + c) * LANES, LANES), LANES)
        for i in range(rounds):
            tables[i, :, cols] = known_q[i]
        tables[rounds, :, cols] = free_q[...]
    for r in range(rounds):
        home = lax.rem(high + r, 2)
        for i in range(half):
            lanes = pl.ds(pl.multiple_of((2 * i + home) * SPAN, SPAN), SPAN)
            mine = pl.ds(r * blocks + half * high + i, 1)
            idx[mine, 0:SPAN] = srcs[r:r + 1, lanes]
            idx[mine, SPAN:2 * SPAN] = dsts[r:r + 1, lanes]
            idx[mine, 2 * SPAN:3 * SPAN] = rels[r:r + 1, lanes]
            idx[mine, 3 * SPAN:] = negs[r, pl.ds(2 * i + home, 1), :]
            other = pl.ds(r * blocks + half * (1 - high) + i, 1)
            idx[other, :] = pack[r * half + i:r * half + i + 1, :]
    src_t = tables[0]
    known_rows = [bucket_row(known, plan) for known in KNOWN + (None,)]

    def one_round(which, carry):
        row = known_rows[rounds - 1]
        for i in range(rounds - 1):
            row = jnp.where(which == i, known_rows[i], row)
        count = edge_count[row, dom]
        total = (count + (SPAN - 1)) // SPAN
        home = lax.rem(high + row, 2)

        def global_block(i):
            return (i // half) * (2 * blocks) + core * blocks + 2 * (i % half) + home

        used = jnp.int32(0)
        for i in range(blocks):
            used = used + (global_block(i) < total).astype(jnp.int32)
        dst_at = which + which // (rounds - 1)
        dst_t = tables[which + 1]
        dst_wide = dst_t.astype(F32)
        dst_rows = dst_wide.T.astype(BF16)

        def one_group(step, inner):
            first = step * GROUP
            at = row * blocks + first

            def take(a, n):
                return [idx[pl.ds(at + g, 1), a:a + n] for g in range(GROUP)]

            src_i = jnp.concatenate(take(0, SPAN), axis=1)
            dst_i = jnp.concatenate(take(SPAN, SPAN), axis=1)
            rel_i = jnp.concatenate(take(2 * SPAN, SPAN), axis=1)
            neg_i = take(3 * SPAN, n_neg)
            lane = lax.broadcasted_iota(jnp.int32, (1, SPAN), 1)
            live = jnp.concatenate(
                [
                    (global_block(first + g) * SPAN + lane < count).astype(F32)
                    for g in range(GROUP)
                ],
                axis=1,
            )
            src_hot = one_hot(src_i, part)
            dst_hot = one_hot(dst_i, part)
            w = jnp.zeros((width, span), F32)
            for a, n in rel_chunks(n_rel):
                chunk = one_hot(rel_i - a, n)
                hot[a:a + n, :] = chunk
                w = w + mm(rel[:, a:a + n], chunk)
            s = mm(src_t, src_hot)
            t = mm(dst_t, dst_hot)
            lhs = (s * w).astype(BF16)
            lhs_wide = lhs.astype(F32)
            positive = jnp.sum(lhs_wide * t, axis=0, keepdims=True)
            pos_weight = -live * jax.nn.sigmoid(-positive)
            scores = mm(dst_rows, lhs)
            weight = ((live * scale) * jax.nn.sigmoid(scores)).astype(BF16)
            from_neg = []
            dst_part = mm_nt((pos_weight * lhs_wide).astype(BF16), dst_hot)
            for g in range(GROUP):
                edges = slice(g * SPAN, (g + 1) * SPAN)
                low = one_hot(jnp.bitwise_and(neg_i[g], LANES - 1), LANES)
                far = one_hot(jnp.right_shift(neg_i[g], 7), 16)
                times = mm_nt(far, low)
                times = jnp.concatenate([times[q:q + 1, :] for q in range(n_rep)], axis=1)
                counted = times * dst_wide
                counted_hi = counted.astype(BF16)
                counted_lo = (counted - counted_hi.astype(F32)).astype(BF16)
                from_neg.append(
                    mm(counted_hi, weight[:, edges]) + mm(counted_lo, weight[:, edges])
                )
                grad_neg = mm_nt(lhs[:, edges], weight[:, edges]).astype(BF16).astype(F32)
                dst_part = dst_part + times * grad_neg
            grad_lhs = pos_weight * t + jnp.concatenate(from_neg, axis=1)
            grad_src = (grad_lhs * w).astype(BF16)
            grad_rel = (grad_lhs * s).astype(BF16)
            src_part = mm_nt(grad_src, src_hot)
            for q in range(n_rep):
                cols = slice(q * LANES, (q + 1) * LANES)
                acc[rounds - 1, q] += src_part[:, cols]
                acc[dst_at, q] += dst_part[:, cols]
            for a, n in rel_chunks(n_rel):
                term = mm_nt(grad_rel, hot[a:a + n, :])
                for b in range(n // LANES):
                    side, tile = place(a // LANES + b, half_tiles)
                    rel_acc[side, tile * width:(tile + 1) * width, :] += term[
                        :, b * LANES:(b + 1) * LANES
                    ]
            return inner

        lax.fori_loop(0, (used + (GROUP - 1)) // GROUP, one_group, 0)
        return carry

    lax.fori_loop(0, rounds, one_round, 0)
    rel_keep[...] = rel_acc[core]
    rel_send[...] = rel_acc[1 - core]
    for i in range(rounds + 1):
        for h, side in enumerate((high, 1 - high)):
            parts_keep[h, i] = acc[i, 2 * side + core]
            parts_send[h, i] = acc[i, 2 * side + 1 - core]


def run_rounds(plan, edge_count, where, quarters, rel, indices, pack):
    _, width, lanes = quarters[0].shape
    n_q = 4
    n_rel = rel.shape[1]
    rounds = plan.shape[0]
    half_tiles = -(-(n_rel // LANES) // 2)
    half_rows = -(-half_tiles * width // 2048) * 2048
    vmem = pl.BlockSpec(memory_space=pltpu.VMEM)
    smem = pl.BlockSpec(memory_space=pltpu.SMEM)
    parts = jax.ShapeDtypeStruct((2, rounds + 1, width, lanes), F32)
    side = jax.ShapeDtypeStruct((half_rows, LANES), F32)
    ops = [*quarters, rel, *indices, pack]
    return pl.pallas_call(
        functools.partial(rounds_kernel, half_tiles),
        out_shape=(parts, parts, side, side),
        in_specs=[smem] * 3 + [vmem] * len(ops),
        out_specs=(vmem,) * 4,
        scratch_shapes=[
            pltpu.VMEM((rounds + 1, n_q, width, lanes), F32),
            pltpu.VMEM((2, half_rows, LANES), F32),
            pltpu.VMEM((n_rel, GROUP * SPAN), BF16),
            pltpu.VMEM((2 * pack.shape[0], pack.shape[1]), jnp.int32),
            pltpu.VMEM((rounds + 1, width, n_q * lanes), BF16),
        ],
        compiler_params=pltpu.CompilerParams(vmem_limit_bytes=40 * 1024 * 1024),
        cost_estimate=pl.CostEstimate(flops=2 * 10 ** 10, bytes_accessed=10 ** 7, transcendentals=0),
        name="bucket_rounds",
    )(plan, edge_count, where, *ops)


def join_kernel(half_tiles, core, mine, other, out):
    width = out.shape[0]
    n_tiles = out.shape[1] // LANES

    def put(halves):
        for tile in range(n_tiles):
            half, at = place(tile, half_tiles)
            out[:, tile * LANES:(tile + 1) * LANES] = halves[half][at * width:(at + 1) * width, :]

    @pl.when(core[0] == 0)
    def _():
        put((mine, other))

    @pl.when(core[0] != 0)
    def _():
        put((other, mine))


def join_relations(core, mine, other, shape):
    half_tiles = -(-(shape[1] // LANES) // 2)
    vmem = pl.BlockSpec(memory_space=pltpu.VMEM)
    smem = pl.BlockSpec(memory_space=pltpu.SMEM)
    return pl.pallas_call(
        functools.partial(join_kernel, half_tiles),
        out_shape=jax.ShapeDtypeStruct(shape, F32),
        in_specs=[smem, vmem, vmem],
        out_specs=vmem,
        compiler_params=pltpu.CompilerParams(vmem_limit_bytes=24 * 1024 * 1024),
        name="join_relations",
    )(core, mine, other)


def shifted(value, axes, steps):
    count = 1
    for axis in axes:
        count *= lax.axis_size(axis)
    return lax.ppermute(value, axes, [(a, (a + steps) % count) for a in range(count)])


def crossed(value, axes, axis, steps):
    count = 1
    for name in axes:
        count *= lax.axis_size(name)
    pairs = [
        (2 * a + h, 2 * ((a + steps) % count) + 1 - h) for a in range(count) for h in range(2)
    ]
    return lax.ppermute(value, axes + (axis,), pairs)


def shifted_by(digit, unit, value):
    def move(d):
        return lambda v: shifted(v, DOM, unit * d) if d else v

    return lax.switch(digit, [move(d) for d in range(8)], value)


def both_by(digit, unit, value):
    def move(d):
        return lambda v: jnp.stack(
            [shifted(v, DOM, unit * d) if d else v, crossed(v, DOM, "xh", unit * d)]
        )

    return lax.switch(digit, [move(d) for d in range(8)], value)


def gathered_by(digit, unit, keep, send):
    def move(d):
        return lambda k, s: (shifted(k, DOM, unit * d) if d else k) + crossed(
            s, DOM, "xh", unit * d
        )

    return lax.switch(digit, [move(d) for d in range(8)], keep, send)


def swap(value, axis):
    return lax.ppermute(value, axis, [(0, 1), (1, 0)])


def together(*values):
    return lax.optimization_barrier(values)


def per_device(
    entity_table, relation_diag, plan, edge_count, src_rows, dst_rows, rel_ids, neg_rows
):
    rounds = plan.shape[0]
    core = lax.axis_index("core")
    where = jnp.stack([lax.axis_index(DOM), lax.axis_index("xh"), core]).astype(jnp.int32)
    indices = (src_rows, dst_rows, rel_ids, neg_rows)

    known = [shifted(entity_table, DOM, N_DOM - k) for k in KNOWN]
    pack, digits = pack_indices(plan, where, *indices)
    pack = swap(pack, "xh")
    free = shifted_by(digits[0], 1, entity_table)
    mine, free = together(jnp.stack([entity_table] + known), free)
    other = swap(mine, "xh")
    free = both_by(digits[1], 8, free)
    quarters = [mine, other, free] + [swap(v, "core") for v in (mine, other, free)]
    parts, parts_send, half, half_send = run_rounds(
        plan, edge_count, where, quarters, relation_diag, indices, pack
    )

    half = half + swap(half_send, "core")
    pieces = lax.all_to_all(half, CHIPS, 0, 0, tiled=True)
    parts = parts + swap(parts_send, "core")
    near = shifted(parts[0, 0], DOM, KNOWN[0]) + crossed(parts[1, 0], DOM, "xh", KNOWN[0])
    near = near + shifted(parts[0, 1], DOM, KNOWN[1])
    near = near + crossed(parts[1, 1], DOM, "xh", KNOWN[1])
    far = parts[0, 2:rounds] + swap(parts[1, 2:rounds], "xh")
    free = gathered_by(digits[2], 1, parts[0, rounds], parts[1, rounds])
    pieces, near, far, free = together(pieces, near, far, free)

    peers = 128
    piece = pieces.reshape(peers, -1, LANES).sum(axis=0)
    whole = lax.all_to_all(jnp.tile(piece, (peers, 1)), CHIPS, 0, 0, tiled=True)

    entity_grad = near + far[1] + shifted(far[0], DOM, KNOWN[2])
    entity_grad = entity_grad + shifted_by(digits[3], 8, free)
    whole, entity_grad = together(whole, entity_grad)
    relation_grad = join_relations(
        core.astype(jnp.int32).reshape(1), whole, swap(whole, "core"), relation_diag.shape
    )
    return entity_grad, relation_grad


def solution(mesh):
    fine = Mesh(mesh.devices.reshape(4, 8, 2, 2, 2), DOM + REP)
    cols = P(None, DOM + REP)
    in_specs = (cols, P(), P(), P(), cols, cols, cols, P(None, DOM + REP, None))
    return jax.shard_map(
        per_device, mesh=fine, in_specs=in_specs, out_specs=(cols, P()), check_vma=False
    )
```

```python
import functools

import jax
import jax.numpy as jnp
from jax import lax
from jax.experimental import pallas as pl
from jax.experimental.pallas import tpu as pltpu
from jax.sharding import Mesh, PartitionSpec as P

DOM = ("y", "z", "xl")
REP = ("xh", "core")
CHIPS = ("y", "z", "xl", "xh")
LANES = 128
SPAN = 256
KNOWN = (1, 32, 63)
N_DOM = 64
GROUP = 2
F32 = jnp.float32
BF16 = jnp.bfloat16


def mm(a, b):
    return jnp.dot(a, b, preferred_element_type=F32)


def mm_nt(a, b):
    return lax.dot_general(a, b, (((1,), (1,)), ((), ())), preferred_element_type=F32)


def one_hot(index, height):
    rows = lax.broadcasted_iota(jnp.int16, (height, index.shape[1]), 0)
    return jnp.where(rows == index.astype(jnp.int16), BF16(1.0), BF16(0.0))


def rel_chunks(n_rel):
    return [(a, min(2 * LANES, n_rel - a)) for a in range(0, n_rel, 2 * LANES)]


def place(tile, half_tiles):
    return (0, tile) if tile < half_tiles else (1, tile - half_tiles)


def bucket_row(known, plan):
    row = jnp.int32(0)
    for r in range(plan.shape[0]):
        if known is None:
            hit = plan[r] != KNOWN[0]
            for k in KNOWN[1:]:
                hit = jnp.logical_and(hit, plan[r] != k)
        else:
            hit = plan[r] == known
        row = jnp.where(hit, r, row)
    return row


def pack_kernel(plan, where, srcs, dsts, rels, negs, out, digits):
    rounds, blocks, _ = negs.shape
    half = blocks // 2
    offset = plan[0]
    for r in range(1, rounds):
        offset = offset + plan[r]
    offset = offset - sum(KNOWN)
    for i, steps in enumerate((N_DOM - offset, offset)):
        digits[2 * i] = lax.rem(steps, 8)
        digits[2 * i + 1] = lax.div(steps, jnp.int32(8))
    for r in range(rounds):
        away = lax.rem(where[1] + (r + 1), 2)
        for i in range(half):
            k = 2 * i + away
            at = r * half + i
            lanes = pl.ds(pl.multiple_of(k * SPAN, SPAN), SPAN)
            out[at:at + 1, 0:SPAN] = srcs[r:r + 1, lanes]
            out[at:at + 1, SPAN:2 * SPAN] = dsts[r:r + 1, lanes]
            out[at:at + 1, 2 * SPAN:3 * SPAN] = rels[r:r + 1, lanes]
            out[at:at + 1, 3 * SPAN:] = negs[r, pl.ds(k, 1), :]


def pack_indices(plan, where, srcs, dsts, rels, negs):
    rounds, blocks, n_neg = negs.shape
    vmem = pl.BlockSpec(memory_space=pltpu.VMEM)
    smem = pl.BlockSpec(memory_space=pltpu.SMEM)
    return pl.pallas_call(
        pack_kernel,
        out_shape=(
            jax.ShapeDtypeStruct((rounds * blocks // 2, 3 * SPAN + n_neg), jnp.int32),
            jax.ShapeDtypeStruct((4,), jnp.int32),
        ),
        in_specs=[smem] * 2 + [vmem] * 4,
        out_specs=(vmem, smem),
        name="pack_indices",
    )(plan, where, srcs, dsts, rels, negs)


def rounds_kernel(half_tiles, plan, edge_count, where, *refs):
    quarters, rel, srcs, dsts, rels, negs, pack = refs[:7]
    parts_keep, parts_send, rel_keep, rel_send = refs[7:11]
    acc, rel_acc, hot, idx, dst_buf = refs[11:]
    n_rep = quarters.shape[0]
    width, n_rel = rel.shape
    rounds, blocks, n_neg = negs.shape
    half = blocks // 2
    part = n_rep * LANES
    scale = n_neg ** -0.5
    span = GROUP * SPAN
    dom, high, core = where[0], where[1], where[2]

    acc[...] = jnp.zeros_like(acc)
    rel_acc[...] = jnp.zeros_like(rel_acc)
    for i in range(rounds):
        dst_buf[i] = jnp.concatenate([quarters[q, 1 + i] for q in range(n_rep)], axis=1)
    for r in range(rounds):
        home = lax.rem(high + r, 2)
        for i in range(half):
            lanes = pl.ds(pl.multiple_of((2 * i + home) * SPAN, SPAN), SPAN)
            mine = pl.ds(r * blocks + half * high + i, 1)
            idx[mine, 0:SPAN] = srcs[r:r + 1, lanes]
            idx[mine, SPAN:2 * SPAN] = dsts[r:r + 1, lanes]
            idx[mine, 2 * SPAN:3 * SPAN] = rels[r:r + 1, lanes]
            idx[mine, 3 * SPAN:] = negs[r, pl.ds(2 * i + home, 1), :]
            other = pl.ds(r * blocks + half * (1 - high) + i, 1)
            idx[other, :] = pack[r * half + i:r * half + i + 1, :]
    src_t = jnp.concatenate([quarters[q, 0] for q in range(n_rep)], axis=1)
    known_rows = [bucket_row(known, plan) for known in KNOWN + (None,)]

    def one_round(which, carry):
        row = known_rows[rounds - 1]
        for i in range(rounds - 1):
            row = jnp.where(which == i, known_rows[i], row)
        count = edge_count[row, dom]
        total = (count + (SPAN - 1)) // SPAN
        home = lax.rem(high + row, 2)

        def global_block(i):
            return (i // half) * (2 * blocks) + core * blocks + 2 * (i % half) + home

        used = jnp.int32(0)
        for i in range(blocks):
            used = used + (global_block(i) < total).astype(jnp.int32)
        dst_at = which + which // (rounds - 1)
        dst_t = dst_buf[which]
        dst_wide = dst_t.astype(F32)
        dst_rows = dst_wide.T.astype(BF16)

        def one_group(step, inner):
            first = step * GROUP
            at = row * blocks + first

            def take(a, n):
                return [idx[pl.ds(at + g, 1), a:a + n] for g in range(GROUP)]

            src_i = jnp.concatenate(take(0, SPAN), axis=1)
            dst_i = jnp.concatenate(take(SPAN, SPAN), axis=1)
            rel_i = jnp.concatenate(take(2 * SPAN, SPAN), axis=1)
            neg_i = take(3 * SPAN, n_neg)
            lane = lax.broadcasted_iota(jnp.int32, (1, SPAN), 1)
            live = jnp.concatenate(
                [
                    (global_block(first + g) * SPAN + lane < count).astype(F32)
                    for g in range(GROUP)
                ],
                axis=1,
            )
            src_hot = one_hot(src_i, part)
            dst_hot = one_hot(dst_i, part)
            w = jnp.zeros((width, span), F32)
            for a, n in rel_chunks(n_rel):
                chunk = one_hot(rel_i - a, n)
                hot[a:a + n, :] = chunk
                w = w + mm(rel[:, a:a + n], chunk)
            s = mm(src_t, src_hot)
            t = mm(dst_t, dst_hot)
            lhs = (s * w).astype(BF16)
            lhs_wide = lhs.astype(F32)
            positive = jnp.sum(lhs_wide * t, axis=0, keepdims=True)
            pos_weight = -live * jax.nn.sigmoid(-positive)
            scores = mm(dst_rows, lhs)
            weight = ((live * scale) * jax.nn.sigmoid(scores)).astype(BF16)
            from_neg = []
            dst_part = mm_nt((pos_weight * lhs_wide).astype(BF16), dst_hot)
            for g in range(GROUP):
                edges = slice(g * SPAN, (g + 1) * SPAN)
                low = one_hot(jnp.bitwise_and(neg_i[g], LANES - 1), LANES)
                far = one_hot(jnp.right_shift(neg_i[g], 7), 16)
                times = mm_nt(far, low)
                times = jnp.concatenate([times[q:q + 1, :] for q in range(n_rep)], axis=1)
                counted = times * dst_wide
                counted_hi = counted.astype(BF16)
                counted_lo = (counted - counted_hi.astype(F32)).astype(BF16)
                from_neg.append(
                    mm(counted_hi, weight[:, edges]) + mm(counted_lo, weight[:, edges])
                )
                grad_neg = mm_nt(lhs[:, edges], weight[:, edges]).astype(BF16).astype(F32)
                dst_part = dst_part + times * grad_neg
            grad_lhs = pos_weight * t + jnp.concatenate(from_neg, axis=1)
            grad_src = (grad_lhs * w).astype(BF16)
            grad_rel = (grad_lhs * s).astype(BF16)
            src_part = mm_nt(grad_src, src_hot)
            for q in range(n_rep):
                cols = slice(q * LANES, (q + 1) * LANES)
                acc[rounds - 1, q] += src_part[:, cols]
                acc[dst_at, q] += dst_part[:, cols]
            for a, n in rel_chunks(n_rel):
                term = mm_nt(grad_rel, hot[a:a + n, :])
                for b in range(n // LANES):
                    side, tile = place(a // LANES + b, half_tiles)
                    rel_acc[side, tile * width:(tile + 1) * width, :] += term[
                        :, b * LANES:(b + 1) * LANES
                    ]
            return inner

        lax.fori_loop(0, (used + (GROUP - 1)) // GROUP, one_group, 0)
        return carry

    lax.fori_loop(0, rounds, one_round, 0)
    rel_keep[...] = rel_acc[core]
    rel_send[...] = rel_acc[1 - core]
    for i in range(rounds + 1):
        for h, side in enumerate((high, 1 - high)):
            parts_keep[h, i] = acc[i, 2 * side + core]
            parts_send[h, i] = acc[i, 2 * side + 1 - core]


def run_rounds(plan, edge_count, where, quarters, rel, indices, pack):
    n_q, _, width, lanes = quarters.shape
    n_rel = rel.shape[1]
    rounds = plan.shape[0]
    half_tiles = -(-(n_rel // LANES) // 2)
    half_rows = -(-half_tiles * width // 2048) * 2048
    vmem = pl.BlockSpec(memory_space=pltpu.VMEM)
    smem = pl.BlockSpec(memory_space=pltpu.SMEM)
    parts = jax.ShapeDtypeStruct((2, rounds + 1, width, lanes), F32)
    side = jax.ShapeDtypeStruct((half_rows, LANES), F32)
    ops = [quarters, rel, *indices, pack]
    return pl.pallas_call(
        functools.partial(rounds_kernel, half_tiles),
        out_shape=(parts, parts, side, side),
        in_specs=[smem] * 3 + [vmem] * len(ops),
        out_specs=(vmem,) * 4,
        scratch_shapes=[
            pltpu.VMEM((rounds + 1, n_q, width, lanes), F32),
            pltpu.VMEM((2, half_rows, LANES), F32),
            pltpu.VMEM((n_rel, GROUP * SPAN), BF16),
            pltpu.VMEM((2 * pack.shape[0], pack.shape[1]), jnp.int32),
            pltpu.VMEM((rounds, width, n_q * lanes), BF16),
        ],
        compiler_params=pltpu.CompilerParams(vmem_limit_bytes=40 * 1024 * 1024),
        cost_estimate=pl.CostEstimate(flops=2 * 10 ** 10, bytes_accessed=10 ** 7, transcendentals=0),
        name="bucket_rounds",
    )(plan, edge_count, where, *ops)


def join_kernel(half_tiles, core, mine, other, out):
    width = out.shape[0]
    n_tiles = out.shape[1] // LANES

    def put(halves):
        for tile in range(n_tiles):
            half, at = place(tile, half_tiles)
            out[:, tile * LANES:(tile + 1) * LANES] = halves[half][at * width:(at + 1) * width, :]

    @pl.when(core[0] == 0)
    def _():
        put((mine, other))

    @pl.when(core[0] != 0)
    def _():
        put((other, mine))


def join_relations(core, mine, other, shape):
    half_tiles = -(-(shape[1] // LANES) // 2)
    vmem = pl.BlockSpec(memory_space=pltpu.VMEM)
    smem = pl.BlockSpec(memory_space=pltpu.SMEM)
    return pl.pallas_call(
        functools.partial(join_kernel, half_tiles),
        out_shape=jax.ShapeDtypeStruct(shape, F32),
        in_specs=[smem, vmem, vmem],
        out_specs=vmem,
        compiler_params=pltpu.CompilerParams(vmem_limit_bytes=24 * 1024 * 1024),
        name="join_relations",
    )(core, mine, other)


def shifted(value, axes, steps):
    count = 1
    for axis in axes:
        count *= lax.axis_size(axis)
    return lax.ppermute(value, axes, [(a, (a + steps) % count) for a in range(count)])


def crossed(value, axes, axis, steps):
    count = 1
    for name in axes:
        count *= lax.axis_size(name)
    pairs = [
        (2 * a + h, 2 * ((a + steps) % count) + 1 - h) for a in range(count) for h in range(2)
    ]
    return lax.ppermute(value, axes + (axis,), pairs)


def shifted_by(digit, unit, value):
    def move(d):
        return lambda v: shifted(v, DOM, unit * d) if d else v

    return lax.switch(digit, [move(d) for d in range(8)], value)


def gathered_by(digit, unit, keep, send):
    def move(d):
        return lambda k, s: (shifted(k, DOM, unit * d) if d else k) + crossed(
            s, DOM, "xh", unit * d
        )

    return lax.switch(digit, [move(d) for d in range(8)], keep, send)


def swap(value, axis):
    return lax.ppermute(value, axis, [(0, 1), (1, 0)])


def together(*values):
    return lax.optimization_barrier(values)


def per_device(
    entity_table, relation_diag, plan, edge_count, src_rows, dst_rows, rel_ids, neg_rows
):
    rounds = plan.shape[0]
    core = lax.axis_index("core")
    where = jnp.stack([lax.axis_index(DOM), lax.axis_index("xh"), core]).astype(jnp.int32)
    indices = (src_rows, dst_rows, rel_ids, neg_rows)

    known = [shifted(entity_table, DOM, N_DOM - k) for k in KNOWN]
    pack, digits = pack_indices(plan, where, *indices)
    pack = swap(pack, "xh")
    free = shifted_by(digits[0], 1, entity_table)
    free = shifted_by(digits[1], 8, free)
    quarters = jnp.stack([entity_table] + known + [free])
    quarters = lax.all_gather(quarters, REP, axis=0, tiled=False)
    parts, parts_send, half, half_send = run_rounds(
        plan, edge_count, where, quarters, relation_diag, indices, pack
    )

    half = half + swap(half_send, "core")
    pieces = lax.all_to_all(half.astype(BF16), CHIPS, 0, 0, tiled=True)
    parts = parts + swap(parts_send, "core")
    free = gathered_by(digits[2], 1, parts[0, rounds], parts[1, rounds])
    parts = parts[0, :rounds] + swap(parts[1, :rounds], "xh")
    pieces, parts, free = together(pieces, parts, free)

    peers = 128
    piece = pieces.reshape(peers, -1, LANES).astype(F32).sum(axis=0)
    whole = lax.all_to_all(jnp.tile(piece, (peers, 1)), CHIPS, 0, 0, tiled=True)

    entity_grad = parts[rounds - 1]
    for at, k in enumerate(KNOWN):
        entity_grad = entity_grad + shifted(parts[at], DOM, k)
    entity_grad = entity_grad + shifted_by(digits[3], 8, free)
    whole, entity_grad = together(whole, entity_grad)
    relation_grad = join_relations(
        core.astype(jnp.int32).reshape(1), whole, swap(whole, "core"), relation_diag.shape
    )
    return entity_grad, relation_grad


def solution(mesh):
    fine = Mesh(mesh.devices.reshape(4, 8, 2, 2, 2), DOM + REP)
    cols = P(None, DOM + REP)
    in_specs = (cols, P(), P(), P(), cols, cols, cols, P(None, DOM + REP, None))
    return jax.shard_map(
        per_device, mesh=fine, in_specs=in_specs, out_specs=(cols, P()), check_vma=False
    )
```

```python
import functools

import jax
import jax.numpy as jnp
from jax import lax
from jax.experimental import pallas as pl
from jax.experimental.pallas import tpu as pltpu
from jax.sharding import Mesh, PartitionSpec as P

DOM = ("y", "z", "xl")
REP = ("xh", "core")
CHIPS = ("y", "z", "xl", "xh")
LANES = 128
SPAN = 256
KNOWN = (1, 32, 63)
N_DOM = 64
GROUP = 2
F32 = jnp.float32
BF16 = jnp.bfloat16


def mm(a, b):
    return jnp.dot(a, b, preferred_element_type=F32)


def mm_nt(a, b):
    return lax.dot_general(a, b, (((1,), (1,)), ((), ())), preferred_element_type=F32)


def one_hot(index, height):
    rows = lax.broadcasted_iota(jnp.int16, (height, index.shape[1]), 0)
    return jnp.where(rows == index.astype(jnp.int16), BF16(1.0), BF16(0.0))


def rel_chunks(n_rel):
    return [(a, min(2 * LANES, n_rel - a)) for a in range(0, n_rel, 2 * LANES)]


def place(tile, half_tiles):
    return (0, tile) if tile < half_tiles else (1, tile - half_tiles)


def bucket_row(known, plan):
    row = jnp.int32(0)
    for r in range(plan.shape[0]):
        if known is None:
            hit = plan[r] != KNOWN[0]
            for k in KNOWN[1:]:
                hit = jnp.logical_and(hit, plan[r] != k)
        else:
            hit = plan[r] == known
        row = jnp.where(hit, r, row)
    return row


def pack_kernel(plan, where, srcs, dsts, rels, negs, out, digits):
    rounds, blocks, _ = negs.shape
    half = blocks // 2
    offset = plan[0]
    for r in range(1, rounds):
        offset = offset + plan[r]
    offset = offset - sum(KNOWN)
    for i, steps in enumerate((N_DOM - offset, offset)):
        digits[2 * i] = lax.rem(steps, 8)
        digits[2 * i + 1] = lax.div(steps, jnp.int32(8))
    for r in range(rounds):
        away = lax.rem(where[1] + (r + 1), 2)
        for i in range(half):
            k = 2 * i + away
            at = r * half + i
            lanes = pl.ds(pl.multiple_of(k * SPAN, SPAN), SPAN)
            out[at:at + 1, 0:SPAN] = srcs[r:r + 1, lanes]
            out[at:at + 1, SPAN:2 * SPAN] = dsts[r:r + 1, lanes]
            out[at:at + 1, 2 * SPAN:3 * SPAN] = rels[r:r + 1, lanes]
            out[at:at + 1, 3 * SPAN:] = negs[r, pl.ds(k, 1), :]


def pack_indices(plan, where, srcs, dsts, rels, negs):
    rounds, blocks, n_neg = negs.shape
    vmem = pl.BlockSpec(memory_space=pltpu.VMEM)
    smem = pl.BlockSpec(memory_space=pltpu.SMEM)
    return pl.pallas_call(
        pack_kernel,
        out_shape=(
            jax.ShapeDtypeStruct((rounds * blocks // 2, 3 * SPAN + n_neg), jnp.int32),
            jax.ShapeDtypeStruct((4,), jnp.int32),
        ),
        in_specs=[smem] * 2 + [vmem] * 4,
        out_specs=(vmem, smem),
        name="pack_indices",
    )(plan, where, srcs, dsts, rels, negs)


def rounds_kernel(half_tiles, plan, edge_count, where, *refs):
    quarters, rel, srcs, dsts, rels, negs, pack = refs[:7]
    parts_keep, parts_send, rel_keep, rel_send = refs[7:11]
    acc, rel_acc, hot, idx, dst_buf = refs[11:]
    n_rep = quarters.shape[0]
    width, n_rel = rel.shape
    rounds, blocks, n_neg = negs.shape
    half = blocks // 2
    part = n_rep * LANES
    scale = n_neg ** -0.5
    span = GROUP * SPAN
    dom, high, core = where[0], where[1], where[2]

    acc[...] = jnp.zeros_like(acc)
    rel_acc[...] = jnp.zeros_like(rel_acc)
    for i in range(rounds):
        dst_buf[i] = jnp.concatenate([quarters[q, 1 + i] for q in range(n_rep)], axis=1)
    for r in range(rounds):
        home = lax.rem(high + r, 2)
        for i in range(half):
            lanes = pl.ds(pl.multiple_of((2 * i + home) * SPAN, SPAN), SPAN)
            mine = pl.ds(r * blocks + half * high + i, 1)
            idx[mine, 0:SPAN] = srcs[r:r + 1, lanes]
            idx[mine, SPAN:2 * SPAN] = dsts[r:r + 1, lanes]
            idx[mine, 2 * SPAN:3 * SPAN] = rels[r:r + 1, lanes]
            idx[mine, 3 * SPAN:] = negs[r, pl.ds(2 * i + home, 1), :]
            other = pl.ds(r * blocks + half * (1 - high) + i, 1)
            idx[other, :] = pack[r * half + i:r * half + i + 1, :]
    src_t = jnp.concatenate([quarters[q, 0] for q in range(n_rep)], axis=1)
    known_rows = [bucket_row(known, plan) for known in KNOWN + (None,)]

    def one_round(which, carry):
        row = known_rows[rounds - 1]
        for i in range(rounds - 1):
            row = jnp.where(which == i, known_rows[i], row)
        count = edge_count[row, dom]
        total = (count + (SPAN - 1)) // SPAN
        home = lax.rem(high + row, 2)

        def global_block(i):
            return (i // half) * (2 * blocks) + core * blocks + 2 * (i % half) + home

        used = jnp.int32(0)
        for i in range(blocks):
            used = used + (global_block(i) < total).astype(jnp.int32)
        dst_at = which + which // (rounds - 1)
        dst_t = dst_buf[which]
        dst_wide = dst_t.astype(F32)
        dst_rows = dst_wide.T.astype(BF16)

        def one_group(step, inner):
            first = step * GROUP
            at = row * blocks + first

            def take(a, n):
                return [idx[pl.ds(at + g, 1), a:a + n] for g in range(GROUP)]

            src_i = jnp.concatenate(take(0, SPAN), axis=1)
            dst_i = jnp.concatenate(take(SPAN, SPAN), axis=1)
            rel_i = jnp.concatenate(take(2 * SPAN, SPAN), axis=1)
            neg_i = take(3 * SPAN, n_neg)
            lane = lax.broadcasted_iota(jnp.int32, (1, SPAN), 1)
            live = jnp.concatenate(
                [
                    (global_block(first + g) * SPAN + lane < count).astype(F32)
                    for g in range(GROUP)
                ],
                axis=1,
            )
            src_hot = one_hot(src_i, part)
            dst_hot = one_hot(dst_i, part)
            w = jnp.zeros((width, span), F32)
            for a, n in rel_chunks(n_rel):
                chunk = one_hot(rel_i - a, n)
                hot[a:a + n, :] = chunk
                w = w + mm(rel[:, a:a + n], chunk)
            s = mm(src_t, src_hot)
            t = mm(dst_t, dst_hot)
            lhs = (s * w).astype(BF16)
            lhs_wide = lhs.astype(F32)
            positive = jnp.sum(lhs_wide * t, axis=0, keepdims=True)
            pos_weight = -live * jax.nn.sigmoid(-positive)
            scores = mm(dst_rows, lhs)
            weight = ((live * scale) * jax.nn.sigmoid(scores)).astype(BF16)
            from_neg = []
            dst_part = mm_nt((pos_weight * lhs_wide).astype(BF16), dst_hot)
            for g in range(GROUP):
                edges = slice(g * SPAN, (g + 1) * SPAN)
                low = one_hot(jnp.bitwise_and(neg_i[g], LANES - 1), LANES)
                far = one_hot(jnp.right_shift(neg_i[g], 7), 16)
                times = mm_nt(far, low)
                times = jnp.concatenate([times[q:q + 1, :] for q in range(n_rep)], axis=1)
                counted = times * dst_wide
                counted_hi = counted.astype(BF16)
                counted_lo = (counted - counted_hi.astype(F32)).astype(BF16)
                from_neg.append(
                    mm(counted_hi, weight[:, edges]) + mm(counted_lo, weight[:, edges])
                )
                grad_neg = mm_nt(lhs[:, edges], weight[:, edges]).astype(BF16).astype(F32)
                dst_part = dst_part + times * grad_neg
            grad_lhs = pos_weight * t + jnp.concatenate(from_neg, axis=1)
            grad_src = (grad_lhs * w).astype(BF16)
            grad_rel = (grad_lhs * s).astype(BF16)
            src_part = mm_nt(grad_src, src_hot)
            for q in range(n_rep):
                cols = slice(q * LANES, (q + 1) * LANES)
                acc[rounds - 1, q] += src_part[:, cols]
                acc[dst_at, q] += dst_part[:, cols]
            for a, n in rel_chunks(n_rel):
                term = mm_nt(grad_rel, hot[a:a + n, :])
                for b in range(n // LANES):
                    side, tile = place(a // LANES + b, half_tiles)
                    rel_acc[side, tile * width:(tile + 1) * width, :] += term[
                        :, b * LANES:(b + 1) * LANES
                    ]
            return inner

        lax.fori_loop(0, (used + (GROUP - 1)) // GROUP, one_group, 0)
        return carry

    lax.fori_loop(0, rounds, one_round, 0)
    rel_keep[...] = rel_acc[core]
    rel_send[...] = rel_acc[1 - core]
    for i in range(rounds + 1):
        for h, side in enumerate((high, 1 - high)):
            parts_keep[h, i] = acc[i, 2 * side + core]
            parts_send[h, i] = acc[i, 2 * side + 1 - core]


def run_rounds(plan, edge_count, where, quarters, rel, indices, pack):
    n_q, _, width, lanes = quarters.shape
    n_rel = rel.shape[1]
    rounds = plan.shape[0]
    half_tiles = -(-(n_rel // LANES) // 2)
    half_rows = -(-half_tiles * width // 2048) * 2048
    vmem = pl.BlockSpec(memory_space=pltpu.VMEM)
    smem = pl.BlockSpec(memory_space=pltpu.SMEM)
    parts = jax.ShapeDtypeStruct((2, rounds + 1, width, lanes), F32)
    side = jax.ShapeDtypeStruct((half_rows, LANES), F32)
    ops = [quarters, rel, *indices, pack]
    return pl.pallas_call(
        functools.partial(rounds_kernel, half_tiles),
        out_shape=(parts, parts, side, side),
        in_specs=[smem] * 3 + [vmem] * len(ops),
        out_specs=(vmem,) * 4,
        scratch_shapes=[
            pltpu.VMEM((rounds + 1, n_q, width, lanes), F32),
            pltpu.VMEM((2, half_rows, LANES), F32),
            pltpu.VMEM((n_rel, GROUP * SPAN), BF16),
            pltpu.VMEM((2 * pack.shape[0], pack.shape[1]), jnp.int32),
            pltpu.VMEM((rounds, width, n_q * lanes), BF16),
        ],
        compiler_params=pltpu.CompilerParams(vmem_limit_bytes=40 * 1024 * 1024),
        cost_estimate=pl.CostEstimate(flops=2 * 10 ** 10, bytes_accessed=10 ** 7, transcendentals=0),
        name="bucket_rounds",
    )(plan, edge_count, where, *ops)


def join_kernel(half_tiles, core, mine, other, out):
    width = out.shape[0]
    n_tiles = out.shape[1] // LANES

    def put(halves):
        for tile in range(n_tiles):
            half, at = place(tile, half_tiles)
            out[:, tile * LANES:(tile + 1) * LANES] = halves[half][at * width:(at + 1) * width, :]

    @pl.when(core[0] == 0)
    def _():
        put((mine, other))

    @pl.when(core[0] != 0)
    def _():
        put((other, mine))


def join_relations(core, mine, other, shape):
    half_tiles = -(-(shape[1] // LANES) // 2)
    vmem = pl.BlockSpec(memory_space=pltpu.VMEM)
    smem = pl.BlockSpec(memory_space=pltpu.SMEM)
    return pl.pallas_call(
        functools.partial(join_kernel, half_tiles),
        out_shape=jax.ShapeDtypeStruct(shape, F32),
        in_specs=[smem, vmem, vmem],
        out_specs=vmem,
        compiler_params=pltpu.CompilerParams(vmem_limit_bytes=24 * 1024 * 1024),
        name="join_relations",
    )(core, mine, other)


def shifted(value, axes, steps):
    count = 1
    for axis in axes:
        count *= lax.axis_size(axis)
    return lax.ppermute(value, axes, [(a, (a + steps) % count) for a in range(count)])


def shifted_by(digit, unit, value):
    def move(d):
        return lambda v: shifted(v, DOM, unit * d) if d else v

    return lax.switch(digit, [move(d) for d in range(8)], value)


def swap(value, axis):
    return lax.ppermute(value, axis, [(0, 1), (1, 0)])


def together(*values):
    return lax.optimization_barrier(values)


def per_device(
    entity_table, relation_diag, plan, edge_count, src_rows, dst_rows, rel_ids, neg_rows
):
    rounds = plan.shape[0]
    core = lax.axis_index("core")
    where = jnp.stack([lax.axis_index(DOM), lax.axis_index("xh"), core]).astype(jnp.int32)
    indices = (src_rows, dst_rows, rel_ids, neg_rows)

    known = [shifted(entity_table, DOM, N_DOM - k) for k in KNOWN]
    pack, digits = pack_indices(plan, where, *indices)
    pack = swap(pack, "xh")
    free = shifted_by(digits[0], 1, entity_table)
    free = shifted_by(digits[1], 8, free)
    quarters = jnp.stack([entity_table] + known + [free])
    quarters = lax.all_gather(quarters, REP, axis=0, tiled=False)
    parts, parts_send, half, half_send = run_rounds(
        plan, edge_count, where, quarters, relation_diag, indices, pack
    )

    half_other = swap(half_send, "core")
    parts = parts + swap(parts_send, "core")
    half_other, parts = together(half_other, parts)
    parts_other = swap(parts[1], "xh")
    half = (half + half_other).astype(BF16)
    pieces = lax.all_to_all(half, CHIPS, 0, 0, tiled=True)
    parts = parts[0] + parts_other
    moved = [shifted(parts[at], DOM, k) for at, k in enumerate(KNOWN)]
    free = shifted_by(digits[2], 1, parts[rounds])
    pieces, free, *moved = together(pieces, free, *moved)

    peers = 128
    piece = pieces.reshape(peers, -1, LANES).astype(F32).sum(axis=0)
    whole = lax.all_to_all(jnp.tile(piece, (peers, 1)), CHIPS, 0, 0, tiled=True)

    free = shifted_by(digits[3], 8, free)
    entity_grad = sum(moved, parts[rounds - 1]) + free
    whole, entity_grad = together(whole, entity_grad)
    relation_grad = join_relations(
        core.astype(jnp.int32).reshape(1), whole, swap(whole, "core"), relation_diag.shape
    )
    return entity_grad, relation_grad


def solution(mesh):
    fine = Mesh(mesh.devices.reshape(4, 8, 2, 2, 2), DOM + REP)
    cols = P(None, DOM + REP)
    in_specs = (cols, P(), P(), P(), cols, cols, cols, P(None, DOM + REP, None))
    return jax.shard_map(
        per_device, mesh=fine, in_specs=in_specs, out_specs=(cols, P()), check_vma=False
    )
```

```python
import functools

import jax
import jax.numpy as jnp
from jax import lax
from jax.experimental import pallas as pl
from jax.experimental.pallas import tpu as pltpu
from jax.sharding import Mesh, PartitionSpec as P

DOM = ("y", "z", "xl")
REP = ("xh", "core")
CHIPS = ("y", "z", "xl", "xh")
LANES = 128
SPAN = 256
KNOWN = (1, 32, 63)
N_DOM = 64
GROUP = 2
F32 = jnp.float32
BF16 = jnp.bfloat16


def mm(a, b):
    return jnp.dot(a, b, preferred_element_type=F32)


def mm_nt(a, b):
    return lax.dot_general(a, b, (((1,), (1,)), ((), ())), preferred_element_type=F32)


def one_hot(index, height):
    rows = lax.broadcasted_iota(jnp.int16, (height, index.shape[1]), 0)
    return jnp.where(rows == index.astype(jnp.int16), BF16(1.0), BF16(0.0))


def rel_chunks(n_rel):
    return [(a, min(2 * LANES, n_rel - a)) for a in range(0, n_rel, 2 * LANES)]


def place(tile, half_tiles):
    return (0, tile) if tile < half_tiles else (1, tile - half_tiles)


def bucket_row(known, plan):
    row = jnp.int32(0)
    for r in range(plan.shape[0]):
        if known is None:
            hit = plan[r] != KNOWN[0]
            for k in KNOWN[1:]:
                hit = jnp.logical_and(hit, plan[r] != k)
        else:
            hit = plan[r] == known
        row = jnp.where(hit, r, row)
    return row


def pack_kernel(plan, where, srcs, dsts, rels, negs, out, digits):
    rounds, blocks, _ = negs.shape
    half = blocks // 2
    offset = plan[0]
    for r in range(1, rounds):
        offset = offset + plan[r]
    offset = offset - sum(KNOWN)
    for i, steps in enumerate((N_DOM - offset, offset)):
        digits[2 * i] = lax.rem(steps, 8)
        digits[2 * i + 1] = lax.div(steps, jnp.int32(8))
    for r in range(rounds):
        away = lax.rem(where[1] + (r + 1), 2)
        for i in range(half):
            k = 2 * i + away
            at = r * half + i
            lanes = pl.ds(pl.multiple_of(k * SPAN, SPAN), SPAN)
            out[at:at + 1, 0:SPAN] = srcs[r:r + 1, lanes]
            out[at:at + 1, SPAN:2 * SPAN] = dsts[r:r + 1, lanes]
            out[at:at + 1, 2 * SPAN:3 * SPAN] = rels[r:r + 1, lanes]
            out[at:at + 1, 3 * SPAN:] = negs[r, pl.ds(k, 1), :]


def pack_indices(plan, where, srcs, dsts, rels, negs):
    rounds, blocks, n_neg = negs.shape
    vmem = pl.BlockSpec(memory_space=pltpu.VMEM)
    smem = pl.BlockSpec(memory_space=pltpu.SMEM)
    return pl.pallas_call(
        pack_kernel,
        out_shape=(
            jax.ShapeDtypeStruct((rounds * blocks // 2, 3 * SPAN + n_neg), jnp.int32),
            jax.ShapeDtypeStruct((4,), jnp.int32),
        ),
        in_specs=[smem] * 2 + [vmem] * 4,
        out_specs=(vmem, smem),
        name="pack_indices",
    )(plan, where, srcs, dsts, rels, negs)


def rounds_kernel(half_tiles, plan, edge_count, where, *refs):
    quarters, rel, srcs, dsts, rels, negs, pack = refs[:7]
    parts_keep, parts_send, rel_keep, rel_send = refs[7:11]
    acc, rel_acc, hot, idx, dst_buf = refs[11:]
    n_rep = quarters.shape[0]
    width, n_rel = rel.shape
    rounds, blocks, n_neg = negs.shape
    half = blocks // 2
    part = n_rep * LANES
    scale = n_neg ** -0.5
    span = GROUP * SPAN
    dom, high, core = where[0], where[1], where[2]

    acc[...] = jnp.zeros_like(acc)
    rel_acc[...] = jnp.zeros_like(rel_acc)
    for i in range(rounds):
        dst_buf[i] = jnp.concatenate([quarters[q, 1 + i] for q in range(n_rep)], axis=1)
    for r in range(rounds):
        home = lax.rem(high + r, 2)
        for i in range(half):
            lanes = pl.ds(pl.multiple_of((2 * i + home) * SPAN, SPAN), SPAN)
            mine = pl.ds(r * blocks + half * high + i, 1)
            idx[mine, 0:SPAN] = srcs[r:r + 1, lanes]
            idx[mine, SPAN:2 * SPAN] = dsts[r:r + 1, lanes]
            idx[mine, 2 * SPAN:3 * SPAN] = rels[r:r + 1, lanes]
            idx[mine, 3 * SPAN:] = negs[r, pl.ds(2 * i + home, 1), :]
            other = pl.ds(r * blocks + half * (1 - high) + i, 1)
            idx[other, :] = pack[r * half + i:r * half + i + 1, :]
    src_t = jnp.concatenate([quarters[q, 0] for q in range(n_rep)], axis=1)
    known_rows = [bucket_row(known, plan) for known in KNOWN + (None,)]

    def one_round(which, carry):
        row = known_rows[rounds - 1]
        for i in range(rounds - 1):
            row = jnp.where(which == i, known_rows[i], row)
        count = edge_count[row, dom]
        total = (count + (SPAN - 1)) // SPAN
        home = lax.rem(high + row, 2)

        def global_block(i):
            return (i // half) * (2 * blocks) + core * blocks + 2 * (i % half) + home

        used = jnp.int32(0)
        for i in range(blocks):
            used = used + (global_block(i) < total).astype(jnp.int32)
        dst_at = which + which // (rounds - 1)
        dst_t = dst_buf[which]
        dst_wide = dst_t.astype(F32)
        dst_rows = dst_wide.T.astype(BF16)

        def one_group(step, inner):
            first = step * GROUP
            at = row * blocks + first

            def take(a, n):
                return [idx[pl.ds(at + g, 1), a:a + n] for g in range(GROUP)]

            src_i = jnp.concatenate(take(0, SPAN), axis=1)
            dst_i = jnp.concatenate(take(SPAN, SPAN), axis=1)
            rel_i = jnp.concatenate(take(2 * SPAN, SPAN), axis=1)
            neg_i = take(3 * SPAN, n_neg)
            lane = lax.broadcasted_iota(jnp.int32, (1, SPAN), 1)
            live = jnp.concatenate(
                [
                    (global_block(first + g) * SPAN + lane < count).astype(F32)
                    for g in range(GROUP)
                ],
                axis=1,
            )
            src_hot = one_hot(src_i, part)
            dst_hot = one_hot(dst_i, part)
            w = jnp.zeros((width, span), F32)
            for a, n in rel_chunks(n_rel):
                chunk = one_hot(rel_i - a, n)
                hot[a:a + n, :] = chunk
                w = w + mm(rel[:, a:a + n], chunk)
            s = mm(src_t, src_hot)
            t = mm(dst_t, dst_hot)
            lhs = (s * w).astype(BF16)
            lhs_wide = lhs.astype(F32)
            positive = jnp.sum(lhs_wide * t, axis=0, keepdims=True)
            pos_weight = -live * jax.nn.sigmoid(-positive)
            scores = mm(dst_rows, lhs)
            weight = ((live * scale) * jax.nn.sigmoid(scores)).astype(BF16)
            from_neg = []
            dst_part = mm_nt((pos_weight * lhs_wide).astype(BF16), dst_hot)
            for g in range(GROUP):
                edges = slice(g * SPAN, (g + 1) * SPAN)
                low = one_hot(jnp.bitwise_and(neg_i[g], LANES - 1), LANES)
                far = one_hot(jnp.right_shift(neg_i[g], 7), 16)
                times = mm_nt(far, low)
                times = jnp.concatenate([times[q:q + 1, :] for q in range(n_rep)], axis=1)
                counted = times * dst_wide
                counted_hi = counted.astype(BF16)
                counted_lo = (counted - counted_hi.astype(F32)).astype(BF16)
                from_neg.append(
                    mm(counted_hi, weight[:, edges]) + mm(counted_lo, weight[:, edges])
                )
                grad_neg = mm_nt(lhs[:, edges], weight[:, edges]).astype(BF16).astype(F32)
                dst_part = dst_part + times * grad_neg
            grad_lhs = pos_weight * t + jnp.concatenate(from_neg, axis=1)
            grad_src = (grad_lhs * w).astype(BF16)
            grad_rel = (grad_lhs * s).astype(BF16)
            src_part = mm_nt(grad_src, src_hot)
            for q in range(n_rep):
                cols = slice(q * LANES, (q + 1) * LANES)
                acc[rounds - 1, q] += src_part[:, cols]
                acc[dst_at, q] += dst_part[:, cols]
            for a, n in rel_chunks(n_rel):
                term = mm_nt(grad_rel, hot[a:a + n, :])
                for b in range(n // LANES):
                    side, tile = place(a // LANES + b, half_tiles)
                    rel_acc[side, tile * width:(tile + 1) * width, :] += term[
                        :, b * LANES:(b + 1) * LANES
                    ]
            return inner

        lax.fori_loop(0, (used + (GROUP - 1)) // GROUP, one_group, 0)
        return carry

    lax.fori_loop(0, rounds, one_round, 0)
    rel_keep[...] = rel_acc[core]
    rel_send[...] = rel_acc[1 - core]
    for i in range(rounds + 1):
        for h, side in enumerate((high, 1 - high)):
            parts_keep[h, i] = acc[i, 2 * side + core]
            parts_send[h, i] = acc[i, 2 * side + 1 - core]


def run_rounds(plan, edge_count, where, quarters, rel, indices, pack):
    n_q, _, width, lanes = quarters.shape
    n_rel = rel.shape[1]
    rounds = plan.shape[0]
    half_tiles = -(-(n_rel // LANES) // 2)
    half_rows = -(-half_tiles * width // 2048) * 2048
    vmem = pl.BlockSpec(memory_space=pltpu.VMEM)
    smem = pl.BlockSpec(memory_space=pltpu.SMEM)
    parts = jax.ShapeDtypeStruct((2, rounds + 1, width, lanes), F32)
    side = jax.ShapeDtypeStruct((half_rows, LANES), F32)
    ops = [quarters, rel, *indices, pack]
    return pl.pallas_call(
        functools.partial(rounds_kernel, half_tiles),
        out_shape=(parts, parts, side, side),
        in_specs=[smem] * 3 + [vmem] * len(ops),
        out_specs=(vmem,) * 4,
        scratch_shapes=[
            pltpu.VMEM((rounds + 1, n_q, width, lanes), F32),
            pltpu.VMEM((2, half_rows, LANES), F32),
            pltpu.VMEM((n_rel, GROUP * SPAN), BF16),
            pltpu.VMEM((2 * pack.shape[0], pack.shape[1]), jnp.int32),
            pltpu.VMEM((rounds, width, n_q * lanes), BF16),
        ],
        compiler_params=pltpu.CompilerParams(vmem_limit_bytes=40 * 1024 * 1024),
        cost_estimate=pl.CostEstimate(flops=2 * 10 ** 10, bytes_accessed=10 ** 7, transcendentals=0),
        name="bucket_rounds",
    )(plan, edge_count, where, *ops)


def join_kernel(half_tiles, core, mine, other, out):
    width = out.shape[0]
    n_tiles = out.shape[1] // LANES

    def put(halves):
        for tile in range(n_tiles):
            half, at = place(tile, half_tiles)
            out[:, tile * LANES:(tile + 1) * LANES] = halves[half][at * width:(at + 1) * width, :]

    @pl.when(core[0] == 0)
    def _():
        put((mine, other))

    @pl.when(core[0] != 0)
    def _():
        put((other, mine))


def join_relations(core, mine, other, shape):
    half_tiles = -(-(shape[1] // LANES) // 2)
    vmem = pl.BlockSpec(memory_space=pltpu.VMEM)
    smem = pl.BlockSpec(memory_space=pltpu.SMEM)
    return pl.pallas_call(
        functools.partial(join_kernel, half_tiles),
        out_shape=jax.ShapeDtypeStruct(shape, F32),
        in_specs=[smem, vmem, vmem],
        out_specs=vmem,
        compiler_params=pltpu.CompilerParams(vmem_limit_bytes=24 * 1024 * 1024),
        name="join_relations",
    )(core, mine, other)


def shifted(value, axes, steps):
    count = 1
    for axis in axes:
        count *= lax.axis_size(axis)
    return lax.ppermute(value, axes, [(a, (a + steps) % count) for a in range(count)])


def shifted_by(digit, unit, value):
    def move(d):
        return lambda v: shifted(v, DOM, unit * d) if d else v

    return lax.switch(digit, [move(d) for d in range(8)], value)


def swap(value, axis):
    return lax.ppermute(value, axis, [(0, 1), (1, 0)])


def together(*values):
    return lax.optimization_barrier(values)


def per_device(
    entity_table, relation_diag, plan, edge_count, src_rows, dst_rows, rel_ids, neg_rows
):
    rounds = plan.shape[0]
    core = lax.axis_index("core")
    where = jnp.stack([lax.axis_index(DOM), lax.axis_index("xh"), core]).astype(jnp.int32)
    indices = (src_rows, dst_rows, rel_ids, neg_rows)

    known = [shifted(entity_table, DOM, N_DOM - k) for k in KNOWN]
    pack, digits = pack_indices(plan, where, *indices)
    pack = swap(pack, "xh")
    free = shifted_by(digits[0], 1, entity_table)
    free = shifted_by(digits[1], 8, free)
    quarters = jnp.stack([entity_table] + known + [free])
    quarters = lax.all_gather(quarters, REP, axis=0, tiled=False)
    parts, parts_send, half, half_send = run_rounds(
        plan, edge_count, where, quarters, relation_diag, indices, pack
    )

    half_other = swap(half_send, "core")
    parts = parts + swap(parts_send, "core")
    half_other, parts = together(half_other, parts)
    parts_other = swap(parts[1], "xh")
    half = (half + half_other).astype(BF16)
    pieces = lax.all_to_all(half, CHIPS, 0, 0, tiled=True)
    parts = parts[0] + parts_other
    moved = [shifted(parts[at], DOM, k) for at, k in enumerate(KNOWN)]
    free = shifted_by(digits[2], 1, parts[rounds])
    peers = 128
    piece = pieces.reshape(peers, -1, LANES).astype(F32).sum(axis=0)
    free = shifted_by(digits[3], 8, free)
    entity_grad = sum(moved, parts[rounds - 1]) + free
    piece, entity_grad = together(piece, entity_grad)
    whole = lax.all_to_all(jnp.tile(piece, (peers, 1)), CHIPS, 0, 0, tiled=True)
    relation_grad = join_relations(
        core.astype(jnp.int32).reshape(1), whole, swap(whole, "core"), relation_diag.shape
    )
    return entity_grad, relation_grad


def solution(mesh):
    fine = Mesh(mesh.devices.reshape(4, 8, 2, 2, 2), DOM + REP)
    cols = P(None, DOM + REP)
    in_specs = (cols, P(), P(), P(), cols, cols, cols, P(None, DOM + REP, None))
    return jax.shard_map(
        per_device, mesh=fine, in_specs=in_specs, out_specs=(cols, P()), check_vma=False
    )
```

```python
import functools

import jax
import jax.numpy as jnp
from jax import lax
from jax.experimental import pallas as pl
from jax.experimental.pallas import tpu as pltpu
from jax.sharding import Mesh, PartitionSpec as P

DOM = ("y", "z", "xl")
REP = ("xh", "core")
CHIPS = ("y", "z", "xl", "xh")
LANES = 128
SPAN = 256
KNOWN = (1, 32, 63)
N_DOM = 64
GROUP = 2
PEERS = 128
CHUNK = 14
ROWS = 16
TURN = 4
F32 = jnp.float32
BF16 = jnp.bfloat16


def mm(a, b):
    return jnp.dot(a, b, preferred_element_type=F32)


def mm_nt(a, b):
    return lax.dot_general(a, b, (((1,), (1,)), ((), ())), preferred_element_type=F32)


def one_hot(index, height):
    rows = lax.broadcasted_iota(jnp.int16, (height, index.shape[1]), 0)
    return jnp.where(rows == index.astype(jnp.int16), BF16(1.0), BF16(0.0))


def rel_chunks(n_rel):
    return [(a, min(2 * LANES, n_rel - a)) for a in range(0, n_rel, 2 * LANES)]


def pieces_of(tile, n_tiles, width):
    mid = n_tiles // 2
    cut = -(-width // 16) * 8
    if tile < mid:
        return [(0, tile * width, 0, width)]
    if tile == mid:
        return [(0, mid * width, 0, cut), (1, 0, cut, width - cut)]
    return [(1, width - cut + (tile - mid - 1) * width, 0, width)]


def bucket_row(known, plan):
    row = jnp.int32(0)
    for r in range(plan.shape[0]):
        if known is None:
            hit = plan[r] != KNOWN[0]
            for k in KNOWN[1:]:
                hit = jnp.logical_and(hit, plan[r] != k)
        else:
            hit = plan[r] == known
        row = jnp.where(hit, r, row)
    return row


def pack_kernel(plan, where, srcs, dsts, rels, negs, out, digits):
    rounds, blocks, _ = negs.shape
    half = blocks // 2
    offset = plan[0]
    for r in range(1, rounds):
        offset = offset + plan[r]
    offset = offset - sum(KNOWN)
    steps = N_DOM - offset
    digits[0] = lax.rem(steps, 8)
    digits[1] = lax.div(steps, jnp.int32(8))
    for r in range(rounds):
        away = lax.rem(where[1] + (r + 1), 2)
        for i in range(half):
            k = 2 * i + away
            at = r * half + i
            lanes = pl.ds(pl.multiple_of(k * SPAN, SPAN), SPAN)
            out[at:at + 1, 0:SPAN] = srcs[r:r + 1, lanes]
            out[at:at + 1, SPAN:2 * SPAN] = dsts[r:r + 1, lanes]
            out[at:at + 1, 2 * SPAN:3 * SPAN] = rels[r:r + 1, lanes]
            out[at:at + 1, 3 * SPAN:] = negs[r, pl.ds(k, 1), :]


def pack_indices(plan, where, srcs, dsts, rels, negs):
    rounds, blocks, n_neg = negs.shape
    vmem = pl.BlockSpec(memory_space=pltpu.VMEM)
    smem = pl.BlockSpec(memory_space=pltpu.SMEM)
    return pl.pallas_call(
        pack_kernel,
        out_shape=(
            jax.ShapeDtypeStruct((rounds * blocks // 2, 3 * SPAN + n_neg), jnp.int32),
            jax.ShapeDtypeStruct((2,), jnp.int32),
        ),
        in_specs=[smem] * 2 + [vmem] * 4,
        out_specs=(vmem, smem),
        name="pack_indices",
    )(plan, where, srcs, dsts, rels, negs)


def rounds_kernel(plan, edge_count, where, *refs):
    quarters, rel, srcs, dsts, rels, negs, pack = refs[:7]
    parts_keep, parts_send, free_keep, free_send, rel_keep, rel_send = refs[7:13]
    acc, rel_acc, hot, idx, dst_buf = refs[13:]
    n_rep = quarters.shape[0]
    width, n_rel = rel.shape
    rounds, blocks, n_neg = negs.shape
    half = blocks // 2
    part = n_rep * LANES
    scale = n_neg ** -0.5
    span = GROUP * SPAN
    dom, high, core = where[0], where[1], where[2]

    acc[...] = jnp.zeros_like(acc)
    rel_acc[...] = jnp.zeros_like(rel_acc)
    for i in range(rounds):
        dst_buf[i] = jnp.concatenate([quarters[q, 1 + i] for q in range(n_rep)], axis=1)
    for r in range(rounds):
        home = lax.rem(high + r, 2)
        for i in range(half):
            lanes = pl.ds(pl.multiple_of((2 * i + home) * SPAN, SPAN), SPAN)
            mine = pl.ds(r * blocks + half * high + i, 1)
            idx[mine, 0:SPAN] = srcs[r:r + 1, lanes]
            idx[mine, SPAN:2 * SPAN] = dsts[r:r + 1, lanes]
            idx[mine, 2 * SPAN:3 * SPAN] = rels[r:r + 1, lanes]
            idx[mine, 3 * SPAN:] = negs[r, pl.ds(2 * i + home, 1), :]
            other = pl.ds(r * blocks + half * (1 - high) + i, 1)
            idx[other, :] = pack[r * half + i:r * half + i + 1, :]
    src_t = jnp.concatenate([quarters[q, 0] for q in range(n_rep)], axis=1)
    known_rows = [bucket_row(known, plan) for known in KNOWN + (None,)]

    def one_round(which, carry):
        row = known_rows[rounds - 1]
        for i in range(rounds - 1):
            row = jnp.where(which == i, known_rows[i], row)
        count = edge_count[row, dom]
        total = (count + (SPAN - 1)) // SPAN
        home = lax.rem(high + row, 2)

        def global_block(i):
            return (i // half) * (2 * blocks) + core * blocks + 2 * (i % half) + home

        used = jnp.int32(0)
        for i in range(blocks):
            used = used + (global_block(i) < total).astype(jnp.int32)
        dst_at = which + which // (rounds - 1)
        dst_t = dst_buf[which]
        dst_wide = dst_t.astype(F32)
        dst_rows = dst_wide.T.astype(BF16)

        def one_group(step, inner):
            first = step * GROUP
            at = row * blocks + first

            def take(a, n):
                return [idx[pl.ds(at + g, 1), a:a + n] for g in range(GROUP)]

            src_i = jnp.concatenate(take(0, SPAN), axis=1)
            dst_i = jnp.concatenate(take(SPAN, SPAN), axis=1)
            rel_i = jnp.concatenate(take(2 * SPAN, SPAN), axis=1)
            neg_i = take(3 * SPAN, n_neg)
            lane = lax.broadcasted_iota(jnp.int32, (1, SPAN), 1)
            live = jnp.concatenate(
                [
                    (global_block(first + g) * SPAN + lane < count).astype(F32)
                    for g in range(GROUP)
                ],
                axis=1,
            )
            src_hot = one_hot(src_i, part)
            dst_hot = one_hot(dst_i, part)
            w = jnp.zeros((width, span), F32)
            for a, n in rel_chunks(n_rel):
                chunk = one_hot(rel_i - a, n)
                hot[a:a + n, :] = chunk
                w = w + mm(rel[:, a:a + n], chunk)
            s = mm(src_t, src_hot)
            t = mm(dst_t, dst_hot)
            lhs = (s * w).astype(BF16)
            lhs_wide = lhs.astype(F32)
            positive = jnp.sum(lhs_wide * t, axis=0, keepdims=True)
            pos_weight = -live * jax.nn.sigmoid(-positive)
            scores = mm(dst_rows, lhs)
            weight = ((live * scale) * jax.nn.sigmoid(scores)).astype(BF16)
            from_neg = []
            dst_part = mm_nt((pos_weight * lhs_wide).astype(BF16), dst_hot)
            for g in range(GROUP):
                edges = slice(g * SPAN, (g + 1) * SPAN)
                low = one_hot(jnp.bitwise_and(neg_i[g], LANES - 1), LANES)
                far = one_hot(jnp.right_shift(neg_i[g], 7), 16)
                times = mm_nt(far, low)
                times = jnp.concatenate([times[q:q + 1, :] for q in range(n_rep)], axis=1)
                counted = times * dst_wide
                counted_hi = counted.astype(BF16)
                counted_lo = (counted - counted_hi.astype(F32)).astype(BF16)
                from_neg.append(
                    mm(counted_hi, weight[:, edges]) + mm(counted_lo, weight[:, edges])
                )
                grad_neg = mm_nt(lhs[:, edges], weight[:, edges]).astype(BF16).astype(F32)
                dst_part = dst_part + times * grad_neg
            grad_lhs = pos_weight * t + jnp.concatenate(from_neg, axis=1)
            grad_src = (grad_lhs * w).astype(BF16)
            grad_rel = (grad_lhs * s).astype(BF16)
            src_part = mm_nt(grad_src, src_hot)
            for q in range(n_rep):
                cols = slice(q * LANES, (q + 1) * LANES)
                acc[rounds - 1, q] += src_part[:, cols]
                acc[dst_at, q] += dst_part[:, cols]
            for a, n in rel_chunks(n_rel):
                term = mm_nt(grad_rel, hot[a:a + n, :])
                for b in range(n // LANES):
                    for side, to, at_row, n_rows in pieces_of(
                        a // LANES + b, n_rel // LANES, width
                    ):
                        rel_acc[side, to:to + n_rows, :] += term[
                            at_row:at_row + n_rows, b * LANES:(b + 1) * LANES
                        ]
            return inner

        lax.fori_loop(0, (used + (GROUP - 1)) // GROUP, one_group, 0)
        return carry

    lax.fori_loop(0, rounds, one_round, 0)
    rel_keep[...] = rel_acc[core]
    rel_send[...] = rel_acc[1 - core]
    for h, side in enumerate((high, 1 - high)):
        for i in range(rounds):
            parts_keep[h, i] = acc[i, 2 * side + core]
            parts_send[h, i] = acc[i, 2 * side + 1 - core]
        free_keep[h] = acc[rounds, 2 * side + core]
        free_send[h] = acc[rounds, 2 * side + 1 - core]


def run_rounds(plan, edge_count, where, quarters, rel, indices, pack):
    n_q, _, width, lanes = quarters.shape
    n_rel = rel.shape[1]
    rounds = plan.shape[0]
    half_rows = CHUNK * PEERS
    vmem = pl.BlockSpec(memory_space=pltpu.VMEM)
    smem = pl.BlockSpec(memory_space=pltpu.SMEM)
    parts = jax.ShapeDtypeStruct((2, rounds, width, lanes), F32)
    free = jax.ShapeDtypeStruct((2, width, lanes), F32)
    side = jax.ShapeDtypeStruct((half_rows, LANES), F32)
    ops = [quarters, rel, *indices, pack]
    return pl.pallas_call(
        rounds_kernel,
        out_shape=(parts, parts, free, free, side, side),
        in_specs=[smem] * 3 + [vmem] * len(ops),
        out_specs=(vmem,) * 6,
        scratch_shapes=[
            pltpu.VMEM((rounds + 1, n_q, width, lanes), F32),
            pltpu.VMEM((2, half_rows, LANES), F32),
            pltpu.VMEM((n_rel, GROUP * SPAN), BF16),
            pltpu.VMEM((2 * pack.shape[0], pack.shape[1]), jnp.int32),
            pltpu.VMEM((rounds, width, n_q * lanes), BF16),
        ],
        compiler_params=pltpu.CompilerParams(vmem_limit_bytes=40 * 1024 * 1024),
        cost_estimate=pl.CostEstimate(flops=2 * 10 ** 10, bytes_accessed=10 ** 7, transcendentals=0),
        name="bucket_rounds",
    )(plan, edge_count, where, *ops)


def load_kernel(keep, other, free_mine, free_other, out, free):
    width = free_mine.shape[0]
    free[0:width, :] = free_mine[...] + free_other[...]
    free[width:, :] = jnp.zeros_like(free[width:, :])

    def step(m, carry):
        rows = pl.ds(pl.multiple_of(m * TURN * CHUNK, 8), TURN * CHUNK)
        x = keep[rows, :] + other[rows, :]
        for q in range(TURN):
            k = m * TURN + q
            chunk = [x[q * CHUNK:(q + 1) * CHUNK, :]]
            chunk += [free[pl.ds(k + i * PEERS, 1), :] for i in range(ROWS - CHUNK)]
            out[k] = jnp.concatenate(chunk, axis=0).astype(BF16)
        return carry

    lax.fori_loop(0, PEERS // TURN, step, 0)


def load_chunks(keep, other, free_mine, free_other):
    vmem = pl.BlockSpec(memory_space=pltpu.VMEM)
    return pl.pallas_call(
        load_kernel,
        out_shape=jax.ShapeDtypeStruct((PEERS, ROWS, LANES), BF16),
        in_specs=[vmem] * 4,
        out_specs=vmem,
        scratch_shapes=[pltpu.VMEM(((ROWS - CHUNK) * PEERS, LANES), F32)],
        name="load_chunks",
    )(keep, other, free_mine, free_other)


def turn_kernel(plan, pieces, out):
    offset = plan[0]
    for r in range(1, plan.shape[0]):
        offset = offset + plan[r]
    back = 2 * (offset - sum(KNOWN))
    total = jnp.sum(pieces[...].astype(F32), axis=0)
    summed = lax.broadcasted_iota(jnp.int32, (ROWS, LANES), 0) < CHUNK

    def step(m, carry):
        for q in range(TURN):
            k = m * TURN + q
            origin = lax.rem(k + PEERS - back, PEERS)
            out[k] = jnp.where(summed, total, pieces[origin].astype(F32))
        return carry

    lax.fori_loop(0, PEERS // TURN, step, 0)


def turn_chunks(plan, pieces):
    vmem = pl.BlockSpec(memory_space=pltpu.VMEM)
    smem = pl.BlockSpec(memory_space=pltpu.SMEM)
    return pl.pallas_call(
        turn_kernel,
        out_shape=jax.ShapeDtypeStruct(pieces.shape, F32),
        in_specs=[smem, vmem],
        out_specs=vmem,
        name="turn_chunks",
    )(plan, pieces)


def join_kernel(core, mine, other, own, near0, near1, near2, rel_out, ent_out, lines, free):
    width = rel_out.shape[0]
    n_tiles = rel_out.shape[1] // LANES

    def step(m, carry):
        rows = pl.ds(pl.multiple_of(m * TURN * CHUNK, 8), TURN * CHUNK)
        for side, chunks in ((core[0], mine), (1 - core[0], other)):
            lines[side, rows, :] = jnp.concatenate(
                [chunks[m * TURN + q][0:CHUNK, :] for q in range(TURN)], axis=0
            )
        for q in range(TURN):
            k = m * TURN + q
            x = mine[k]
            for i in range(ROWS - CHUNK):
                free[pl.ds(k + i * PEERS, 1), :] = x[CHUNK + i:CHUNK + i + 1, :]
        return carry

    lax.fori_loop(0, PEERS // TURN, step, 0)
    for tile in range(n_tiles):
        cols = slice(tile * LANES, (tile + 1) * LANES)
        for side, at, to, n_rows in pieces_of(tile, n_tiles, width):
            rel_out[to:to + n_rows, cols] = lines[side, at:at + n_rows, :]
    ent_out[...] = (own[...] + near0[...]) + (near1[...] + near2[...]) + free[0:width, :]


def join_outputs(core, mine, other, own, near, rel_shape):
    vmem = pl.BlockSpec(memory_space=pltpu.VMEM)
    smem = pl.BlockSpec(memory_space=pltpu.SMEM)
    return pl.pallas_call(
        join_kernel,
        out_shape=(
            jax.ShapeDtypeStruct(rel_shape, F32),
            jax.ShapeDtypeStruct(own.shape, F32),
        ),
        in_specs=[smem] + [vmem] * 6,
        out_specs=(vmem, vmem),
        scratch_shapes=[
            pltpu.VMEM((2, CHUNK * PEERS, LANES), F32),
            pltpu.VMEM(((ROWS - CHUNK) * PEERS, LANES), F32),
        ],
        compiler_params=pltpu.CompilerParams(vmem_limit_bytes=24 * 1024 * 1024),
        name="join_outputs",
    )(core, mine, other, own, *near)


def shifted(value, axes, steps):
    count = 1
    for axis in axes:
        count *= lax.axis_size(axis)
    return lax.ppermute(value, axes, [(a, (a + steps) % count) for a in range(count)])


def shifted_by(digit, unit, value):
    def move(d):
        return lambda v: shifted(v, DOM, unit * d) if d else v

    return lax.switch(digit, [move(d) for d in range(8)], value)


def swap(value, axis):
    return lax.ppermute(value, axis, [(0, 1), (1, 0)])


def together(*values):
    return lax.optimization_barrier(values)


def per_device(
    entity_table, relation_diag, plan, edge_count, src_rows, dst_rows, rel_ids, neg_rows
):
    rounds = plan.shape[0]
    core = lax.axis_index("core")
    where = jnp.stack([lax.axis_index(DOM), lax.axis_index("xh"), core]).astype(jnp.int32)
    indices = (src_rows, dst_rows, rel_ids, neg_rows)

    known = [shifted(entity_table, DOM, N_DOM - k) for k in KNOWN]
    pack, digits = pack_indices(plan, where, *indices)
    pack = swap(pack, "xh")
    free = shifted_by(digits[0], 1, entity_table)
    free = shifted_by(digits[1], 8, free)
    quarters = jnp.stack([entity_table] + known + [free])
    quarters = lax.all_gather(quarters, REP, axis=0, tiled=False)
    parts, parts_send, free, free_send, half, half_send = run_rounds(
        plan, edge_count, where, quarters, relation_diag, indices, pack
    )

    half_other = swap(half_send, "core")
    free_send = swap(free_send, "core")
    free_mine = free[0] + free_send[0]
    free_other = swap(free[1] + free_send[1], "xh")
    parts = parts + swap(parts_send, "core")
    parts_other = swap(parts[1], "xh")
    pieces = lax.all_to_all(
        load_chunks(half, half_other, free_mine, free_other), CHIPS, 0, 0, tiled=True
    )
    parts = parts[0] + parts_other
    near = [shifted(parts[at], DOM, k) for at, k in enumerate(KNOWN)]
    pieces, own, *near = together(pieces, parts[rounds - 1], *near)
    whole = lax.all_to_all(turn_chunks(plan, pieces), CHIPS, 0, 0, tiled=True)
    relation_grad, entity_grad = join_outputs(
        core.astype(jnp.int32).reshape(1),
        whole,
        swap(whole, "core"),
        own,
        near,
        relation_diag.shape,
    )
    return entity_grad, relation_grad


def solution(mesh):
    fine = Mesh(mesh.devices.reshape(4, 8, 2, 2, 2), DOM + REP)
    cols = P(None, DOM + REP)
    in_specs = (cols, P(), P(), P(), cols, cols, cols, P(None, DOM + REP, None))
    return jax.shard_map(
        per_device, mesh=fine, in_specs=in_specs, out_specs=(cols, P()), check_vma=False
    )
```

```python
import functools

import jax
import jax.numpy as jnp
from jax import lax
from jax.experimental import pallas as pl
from jax.experimental.pallas import tpu as pltpu
from jax.sharding import Mesh, PartitionSpec as P

DOM = ("y", "z", "xl")
REP = ("xh", "core")
CHIPS = ("y", "z", "xl", "xh")
LANES = 128
SPAN = 256
KNOWN = (1, 32, 63)
N_DOM = 64
GROUP = 2
PEERS = 128
CHUNK = 14
ROWS = 16
TURN = 4
F32 = jnp.float32
BF16 = jnp.bfloat16


def mm(a, b):
    return jnp.dot(a, b, preferred_element_type=F32)


def mm_nt(a, b):
    return lax.dot_general(a, b, (((1,), (1,)), ((), ())), preferred_element_type=F32)


def one_hot(index, height):
    rows = lax.broadcasted_iota(jnp.int16, (height, index.shape[1]), 0)
    return jnp.where(rows == index.astype(jnp.int16), BF16(1.0), BF16(0.0))


def rel_chunks(n_rel):
    return [(a, min(2 * LANES, n_rel - a)) for a in range(0, n_rel, 2 * LANES)]


def pieces_of(tile, n_tiles, width):
    mid = n_tiles // 2
    cut = -(-width // 16) * 8
    if tile < mid:
        return [(0, tile * width, 0, width)]
    if tile == mid:
        return [(0, mid * width, 0, cut), (1, 0, cut, width - cut)]
    return [(1, width - cut + (tile - mid - 1) * width, 0, width)]


def bucket_row(known, plan):
    row = jnp.int32(0)
    for r in range(plan.shape[0]):
        if known is None:
            hit = plan[r] != KNOWN[0]
            for k in KNOWN[1:]:
                hit = jnp.logical_and(hit, plan[r] != k)
        else:
            hit = plan[r] == known
        row = jnp.where(hit, r, row)
    return row


def pack_kernel(plan, where, srcs, dsts, rels, negs, out, digits):
    rounds, blocks, _ = negs.shape
    half = blocks // 2
    offset = plan[0]
    for r in range(1, rounds):
        offset = offset + plan[r]
    offset = offset - sum(KNOWN)
    steps = N_DOM - offset
    digits[0] = lax.rem(steps, 8)
    digits[1] = lax.div(steps, jnp.int32(8))
    for r in range(rounds):
        away = lax.rem(where[1] + (r + 1), 2)
        for i in range(half):
            k = 2 * i + away
            at = r * half + i
            lanes = pl.ds(pl.multiple_of(k * SPAN, SPAN), SPAN)
            out[at:at + 1, 0:SPAN] = srcs[r:r + 1, lanes]
            out[at:at + 1, SPAN:2 * SPAN] = dsts[r:r + 1, lanes]
            out[at:at + 1, 2 * SPAN:3 * SPAN] = rels[r:r + 1, lanes]
            out[at:at + 1, 3 * SPAN:] = negs[r, pl.ds(k, 1), :]


def pack_indices(plan, where, srcs, dsts, rels, negs):
    rounds, blocks, n_neg = negs.shape
    vmem = pl.BlockSpec(memory_space=pltpu.VMEM)
    smem = pl.BlockSpec(memory_space=pltpu.SMEM)
    return pl.pallas_call(
        pack_kernel,
        out_shape=(
            jax.ShapeDtypeStruct((rounds * blocks // 2, 3 * SPAN + n_neg), jnp.int32),
            jax.ShapeDtypeStruct((2,), jnp.int32),
        ),
        in_specs=[smem] * 2 + [vmem] * 4,
        out_specs=(vmem, smem),
        name="pack_indices",
    )(plan, where, srcs, dsts, rels, negs)


def rounds_kernel(plan, edge_count, where, *refs):
    quarters, rel, srcs, dsts, rels, negs, pack = refs[:7]
    parts_keep, parts_send, free_keep, free_send, rel_keep, rel_send = refs[7:13]
    acc, rel_acc, hot, idx, dst_buf = refs[13:]
    n_rep = quarters.shape[0]
    width, n_rel = rel.shape
    rounds, blocks, n_neg = negs.shape
    half = blocks // 2
    part = n_rep * LANES
    scale = n_neg ** -0.5
    span = GROUP * SPAN
    dom, high, core = where[0], where[1], where[2]

    acc[...] = jnp.zeros_like(acc)
    rel_acc[...] = jnp.zeros_like(rel_acc)
    for i in range(rounds):
        dst_buf[i] = jnp.concatenate([quarters[q, 1 + i] for q in range(n_rep)], axis=1)
    for r in range(rounds):
        home = lax.rem(high + r, 2)
        for i in range(half):
            lanes = pl.ds(pl.multiple_of((2 * i + home) * SPAN, SPAN), SPAN)
            mine = pl.ds(r * blocks + half * high + i, 1)
            idx[mine, 0:SPAN] = srcs[r:r + 1, lanes]
            idx[mine, SPAN:2 * SPAN] = dsts[r:r + 1, lanes]
            idx[mine, 2 * SPAN:3 * SPAN] = rels[r:r + 1, lanes]
            idx[mine, 3 * SPAN:] = negs[r, pl.ds(2 * i + home, 1), :]
            other = pl.ds(r * blocks + half * (1 - high) + i, 1)
            idx[other, :] = pack[r * half + i:r * half + i + 1, :]
    src_t = jnp.concatenate([quarters[q, 0] for q in range(n_rep)], axis=1)
    known_rows = [bucket_row(known, plan) for known in KNOWN + (None,)]

    def one_round(which, carry):
        row = known_rows[rounds - 1]
        for i in range(rounds - 1):
            row = jnp.where(which == i, known_rows[i], row)
        count = edge_count[row, dom]
        total = (count + (SPAN - 1)) // SPAN
        home = lax.rem(high + row, 2)

        def global_block(i):
            return (i // half) * (2 * blocks) + core * blocks + 2 * (i % half) + home

        used = jnp.int32(0)
        for i in range(blocks):
            used = used + (global_block(i) < total).astype(jnp.int32)
        dst_at = which + which // (rounds - 1)
        dst_t = dst_buf[which]
        dst_wide = dst_t.astype(F32)
        dst_rows = dst_wide.T.astype(BF16)

        def one_group(step, inner):
            first = step * GROUP
            at = row * blocks + first

            def take(a, n):
                return [idx[pl.ds(at + g, 1), a:a + n] for g in range(GROUP)]

            src_i = jnp.concatenate(take(0, SPAN), axis=1)
            dst_i = jnp.concatenate(take(SPAN, SPAN), axis=1)
            rel_i = jnp.concatenate(take(2 * SPAN, SPAN), axis=1)
            neg_i = take(3 * SPAN, n_neg)
            lane = lax.broadcasted_iota(jnp.int32, (1, SPAN), 1)
            live = jnp.concatenate(
                [
                    (global_block(first + g) * SPAN + lane < count).astype(F32)
                    for g in range(GROUP)
                ],
                axis=1,
            )
            src_hot = one_hot(src_i, part)
            dst_hot = one_hot(dst_i, part)
            w = jnp.zeros((width, span), F32)
            for a, n in rel_chunks(n_rel):
                chunk = one_hot(rel_i - a, n)
                hot[a:a + n, :] = chunk
                w = w + mm(rel[:, a:a + n], chunk)
            s = mm(src_t, src_hot)
            t = mm(dst_t, dst_hot)
            lhs = (s * w).astype(BF16)
            lhs_wide = lhs.astype(F32)
            positive = jnp.sum(lhs_wide * t, axis=0, keepdims=True)
            pos_weight = -live * jax.nn.sigmoid(-positive)
            scores = mm(dst_rows, lhs)
            weight = ((live * scale) * jax.nn.sigmoid(scores)).astype(BF16)
            from_neg = []
            dst_part = mm_nt((pos_weight * lhs_wide).astype(BF16), dst_hot)
            for g in range(GROUP):
                edges = slice(g * SPAN, (g + 1) * SPAN)
                low = one_hot(jnp.bitwise_and(neg_i[g], LANES - 1), LANES)
                far = one_hot(jnp.right_shift(neg_i[g], 7), 16)
                times = mm_nt(far, low)
                times = jnp.concatenate([times[q:q + 1, :] for q in range(n_rep)], axis=1)
                counted = times * dst_wide
                counted_hi = counted.astype(BF16)
                counted_lo = (counted - counted_hi.astype(F32)).astype(BF16)
                from_neg.append(
                    mm(counted_hi, weight[:, edges]) + mm(counted_lo, weight[:, edges])
                )
                grad_neg = mm_nt(lhs[:, edges], weight[:, edges]).astype(BF16).astype(F32)
                dst_part = dst_part + times * grad_neg
            grad_lhs = pos_weight * t + jnp.concatenate(from_neg, axis=1)
            grad_src = (grad_lhs * w).astype(BF16)
            grad_rel = (grad_lhs * s).astype(BF16)
            src_part = mm_nt(grad_src, src_hot)
            for q in range(n_rep):
                cols = slice(q * LANES, (q + 1) * LANES)
                acc[rounds - 1, q] += src_part[:, cols]
                acc[dst_at, q] += dst_part[:, cols]
            for a, n in rel_chunks(n_rel):
                term = mm_nt(grad_rel, hot[a:a + n, :])
                for b in range(n // LANES):
                    for side, to, at_row, n_rows in pieces_of(
                        a // LANES + b, n_rel // LANES, width
                    ):
                        rel_acc[side, to:to + n_rows, :] += term[
                            at_row:at_row + n_rows, b * LANES:(b + 1) * LANES
                        ]
            return inner

        lax.fori_loop(0, (used + (GROUP - 1)) // GROUP, one_group, 0)
        return carry

    lax.fori_loop(0, rounds, one_round, 0)
    rel_keep[...] = rel_acc[core]
    rel_send[...] = rel_acc[1 - core]
    for h, side in enumerate((high, 1 - high)):
        for i in range(rounds):
            parts_keep[h, i] = acc[i, 2 * side + core]
            parts_send[h, i] = acc[i, 2 * side + 1 - core]
        free_keep[h] = acc[rounds, 2 * side + core]
        free_send[h] = acc[rounds, 2 * side + 1 - core]


def run_rounds(plan, edge_count, where, quarters, rel, indices, pack):
    n_q, _, width, lanes = quarters.shape
    n_rel = rel.shape[1]
    rounds = plan.shape[0]
    half_rows = CHUNK * PEERS
    vmem = pl.BlockSpec(memory_space=pltpu.VMEM)
    smem = pl.BlockSpec(memory_space=pltpu.SMEM)
    parts = jax.ShapeDtypeStruct((2, rounds, width, lanes), F32)
    free = jax.ShapeDtypeStruct((2, width, lanes), F32)
    side = jax.ShapeDtypeStruct((half_rows, LANES), F32)
    ops = [quarters, rel, *indices, pack]
    return pl.pallas_call(
        rounds_kernel,
        out_shape=(parts, parts, free, free, side, side),
        in_specs=[smem] * 3 + [vmem] * len(ops),
        out_specs=(vmem,) * 6,
        scratch_shapes=[
            pltpu.VMEM((rounds + 1, n_q, width, lanes), F32),
            pltpu.VMEM((2, half_rows, LANES), F32),
            pltpu.VMEM((n_rel, GROUP * SPAN), BF16),
            pltpu.VMEM((2 * pack.shape[0], pack.shape[1]), jnp.int32),
            pltpu.VMEM((rounds, width, n_q * lanes), BF16),
        ],
        compiler_params=pltpu.CompilerParams(vmem_limit_bytes=24 * 1024 * 1024),
        cost_estimate=pl.CostEstimate(flops=2 * 10 ** 10, bytes_accessed=10 ** 7, transcendentals=0),
        name="bucket_rounds",
    )(plan, edge_count, where, *ops)


def stack_kernel(*refs):
    out = refs[-1]
    for i, ref in enumerate(refs[:-1]):
        out[i] = ref[...]


def stacked(values):
    vmem = pl.BlockSpec(memory_space=pltpu.VMEM)
    return pl.pallas_call(
        stack_kernel,
        out_shape=jax.ShapeDtypeStruct((len(values),) + values[0].shape, values[0].dtype),
        in_specs=[vmem] * len(values),
        out_specs=vmem,
        compiler_params=pltpu.CompilerParams(vmem_limit_bytes=4 * 1024 * 1024),
        name="stack_quarters",
    )(*values)


def load_kernel(keep, other, free_mine, free_other, out, free):
    width = free_mine.shape[0]
    free[0:width, :] = free_mine[...] + free_other[...]
    free[width:, :] = jnp.zeros_like(free[width:, :])

    def step(m, carry):
        rows = pl.ds(pl.multiple_of(m * TURN * CHUNK, 8), TURN * CHUNK)
        x = keep[rows, :] + other[rows, :]
        for q in range(TURN):
            k = m * TURN + q
            chunk = [x[q * CHUNK:(q + 1) * CHUNK, :]]
            chunk += [free[pl.ds(k + i * PEERS, 1), :] for i in range(ROWS - CHUNK)]
            out[k] = jnp.concatenate(chunk, axis=0).astype(BF16)
        return carry

    lax.fori_loop(0, PEERS // TURN, step, 0, unroll=8)


def load_chunks(keep, other, free_mine, free_other):
    vmem = pl.BlockSpec(memory_space=pltpu.VMEM)
    return pl.pallas_call(
        load_kernel,
        out_shape=jax.ShapeDtypeStruct((PEERS, ROWS, LANES), BF16),
        in_specs=[vmem] * 4,
        out_specs=vmem,
        scratch_shapes=[pltpu.VMEM(((ROWS - CHUNK) * PEERS, LANES), F32)],
        compiler_params=pltpu.CompilerParams(vmem_limit_bytes=8 * 1024 * 1024),
        name="load_chunks",
    )(keep, other, free_mine, free_other)


def turn_kernel(plan, pieces, out):
    offset = plan[0]
    for r in range(1, plan.shape[0]):
        offset = offset + plan[r]
    back = 2 * (offset - sum(KNOWN))
    total = jnp.sum(pieces[...].astype(F32), axis=0)
    summed = lax.broadcasted_iota(jnp.int32, (ROWS - 8, LANES), 0) < CHUNK - 8

    def step(m, carry):
        for q in range(TURN):
            k = m * TURN + q
            origin = lax.rem(k + PEERS - back, PEERS)
            out[k, 0:8] = total[0:8]
            out[k, 8:ROWS] = jnp.where(summed, total[8:], pieces[origin].astype(F32)[8:])
        return carry

    lax.fori_loop(0, PEERS // TURN, step, 0, unroll=8)


def turn_chunks(plan, pieces):
    vmem = pl.BlockSpec(memory_space=pltpu.VMEM)
    smem = pl.BlockSpec(memory_space=pltpu.SMEM)
    return pl.pallas_call(
        turn_kernel,
        out_shape=jax.ShapeDtypeStruct(pieces.shape, F32),
        in_specs=[smem, vmem],
        out_specs=vmem,
        compiler_params=pltpu.CompilerParams(vmem_limit_bytes=8 * 1024 * 1024),
        name="turn_chunks",
    )(plan, pieces)


def join_kernel(core, mine, other, own, near0, near1, near2, rel_out, ent_out, lines, free):
    width = rel_out.shape[0]
    n_tiles = rel_out.shape[1] // LANES

    def step(m, carry):
        rows = pl.ds(pl.multiple_of(m * TURN * CHUNK, 8), TURN * CHUNK)
        for side, chunks in ((core[0], mine), (1 - core[0], other)):
            lines[side, rows, :] = jnp.concatenate(
                [chunks[m * TURN + q][0:CHUNK, :] for q in range(TURN)], axis=0
            )
        for q in range(TURN):
            k = m * TURN + q
            x = mine[k]
            for i in range(ROWS - CHUNK):
                free[pl.ds(k + i * PEERS, 1), :] = x[CHUNK + i:CHUNK + i + 1, :]
        return carry

    lax.fori_loop(0, PEERS // TURN, step, 0, unroll=8)
    for tile in range(n_tiles):
        cols = slice(tile * LANES, (tile + 1) * LANES)
        for side, at, to, n_rows in pieces_of(tile, n_tiles, width):
            rel_out[to:to + n_rows, cols] = lines[side, at:at + n_rows, :]
    ent_out[...] = (own[...] + near0[...]) + (near1[...] + near2[...]) + free[0:width, :]


def join_outputs(core, mine, other, own, near, rel_shape):
    vmem = pl.BlockSpec(memory_space=pltpu.VMEM)
    smem = pl.BlockSpec(memory_space=pltpu.SMEM)
    return pl.pallas_call(
        join_kernel,
        out_shape=(
            jax.ShapeDtypeStruct(rel_shape, F32),
            jax.ShapeDtypeStruct(own.shape, F32),
        ),
        in_specs=[smem] + [vmem] * 6,
        out_specs=(vmem, vmem),
        scratch_shapes=[
            pltpu.VMEM((2, CHUNK * PEERS, LANES), F32),
            pltpu.VMEM(((ROWS - CHUNK) * PEERS, LANES), F32),
        ],
        compiler_params=pltpu.CompilerParams(vmem_limit_bytes=12 * 1024 * 1024),
        name="join_outputs",
    )(core, mine, other, own, *near)


def shifted(value, axes, steps):
    count = 1
    for axis in axes:
        count *= lax.axis_size(axis)
    return lax.ppermute(value, axes, [(a, (a + steps) % count) for a in range(count)])


def shifted_by(digit, unit, value):
    def move(d):
        return lambda v: shifted(v, DOM, unit * d) if d else v

    return lax.switch(digit, [move(d) for d in range(8)], value)


def swap(value, axis):
    return lax.ppermute(value, axis, [(0, 1), (1, 0)])


def together(*values):
    return lax.optimization_barrier(values)


def per_device(
    entity_table, relation_diag, plan, edge_count, src_rows, dst_rows, rel_ids, neg_rows
):
    rounds = plan.shape[0]
    core = lax.axis_index("core")
    where = jnp.stack([lax.axis_index(DOM), lax.axis_index("xh"), core]).astype(jnp.int32)
    indices = (src_rows, dst_rows, rel_ids, neg_rows)

    known = [shifted(entity_table, DOM, N_DOM - k) for k in KNOWN]
    pack, digits = pack_indices(plan, where, *indices)
    pack = swap(pack, "xh")
    free = shifted_by(digits[0], 1, entity_table)
    free = shifted_by(digits[1], 8, free)
    quarters = stacked([entity_table] + known + [free])
    quarters = lax.all_gather(quarters, REP, axis=0, tiled=False)
    parts, parts_send, free, free_send, half, half_send = run_rounds(
        plan, edge_count, where, quarters, relation_diag, indices, pack
    )

    half_other = swap(half_send, "core")
    free_send = swap(free_send, "core")
    parts_send = swap(parts_send, "core")
    free_mine = free[0] + free_send[0]
    free_other = swap(free[1] + free_send[1], "xh")
    parts_mine = parts[0] + parts_send[0]
    parts_other = swap((parts[1] + parts_send[1]).astype(BF16), "xh")
    pieces = lax.all_to_all(
        load_chunks(half, half_other, free_mine, free_other), CHIPS, 0, 0, tiled=True
    )
    parts = parts_mine + parts_other.astype(F32)
    pieces, parts = together(pieces, parts)
    near = [shifted(parts[at], DOM, k) for at, k in enumerate(KNOWN)]
    whole = lax.all_to_all(turn_chunks(plan, pieces), CHIPS, 0, 0, tiled=True)
    whole, *near = together(whole, *near)
    relation_grad, entity_grad = join_outputs(
        core.astype(jnp.int32).reshape(1),
        whole,
        swap(whole, "core"),
        parts[rounds - 1],
        near,
        relation_diag.shape,
    )
    return entity_grad, relation_grad


def solution(mesh):
    fine = Mesh(mesh.devices.reshape(4, 8, 2, 2, 2), DOM + REP)
    cols = P(None, DOM + REP)
    in_specs = (cols, P(), P(), P(), cols, cols, cols, P(None, DOM + REP, None))
    return jax.shard_map(
        per_device, mesh=fine, in_specs=in_specs, out_specs=(cols, P()), check_vma=False
    )
```

```python
import functools

import jax
import jax.numpy as jnp
from jax import lax
from jax.experimental import pallas as pl
from jax.experimental.pallas import tpu as pltpu
from jax.sharding import Mesh, PartitionSpec as P

DOM = ("y", "z", "xl")
REP = ("xh", "core")
CHIPS = ("y", "z", "xl", "xh")
LANES = 128
SPAN = 256
KNOWN = (1, 32, 63)
N_DOM = 64
GROUP = 2
PEERS = 128
CHUNK = 14
ROWS = 16
TURN = 4
F32 = jnp.float32
BF16 = jnp.bfloat16


def mm(a, b):
    return jnp.dot(a, b, preferred_element_type=F32)


def mm_nt(a, b):
    return lax.dot_general(a, b, (((1,), (1,)), ((), ())), preferred_element_type=F32)


def one_hot(index, height):
    rows = lax.broadcasted_iota(jnp.int16, (height, index.shape[1]), 0)
    return jnp.where(rows == index.astype(jnp.int16), BF16(1.0), BF16(0.0))


def one_hot_t(column, width):
    cols = lax.broadcasted_iota(jnp.int16, (column.shape[0], width), 1)
    return jnp.where(cols == column.astype(jnp.int16), BF16(1.0), BF16(0.0))


def column_of(index):
    return jnp.transpose(jnp.broadcast_to(index, (8, index.shape[1])))[:, 0:1]


def rel_chunks(n_rel):
    return [(a, min(2 * LANES, n_rel - a)) for a in range(0, n_rel, 2 * LANES)]


def pieces_of(tile, n_tiles, width):
    mid = n_tiles // 2
    cut = -(-width // 16) * 8
    if tile < mid:
        return [(0, tile * width, 0, width)]
    if tile == mid:
        return [(0, mid * width, 0, cut), (1, 0, cut, width - cut)]
    return [(1, width - cut + (tile - mid - 1) * width, 0, width)]


def bucket_row(known, plan):
    row = jnp.int32(0)
    for r in range(plan.shape[0]):
        if known is None:
            hit = plan[r] != KNOWN[0]
            for k in KNOWN[1:]:
                hit = jnp.logical_and(hit, plan[r] != k)
        else:
            hit = plan[r] == known
        row = jnp.where(hit, r, row)
    return row


def pack_kernel(plan, where, srcs, dsts, rels, negs, out, digits):
    rounds, blocks, _ = negs.shape
    half = blocks // 2
    offset = plan[0]
    for r in range(1, rounds):
        offset = offset + plan[r]
    offset = offset - sum(KNOWN)
    steps = N_DOM - offset
    digits[0] = lax.rem(steps, 8)
    digits[1] = lax.div(steps, jnp.int32(8))
    for r in range(rounds):
        away = lax.rem(where[1] + (r + 1), 2)
        for i in range(half):
            k = 2 * i + away
            at = r * half + i
            lanes = pl.ds(pl.multiple_of(k * SPAN, SPAN), SPAN)
            out[at:at + 1, 0:SPAN] = srcs[r:r + 1, lanes]
            out[at:at + 1, SPAN:2 * SPAN] = dsts[r:r + 1, lanes]
            out[at:at + 1, 2 * SPAN:3 * SPAN] = rels[r:r + 1, lanes]
            out[at:at + 1, 3 * SPAN:] = negs[r, pl.ds(k, 1), :]


def pack_indices(plan, where, srcs, dsts, rels, negs):
    rounds, blocks, n_neg = negs.shape
    vmem = pl.BlockSpec(memory_space=pltpu.VMEM)
    smem = pl.BlockSpec(memory_space=pltpu.SMEM)
    return pl.pallas_call(
        pack_kernel,
        out_shape=(
            jax.ShapeDtypeStruct((rounds * blocks // 2, 3 * SPAN + n_neg), jnp.int32),
            jax.ShapeDtypeStruct((2,), jnp.int32),
        ),
        in_specs=[smem] * 2 + [vmem] * 4,
        out_specs=(vmem, smem),
        name="pack_indices",
    )(plan, where, srcs, dsts, rels, negs)


def rounds_kernel(plan, edge_count, where, *refs):
    quarters, rel, srcs, dsts, rels, negs, pack = refs[:7]
    parts_keep, parts_send, free_keep, free_send, rel_keep, rel_send = refs[7:13]
    acc, rel_acc, idx, dst_buf = refs[13:]
    n_rep = quarters.shape[0]
    width, n_rel = rel.shape
    rounds, blocks, n_neg = negs.shape
    half = blocks // 2
    part = n_rep * LANES
    scale = n_neg ** -0.5
    span = GROUP * SPAN
    dom, high, core = where[0], where[1], where[2]

    acc[...] = jnp.zeros_like(acc)
    rel_acc[...] = jnp.zeros_like(rel_acc)
    for i in range(rounds):
        dst_buf[i] = jnp.concatenate([quarters[q, 1 + i] for q in range(n_rep)], axis=1)
    for r in range(rounds):
        home = lax.rem(high + r, 2)
        for i in range(half):
            lanes = pl.ds(pl.multiple_of((2 * i + home) * SPAN, SPAN), SPAN)
            mine = pl.ds(r * blocks + half * high + i, 1)
            idx[mine, 0:SPAN] = srcs[r:r + 1, lanes]
            idx[mine, SPAN:2 * SPAN] = dsts[r:r + 1, lanes]
            idx[mine, 2 * SPAN:3 * SPAN] = rels[r:r + 1, lanes]
            idx[mine, 3 * SPAN:] = negs[r, pl.ds(2 * i + home, 1), :]
            other = pl.ds(r * blocks + half * (1 - high) + i, 1)
            idx[other, :] = pack[r * half + i:r * half + i + 1, :]
    src_t = jnp.concatenate([quarters[q, 0] for q in range(n_rep)], axis=1)
    known_rows = [bucket_row(known, plan) for known in KNOWN + (None,)]

    def one_round(which, carry):
        row = known_rows[rounds - 1]
        for i in range(rounds - 1):
            row = jnp.where(which == i, known_rows[i], row)
        count = edge_count[row, dom]
        total = (count + (SPAN - 1)) // SPAN
        home = lax.rem(high + row, 2)

        def global_block(i):
            return (i // half) * (2 * blocks) + core * blocks + 2 * (i % half) + home

        used = jnp.int32(0)
        for i in range(blocks):
            used = used + (global_block(i) < total).astype(jnp.int32)
        dst_at = which + which // (rounds - 1)
        dst_t = dst_buf[which]
        dst_wide = dst_t.astype(F32)
        dst_rows = dst_wide.T.astype(BF16)

        def one_group(step, inner):
            first = step * GROUP
            at = row * blocks + first

            def take(a, n):
                return [idx[pl.ds(at + g, 1), a:a + n] for g in range(GROUP)]

            src_i = jnp.concatenate(take(0, SPAN), axis=1)
            dst_i = jnp.concatenate(take(SPAN, SPAN), axis=1)
            rel_i = jnp.concatenate(take(2 * SPAN, SPAN), axis=1)
            neg_i = take(3 * SPAN, n_neg)
            lane = lax.broadcasted_iota(jnp.int32, (1, SPAN), 1)
            live = jnp.concatenate(
                [
                    (global_block(first + g) * SPAN + lane < count).astype(F32)
                    for g in range(GROUP)
                ],
                axis=1,
            )
            rel_c = column_of(rel_i)
            w = jnp.zeros((width, span), F32)
            for a, n in rel_chunks(n_rel):
                w = w + mm(rel[:, a:a + n], one_hot(rel_i - a, n))
            s = mm(src_t, one_hot(src_i, part))
            t = mm(dst_t, one_hot(dst_i, part))
            lhs = (s * w).astype(BF16)
            lhs_wide = lhs.astype(F32)
            positive = jnp.sum(lhs_wide * t, axis=0, keepdims=True)
            pos_weight = -live * jax.nn.sigmoid(-positive)
            scores = mm(dst_rows, lhs)
            weight = ((live * scale) * jax.nn.sigmoid(scores)).astype(BF16)
            from_neg = []
            grad_dst = (pos_weight * lhs_wide).astype(BF16)
            dst_part = mm(grad_dst, one_hot_t(column_of(dst_i), part))
            for g in range(GROUP):
                edges = slice(g * SPAN, (g + 1) * SPAN)
                low = one_hot(jnp.bitwise_and(neg_i[g], LANES - 1), LANES)
                far = one_hot(jnp.right_shift(neg_i[g], 7), 16)
                times = mm_nt(far, low)
                times = jnp.concatenate([times[q:q + 1, :] for q in range(n_rep)], axis=1)
                counted = times * dst_wide
                counted_hi = counted.astype(BF16)
                counted_lo = (counted - counted_hi.astype(F32)).astype(BF16)
                from_neg.append(
                    mm(counted_hi, weight[:, edges]) + mm(counted_lo, weight[:, edges])
                )
                grad_neg = mm_nt(lhs[:, edges], weight[:, edges]).astype(BF16).astype(F32)
                dst_part = dst_part + times * grad_neg
            grad_lhs = pos_weight * t + jnp.concatenate(from_neg, axis=1)
            grad_src = (grad_lhs * w).astype(BF16)
            grad_rel = (grad_lhs * s).astype(BF16)
            src_part = mm(grad_src, one_hot_t(column_of(src_i), part))
            for q in range(n_rep):
                cols = slice(q * LANES, (q + 1) * LANES)
                acc[rounds - 1, q] += src_part[:, cols]
                acc[dst_at, q] += dst_part[:, cols]
            for a, n in rel_chunks(n_rel):
                term = mm(grad_rel, one_hot_t(rel_c - a, n))
                for b in range(n // LANES):
                    for side, to, at_row, n_rows in pieces_of(
                        a // LANES + b, n_rel // LANES, width
                    ):
                        rel_acc[side, to:to + n_rows, :] += term[
                            at_row:at_row + n_rows, b * LANES:(b + 1) * LANES
                        ]
            return inner

        lax.fori_loop(0, (used + (GROUP - 1)) // GROUP, one_group, 0)
        return carry

    lax.fori_loop(0, rounds, one_round, 0)
    rel_keep[...] = rel_acc[core]
    rel_send[...] = rel_acc[1 - core]
    for h, side in enumerate((high, 1 - high)):
        for i in range(rounds):
            parts_keep[h, i] = acc[i, 2 * side + core]
            parts_send[h, i] = acc[i, 2 * side + 1 - core]
        free_keep[h] = acc[rounds, 2 * side + core]
        free_send[h] = acc[rounds, 2 * side + 1 - core]


def run_rounds(plan, edge_count, where, quarters, rel, indices, pack):
    n_q, _, width, lanes = quarters.shape
    n_rel = rel.shape[1]
    rounds = plan.shape[0]
    half_rows = CHUNK * PEERS
    vmem = pl.BlockSpec(memory_space=pltpu.VMEM)
    smem = pl.BlockSpec(memory_space=pltpu.SMEM)
    parts = jax.ShapeDtypeStruct((2, rounds, width, lanes), F32)
    free = jax.ShapeDtypeStruct((2, width, lanes), F32)
    side = jax.ShapeDtypeStruct((half_rows, LANES), F32)
    ops = [quarters, rel, *indices, pack]
    return pl.pallas_call(
        rounds_kernel,
        out_shape=(parts, parts, free, free, side, side),
        in_specs=[smem] * 3 + [vmem] * len(ops),
        out_specs=(vmem,) * 6,
        scratch_shapes=[
            pltpu.VMEM((rounds + 1, n_q, width, lanes), F32),
            pltpu.VMEM((2, half_rows, LANES), F32),
            pltpu.VMEM((2 * pack.shape[0], pack.shape[1]), jnp.int32),
            pltpu.VMEM((rounds, width, n_q * lanes), BF16),
        ],
        compiler_params=pltpu.CompilerParams(vmem_limit_bytes=24 * 1024 * 1024),
        cost_estimate=pl.CostEstimate(flops=2 * 10 ** 10, bytes_accessed=10 ** 7, transcendentals=0),
        name="bucket_rounds",
    )(plan, edge_count, where, *ops)


def stack_kernel(*refs):
    out = refs[-1]
    for i, ref in enumerate(refs[:-1]):
        out[i] = ref[...]


def stacked(values):
    vmem = pl.BlockSpec(memory_space=pltpu.VMEM)
    return pl.pallas_call(
        stack_kernel,
        out_shape=jax.ShapeDtypeStruct((len(values),) + values[0].shape, values[0].dtype),
        in_specs=[vmem] * len(values),
        out_specs=vmem,
        compiler_params=pltpu.CompilerParams(vmem_limit_bytes=4 * 1024 * 1024),
        name="stack_quarters",
    )(*values)


def load_kernel(keep, other, free_mine, free_other, out, free):
    width = free_mine.shape[0]
    free[0:width, :] = free_mine[...] + free_other[...]
    free[width:, :] = jnp.zeros_like(free[width:, :])

    def step(m, carry):
        rows = pl.ds(pl.multiple_of(m * TURN * CHUNK, 8), TURN * CHUNK)
        x = keep[rows, :] + other[rows, :]
        for q in range(TURN):
            k = m * TURN + q
            chunk = [x[q * CHUNK:(q + 1) * CHUNK, :]]
            chunk += [free[pl.ds(k + i * PEERS, 1), :] for i in range(ROWS - CHUNK)]
            out[k] = jnp.concatenate(chunk, axis=0).astype(BF16)
        return carry

    lax.fori_loop(0, PEERS // TURN, step, 0, unroll=8)


def load_chunks(keep, other, free_mine, free_other):
    vmem = pl.BlockSpec(memory_space=pltpu.VMEM)
    return pl.pallas_call(
        load_kernel,
        out_shape=jax.ShapeDtypeStruct((PEERS, ROWS, LANES), BF16),
        in_specs=[vmem] * 4,
        out_specs=vmem,
        scratch_shapes=[pltpu.VMEM(((ROWS - CHUNK) * PEERS, LANES), F32)],
        compiler_params=pltpu.CompilerParams(vmem_limit_bytes=8 * 1024 * 1024),
        name="load_chunks",
    )(keep, other, free_mine, free_other)


def turn_kernel(plan, pieces, out):
    offset = plan[0]
    for r in range(1, plan.shape[0]):
        offset = offset + plan[r]
    back = 2 * (offset - sum(KNOWN))
    total = jnp.sum(pieces[...].astype(F32), axis=0)
    summed = lax.broadcasted_iota(jnp.int32, (ROWS - 8, LANES), 0) < CHUNK - 8

    def step(m, carry):
        for q in range(TURN):
            k = m * TURN + q
            origin = lax.rem(k + PEERS - back, PEERS)
            out[k, 0:8] = total[0:8]
            out[k, 8:ROWS] = jnp.where(summed, total[8:], pieces[origin].astype(F32)[8:])
        return carry

    lax.fori_loop(0, PEERS // TURN, step, 0, unroll=8)


def turn_chunks(plan, pieces):
    vmem = pl.BlockSpec(memory_space=pltpu.VMEM)
    smem = pl.BlockSpec(memory_space=pltpu.SMEM)
    return pl.pallas_call(
        turn_kernel,
        out_shape=jax.ShapeDtypeStruct(pieces.shape, F32),
        in_specs=[smem, vmem],
        out_specs=vmem,
        compiler_params=pltpu.CompilerParams(vmem_limit_bytes=8 * 1024 * 1024),
        name="turn_chunks",
    )(plan, pieces)


def join_kernel(core, mine, other, own, near0, near1, near2, rel_out, ent_out, lines, free):
    width = rel_out.shape[0]
    n_tiles = rel_out.shape[1] // LANES

    def step(m, carry):
        rows = pl.ds(pl.multiple_of(m * TURN * CHUNK, 8), TURN * CHUNK)
        for side, chunks in ((core[0], mine), (1 - core[0], other)):
            lines[side, rows, :] = jnp.concatenate(
                [chunks[m * TURN + q][0:CHUNK, :] for q in range(TURN)], axis=0
            )
        for q in range(TURN):
            k = m * TURN + q
            x = mine[k]
            for i in range(ROWS - CHUNK):
                free[pl.ds(k + i * PEERS, 1), :] = x[CHUNK + i:CHUNK + i + 1, :]
        return carry

    lax.fori_loop(0, PEERS // TURN, step, 0, unroll=8)
    for tile in range(n_tiles):
        cols = slice(tile * LANES, (tile + 1) * LANES)
        for side, at, to, n_rows in pieces_of(tile, n_tiles, width):
            rel_out[to:to + n_rows, cols] = lines[side, at:at + n_rows, :]
    ent_out[...] = (own[...] + near0[...]) + (near1[...] + near2[...]) + free[0:width, :]


def join_outputs(core, mine, other, own, near, rel_shape):
    vmem = pl.BlockSpec(memory_space=pltpu.VMEM)
    smem = pl.BlockSpec(memory_space=pltpu.SMEM)
    return pl.pallas_call(
        join_kernel,
        out_shape=(
            jax.ShapeDtypeStruct(rel_shape, F32),
            jax.ShapeDtypeStruct(own.shape, F32),
        ),
        in_specs=[smem] + [vmem] * 6,
        out_specs=(vmem, vmem),
        scratch_shapes=[
            pltpu.VMEM((2, CHUNK * PEERS, LANES), F32),
            pltpu.VMEM(((ROWS - CHUNK) * PEERS, LANES), F32),
        ],
        compiler_params=pltpu.CompilerParams(vmem_limit_bytes=12 * 1024 * 1024),
        name="join_outputs",
    )(core, mine, other, own, *near)


def shifted(value, axes, steps):
    count = 1
    for axis in axes:
        count *= lax.axis_size(axis)
    return lax.ppermute(value, axes, [(a, (a + steps) % count) for a in range(count)])


def shifted_by(digit, unit, value):
    def move(d):
        return lambda v: shifted(v, DOM, unit * d) if d else v

    return lax.switch(digit, [move(d) for d in range(8)], value)


def swap(value, axis):
    return lax.ppermute(value, axis, [(0, 1), (1, 0)])


def together(*values):
    return lax.optimization_barrier(values)


def per_device(
    entity_table, relation_diag, plan, edge_count, src_rows, dst_rows, rel_ids, neg_rows
):
    rounds = plan.shape[0]
    core = lax.axis_index("core")
    where = jnp.stack([lax.axis_index(DOM), lax.axis_index("xh"), core]).astype(jnp.int32)
    indices = (src_rows, dst_rows, rel_ids, neg_rows)

    known = [shifted(entity_table, DOM, N_DOM - k) for k in KNOWN]
    pack, digits = pack_indices(plan, where, *indices)
    pack = swap(pack, "xh")
    free = shifted_by(digits[0], 1, entity_table)
    free = shifted_by(digits[1], 8, free)
    quarters = stacked([entity_table] + known + [free])
    quarters = lax.all_gather(quarters, REP, axis=0, tiled=False)
    parts, parts_send, free, free_send, half, half_send = run_rounds(
        plan, edge_count, where, quarters, relation_diag, indices, pack
    )

    half_other = swap(half_send, "core")
    free_send = swap(free_send, "core")
    parts_send = swap(parts_send, "core")
    free_mine = free[0] + free_send[0]
    free_other = swap(free[1] + free_send[1], "xh")
    parts_mine = parts[0] + parts_send[0]
    parts_other = swap((parts[1] + parts_send[1]).astype(BF16), "xh")
    pieces = lax.all_to_all(
        load_chunks(half, half_other, free_mine, free_other), CHIPS, 0, 0, tiled=True
    )
    parts = parts_mine + parts_other.astype(F32)
    pieces, parts = together(pieces, parts)
    near = [shifted(parts[at], DOM, k) for at, k in enumerate(KNOWN)]
    whole = lax.all_to_all(turn_chunks(plan, pieces), CHIPS, 0, 0, tiled=True)
    whole, *near = together(whole, *near)
    relation_grad, entity_grad = join_outputs(
        core.astype(jnp.int32).reshape(1),
        whole,
        swap(whole, "core"),
        parts[rounds - 1],
        near,
        relation_diag.shape,
    )
    return entity_grad, relation_grad


def solution(mesh):
    fine = Mesh(mesh.devices.reshape(4, 8, 2, 2, 2), DOM + REP)
    cols = P(None, DOM + REP)
    in_specs = (cols, P(), P(), P(), cols, cols, cols, P(None, DOM + REP, None))
    return jax.shard_map(
        per_device, mesh=fine, in_specs=in_specs, out_specs=(cols, P()), check_vma=False
    )
```

```python
import functools

import jax
import jax.numpy as jnp
from jax import lax
from jax.experimental import pallas as pl
from jax.experimental.pallas import tpu as pltpu
from jax.sharding import Mesh, PartitionSpec as P

DOM = ("y", "z", "xl")
REP = ("xh", "core")
CHIPS = ("y", "z", "xl", "xh")
LANES = 128
SPAN = 256
KNOWN = (1, 32, 63)
N_DOM = 64
GROUP = 2
PEERS = 128
CHUNK = 14
ROWS = 16
TURN = 4
F32 = jnp.float32
BF16 = jnp.bfloat16


def mm(a, b):
    return jnp.dot(a, b, preferred_element_type=F32)


def mm_nt(a, b):
    return lax.dot_general(a, b, (((1,), (1,)), ((), ())), preferred_element_type=F32)


def one_hot(index, height):
    rows = lax.broadcasted_iota(jnp.int16, (height, index.shape[1]), 0)
    return jnp.where(rows == index.astype(jnp.int16), BF16(1.0), BF16(0.0))


def one_hot_t(column, width):
    cols = lax.broadcasted_iota(jnp.int16, (column.shape[0], width), 1)
    return jnp.where(cols == column.astype(jnp.int16), BF16(1.0), BF16(0.0))


def column_of(index):
    return jnp.transpose(jnp.broadcast_to(index, (8, index.shape[1])))[:, 0:1]


def rel_chunks(n_rel):
    return [(a, min(2 * LANES, n_rel - a)) for a in range(0, n_rel, 2 * LANES)]


def pieces_of(tile, n_tiles, width):
    mid = n_tiles // 2
    cut = -(-width // 16) * 8
    if tile < mid:
        return [(0, tile * width, 0, width)]
    if tile == mid:
        return [(0, mid * width, 0, cut), (1, 0, cut, width - cut)]
    return [(1, width - cut + (tile - mid - 1) * width, 0, width)]


def bucket_row(known, plan):
    row = jnp.int32(0)
    for r in range(plan.shape[0]):
        if known is None:
            hit = plan[r] != KNOWN[0]
            for k in KNOWN[1:]:
                hit = jnp.logical_and(hit, plan[r] != k)
        else:
            hit = plan[r] == known
        row = jnp.where(hit, r, row)
    return row


def pack_kernel(plan, where, srcs, dsts, rels, negs, out, digits):
    rounds, blocks, _ = negs.shape
    half = blocks // 2
    offset = plan[0]
    for r in range(1, rounds):
        offset = offset + plan[r]
    offset = offset - sum(KNOWN)
    steps = N_DOM - offset
    digits[0] = lax.rem(steps, 8)
    digits[1] = lax.div(steps, jnp.int32(8))
    for r in range(rounds):
        away = lax.rem(where[1] + (r + 1), 2)
        for i in range(half):
            k = 2 * i + away
            at = r * half + i
            lanes = pl.ds(pl.multiple_of(k * SPAN, SPAN), SPAN)
            out[at:at + 1, 0:SPAN] = srcs[r:r + 1, lanes]
            out[at:at + 1, SPAN:2 * SPAN] = dsts[r:r + 1, lanes]
            out[at:at + 1, 2 * SPAN:3 * SPAN] = rels[r:r + 1, lanes]
            out[at:at + 1, 3 * SPAN:] = negs[r, pl.ds(k, 1), :]


def pack_indices(plan, where, srcs, dsts, rels, negs):
    rounds, blocks, n_neg = negs.shape
    vmem = pl.BlockSpec(memory_space=pltpu.VMEM)
    smem = pl.BlockSpec(memory_space=pltpu.SMEM)
    return pl.pallas_call(
        pack_kernel,
        out_shape=(
            jax.ShapeDtypeStruct((rounds * blocks // 2, 3 * SPAN + n_neg), jnp.int32),
            jax.ShapeDtypeStruct((2,), jnp.int32),
        ),
        in_specs=[smem] * 2 + [vmem] * 4,
        out_specs=(vmem, smem),
        name="pack_indices",
    )(plan, where, srcs, dsts, rels, negs)


def rounds_kernel(plan, edge_count, where, *refs):
    quarters, rel, srcs, dsts, rels, negs, pack = refs[:7]
    parts_keep, parts_send, free_keep, free_send, rel_keep, rel_send = refs[7:13]
    acc, rel_acc, idx, dst_buf = refs[13:]
    n_rep = quarters.shape[0]
    width, n_rel = rel.shape
    rounds, blocks, n_neg = negs.shape
    half = blocks // 2
    part = n_rep * LANES
    scale = n_neg ** -0.5
    span = GROUP * SPAN
    dom, high, core = where[0], where[1], where[2]

    acc[...] = jnp.zeros_like(acc)
    rel_acc[...] = jnp.zeros_like(rel_acc)
    for i in range(rounds):
        dst_buf[i] = jnp.concatenate([quarters[q, 1 + i] for q in range(n_rep)], axis=1)
    for r in range(rounds):
        home = lax.rem(high + r, 2)
        for i in range(half):
            lanes = pl.ds(pl.multiple_of((2 * i + home) * SPAN, SPAN), SPAN)
            mine = pl.ds(r * blocks + half * high + i, 1)
            idx[mine, 0:SPAN] = srcs[r:r + 1, lanes]
            idx[mine, SPAN:2 * SPAN] = dsts[r:r + 1, lanes]
            idx[mine, 2 * SPAN:3 * SPAN] = rels[r:r + 1, lanes]
            idx[mine, 3 * SPAN:] = negs[r, pl.ds(2 * i + home, 1), :]
            other = pl.ds(r * blocks + half * (1 - high) + i, 1)
            idx[other, :] = pack[r * half + i:r * half + i + 1, :]
    src_t = jnp.concatenate([quarters[q, 0] for q in range(n_rep)], axis=1)
    known_rows = [bucket_row(known, plan) for known in KNOWN + (None,)]

    def one_round(which, carry):
        row = known_rows[rounds - 1]
        for i in range(rounds - 1):
            row = jnp.where(which == i, known_rows[i], row)
        count = edge_count[row, dom]
        total = (count + (SPAN - 1)) // SPAN
        home = lax.rem(high + row, 2)

        def global_block(i):
            return (i // half) * (2 * blocks) + core * blocks + 2 * (i % half) + home

        used = jnp.int32(0)
        for i in range(blocks):
            used = used + (global_block(i) < total).astype(jnp.int32)
        dst_at = which + which // (rounds - 1)
        dst_t = dst_buf[which]
        dst_wide = dst_t.astype(F32)
        dst_rows = dst_wide.T.astype(BF16)

        def one_group(step, inner):
            first = step * GROUP
            at = row * blocks + first

            def take(a, n):
                return [idx[pl.ds(at + g, 1), a:a + n] for g in range(GROUP)]

            src_i = jnp.concatenate(take(0, SPAN), axis=1)
            dst_i = jnp.concatenate(take(SPAN, SPAN), axis=1)
            rel_i = jnp.concatenate(take(2 * SPAN, SPAN), axis=1)
            neg_i = take(3 * SPAN, n_neg)
            lane = lax.broadcasted_iota(jnp.int32, (1, SPAN), 1)
            live = jnp.concatenate(
                [
                    (global_block(first + g) * SPAN + lane < count).astype(F32)
                    for g in range(GROUP)
                ],
                axis=1,
            )
            rel_c = column_of(rel_i)
            w = jnp.zeros((width, span), F32)
            for a, n in rel_chunks(n_rel):
                w = w + mm(rel[:, a:a + n], one_hot(rel_i - a, n))
            s = mm(src_t, one_hot(src_i, part))
            t = mm(dst_t, one_hot(dst_i, part))
            lhs = (s * w).astype(BF16)
            lhs_wide = lhs.astype(F32)
            positive = jnp.sum(lhs_wide * t, axis=0, keepdims=True)
            pos_weight = -live * jax.nn.sigmoid(-positive)
            scores = mm(dst_rows, lhs)
            weight = ((live * scale) * jax.nn.sigmoid(scores)).astype(BF16)
            from_neg = []
            grad_dst = (pos_weight * lhs_wide).astype(BF16)
            dst_part = mm(grad_dst, one_hot_t(column_of(dst_i), part))
            for g in range(GROUP):
                edges = slice(g * SPAN, (g + 1) * SPAN)
                low = one_hot(jnp.bitwise_and(neg_i[g], LANES - 1), LANES)
                far = one_hot(jnp.right_shift(neg_i[g], 7), 16)
                times = mm_nt(far, low)
                times = jnp.concatenate([times[q:q + 1, :] for q in range(n_rep)], axis=1)
                counted = times * dst_wide
                counted_hi = counted.astype(BF16)
                counted_lo = (counted - counted_hi.astype(F32)).astype(BF16)
                from_neg.append(
                    mm(counted_hi, weight[:, edges]) + mm(counted_lo, weight[:, edges])
                )
                grad_neg = mm_nt(lhs[:, edges], weight[:, edges]).astype(BF16).astype(F32)
                dst_part = dst_part + times * grad_neg
            grad_lhs = pos_weight * t + jnp.concatenate(from_neg, axis=1)
            grad_src = (grad_lhs * w).astype(BF16)
            grad_rel = (grad_lhs * s).astype(BF16)
            src_part = mm(grad_src, one_hot_t(column_of(src_i), part))
            for q in range(n_rep):
                cols = slice(q * LANES, (q + 1) * LANES)
                acc[rounds - 1, q] += src_part[:, cols]
                acc[dst_at, q] += dst_part[:, cols]
            for a, n in rel_chunks(n_rel):
                term = mm(grad_rel, one_hot_t(rel_c - a, n))
                for b in range(n // LANES):
                    for side, to, at_row, n_rows in pieces_of(
                        a // LANES + b, n_rel // LANES, width
                    ):
                        rel_acc[side, to:to + n_rows, :] += term[
                            at_row:at_row + n_rows, b * LANES:(b + 1) * LANES
                        ]
            return inner

        lax.fori_loop(0, (used + (GROUP - 1)) // GROUP, one_group, 0)
        return carry

    lax.fori_loop(0, rounds, one_round, 0)
    rel_keep[...] = rel_acc[core]
    rel_send[...] = rel_acc[1 - core]
    for h, side in enumerate((high, 1 - high)):
        for i in range(rounds):
            parts_keep[h, i] = acc[i, 2 * side + core]
            parts_send[h, i] = acc[i, 2 * side + 1 - core]
        free_keep[h] = acc[rounds, 2 * side + core]
        free_send[h] = acc[rounds, 2 * side + 1 - core]


def run_rounds(plan, edge_count, where, quarters, rel, indices, pack):
    n_q, _, width, lanes = quarters.shape
    n_rel = rel.shape[1]
    rounds = plan.shape[0]
    half_rows = CHUNK * PEERS
    vmem = pl.BlockSpec(memory_space=pltpu.VMEM)
    smem = pl.BlockSpec(memory_space=pltpu.SMEM)
    parts = jax.ShapeDtypeStruct((2, rounds, width, lanes), F32)
    free = jax.ShapeDtypeStruct((2, width, lanes), F32)
    side = jax.ShapeDtypeStruct((half_rows, LANES), F32)
    ops = [quarters, rel, *indices, pack]
    return pl.pallas_call(
        rounds_kernel,
        out_shape=(parts, parts, free, free, side, side),
        in_specs=[smem] * 3 + [vmem] * len(ops),
        out_specs=(vmem,) * 6,
        scratch_shapes=[
            pltpu.VMEM((rounds + 1, n_q, width, lanes), F32),
            pltpu.VMEM((2, half_rows, LANES), F32),
            pltpu.VMEM((2 * pack.shape[0], pack.shape[1]), jnp.int32),
            pltpu.VMEM((rounds, width, n_q * lanes), BF16),
        ],
        compiler_params=pltpu.CompilerParams(vmem_limit_bytes=24 * 1024 * 1024),
        cost_estimate=pl.CostEstimate(flops=2 * 10 ** 10, bytes_accessed=10 ** 7, transcendentals=0),
        name="bucket_rounds",
    )(plan, edge_count, where, *ops)


def stack_kernel(*refs):
    out = refs[-1]
    for i, ref in enumerate(refs[:-1]):
        out[i] = ref[...]


def stacked(values):
    vmem = pl.BlockSpec(memory_space=pltpu.VMEM)
    return pl.pallas_call(
        stack_kernel,
        out_shape=jax.ShapeDtypeStruct((len(values),) + values[0].shape, values[0].dtype),
        in_specs=[vmem] * len(values),
        out_specs=vmem,
        compiler_params=pltpu.CompilerParams(vmem_limit_bytes=4 * 1024 * 1024),
        name="stack_quarters",
    )(*values)


def load_kernel(keep, other, free_mine, free_other, out, free):
    width = free_mine.shape[0]
    free[0:width, :] = free_mine[...] + free_other[...]
    free[width:, :] = jnp.zeros_like(free[width:, :])

    def step(m, carry):
        rows = pl.ds(pl.multiple_of(m * TURN * CHUNK, 8), TURN * CHUNK)
        x = keep[rows, :] + other[rows, :]
        for q in range(TURN):
            k = m * TURN + q
            chunk = [x[q * CHUNK:(q + 1) * CHUNK, :]]
            chunk += [free[pl.ds(k + i * PEERS, 1), :] for i in range(ROWS - CHUNK)]
            out[k] = jnp.concatenate(chunk, axis=0).astype(BF16)
        return carry

    lax.fori_loop(0, PEERS // TURN, step, 0, unroll=8)


def load_chunks(keep, other, free_mine, free_other):
    vmem = pl.BlockSpec(memory_space=pltpu.VMEM)
    return pl.pallas_call(
        load_kernel,
        out_shape=jax.ShapeDtypeStruct((PEERS, ROWS, LANES), BF16),
        in_specs=[vmem] * 4,
        out_specs=vmem,
        scratch_shapes=[pltpu.VMEM(((ROWS - CHUNK) * PEERS, LANES), F32)],
        compiler_params=pltpu.CompilerParams(vmem_limit_bytes=8 * 1024 * 1024),
        name="load_chunks",
    )(keep, other, free_mine, free_other)


def turn_kernel(plan, pieces, out):
    offset = plan[0]
    for r in range(1, plan.shape[0]):
        offset = offset + plan[r]
    back = 2 * (offset - sum(KNOWN))
    total = jnp.sum(pieces[...].astype(F32), axis=0)
    summed = lax.broadcasted_iota(jnp.int32, (ROWS - 8, LANES), 0) < CHUNK - 8

    def step(m, carry):
        for q in range(TURN):
            k = m * TURN + q
            origin = lax.rem(k + PEERS - back, PEERS)
            out[k, 0:8] = total[0:8]
            out[k, 8:ROWS] = jnp.where(summed, total[8:], pieces[origin].astype(F32)[8:])
        return carry

    lax.fori_loop(0, PEERS // TURN, step, 0, unroll=8)


def turn_chunks(plan, pieces):
    vmem = pl.BlockSpec(memory_space=pltpu.VMEM)
    smem = pl.BlockSpec(memory_space=pltpu.SMEM)
    return pl.pallas_call(
        turn_kernel,
        out_shape=jax.ShapeDtypeStruct(pieces.shape, F32),
        in_specs=[smem, vmem],
        out_specs=vmem,
        compiler_params=pltpu.CompilerParams(vmem_limit_bytes=8 * 1024 * 1024),
        name="turn_chunks",
    )(plan, pieces)


def join_kernel(core, mine, other, own, near0, near1, near2, rel_out, ent_out, lines, free):
    width = rel_out.shape[0]
    n_tiles = rel_out.shape[1] // LANES

    def step(m, carry):
        rows = pl.ds(pl.multiple_of(m * TURN * CHUNK, 8), TURN * CHUNK)
        for side, chunks in ((core[0], mine), (1 - core[0], other)):
            lines[side, rows, :] = jnp.concatenate(
                [chunks[m * TURN + q][0:CHUNK, :] for q in range(TURN)], axis=0
            )
        for q in range(TURN):
            k = m * TURN + q
            x = mine[k]
            for i in range(ROWS - CHUNK):
                free[pl.ds(k + i * PEERS, 1), :] = x[CHUNK + i:CHUNK + i + 1, :]
        return carry

    lax.fori_loop(0, PEERS // TURN, step, 0, unroll=8)
    for tile in range(n_tiles):
        cols = slice(tile * LANES, (tile + 1) * LANES)
        for side, at, to, n_rows in pieces_of(tile, n_tiles, width):
            rel_out[to:to + n_rows, cols] = lines[side, at:at + n_rows, :]
    ent_out[...] = (own[...] + near0[...]) + (near1[...] + near2[...]) + free[0:width, :]


def join_outputs(core, mine, other, own, near, rel_shape):
    vmem = pl.BlockSpec(memory_space=pltpu.VMEM)
    smem = pl.BlockSpec(memory_space=pltpu.SMEM)
    return pl.pallas_call(
        join_kernel,
        out_shape=(
            jax.ShapeDtypeStruct(rel_shape, F32),
            jax.ShapeDtypeStruct(own.shape, F32),
        ),
        in_specs=[smem] + [vmem] * 6,
        out_specs=(vmem, vmem),
        scratch_shapes=[
            pltpu.VMEM((2, CHUNK * PEERS, LANES), F32),
            pltpu.VMEM(((ROWS - CHUNK) * PEERS, LANES), F32),
        ],
        compiler_params=pltpu.CompilerParams(vmem_limit_bytes=12 * 1024 * 1024),
        name="join_outputs",
    )(core, mine, other, own, *near)


def shifted(value, axes, steps):
    count = 1
    for axis in axes:
        count *= lax.axis_size(axis)
    return lax.ppermute(value, axes, [(a, (a + steps) % count) for a in range(count)])


def shifted_by(digit, unit, value):
    def move(d):
        return lambda v: shifted(v, DOM, unit * d) if d else v

    return lax.switch(digit, [move(d) for d in range(8)], value)


def swap(value, axis):
    return lax.ppermute(value, axis, [(0, 1), (1, 0)])


def together(*values):
    return lax.optimization_barrier(values)


def per_device(
    entity_table, relation_diag, plan, edge_count, src_rows, dst_rows, rel_ids, neg_rows
):
    rounds = plan.shape[0]
    core = lax.axis_index("core")
    where = jnp.stack([lax.axis_index(DOM), lax.axis_index("xh"), core]).astype(jnp.int32)
    indices = (src_rows, dst_rows, rel_ids, neg_rows)

    known = [shifted(entity_table, DOM, N_DOM - k) for k in KNOWN]
    pack, digits = pack_indices(plan, where, *indices)
    pack = swap(pack, "xh")
    free = shifted_by(digits[0], 1, entity_table)
    free = shifted_by(digits[1], 8, free)
    quarters = stacked([entity_table] + known + [free])
    quarters = lax.all_gather(quarters, REP, axis=0, tiled=False)
    parts, parts_send, free, free_send, half, half_send = run_rounds(
        plan, edge_count, where, quarters, relation_diag, indices, pack
    )

    free_send = swap(free_send, "core")
    free_out = free[1] + free_send[1]
    free_out, half_send, parts_send = together(free_out, half_send, parts_send)
    half_other = swap(half_send, "core")
    parts_send = swap(parts_send, "core")
    free_mine = free[0] + free_send[0]
    free_other = swap(free_out, "xh")
    parts_mine = parts[0] + parts_send[0]
    parts_other = swap((parts[1] + parts_send[1]).astype(BF16), "xh")
    pieces = lax.all_to_all(
        load_chunks(half, half_other, free_mine, free_other), CHIPS, 0, 0, tiled=True
    )
    parts = parts_mine + parts_other.astype(F32)
    pieces, parts = together(pieces, parts)
    near = [shifted(parts[at], DOM, k) for at, k in enumerate(KNOWN)]
    whole = lax.all_to_all(turn_chunks(plan, pieces), CHIPS, 0, 0, tiled=True)
    whole, *near = together(whole, *near)
    relation_grad, entity_grad = join_outputs(
        core.astype(jnp.int32).reshape(1),
        whole,
        swap(whole, "core"),
        parts[rounds - 1],
        near,
        relation_diag.shape,
    )
    return entity_grad, relation_grad


def solution(mesh):
    fine = Mesh(mesh.devices.reshape(4, 8, 2, 2, 2), DOM + REP)
    cols = P(None, DOM + REP)
    in_specs = (cols, P(), P(), P(), cols, cols, cols, P(None, DOM + REP, None))
    return jax.shard_map(
        per_device, mesh=fine, in_specs=in_specs, out_specs=(cols, P()), check_vma=False
    )
```
